32 devices in a mesh: dp: 4 (over y, core), table: 8 (over z, x).
Axes of the slice: x: 2, y: 2, z: 4, core: 2. Of those that a mesh axis runs over, the one named last changes fastest.
Arguments:
- bag_slots: int32 [16384, 32], P(('dp', 'table')), may hold values from -1 to 767
- labels: float32 [16384], P(('dp', 'table')), may hold values from 0 to 1
- cold_ids: int32 [32, 8, 32], P(('dp', 'table')), may hold values from 0 to 1023
- cold_count: int32 [32, 8], P(('dp', 'table')), may hold values from 1 to 32, 128 in all within a row
- table: float32 [8192, 256], P('table'), may hold values from -1.8 to 1.8
- adagrad_sum: float32 [8192], P('table'), may hold values from 0.1 to 10
- hot_ids: int32 [512], P('table'), may hold values from 0 to 1023
- w_in: bfloat16 [256, 4096], replicated, may hold values from -0.375 to 0.375
- w_out: bfloat16 [4096], replicated, may hold values from -0.09375 to 0.09375
Outputs:
- new_table: float32 [8192, 256], P('table')
- new_sum: float32 [8192], P('table')
The draws below stay inside these ranges and needn't reach their ends.
Inputs may be any that keep to these rules, and one draw needn't show every extreme that they name: `bag_slots`: -1 marks an empty bag entry. `cold_count`: each reader's counts sum to 128.
All inputs are finite; a program needn't handle non-finite values.
Results may differ from the reference program's by a relative error of at most 0.0045.
The reference program's roundings to bfloat16 on the way count: a program that leaves them out, or rounds other values in their place, can miss the bound.
Values may be sent and summed in bfloat16 or wider, within the bound.
No kernel may reach another device: no remote copies, remote signals or barrier semaphores. Data moves between devices by JAX's collectives and lax.ppermute only.
A program may use at most 64 MiB of HBM per device.

```python
import math
import jax
import jax.numpy as jnp
import numpy as np
from jax import lax

E = 256
H = 4096
B_DEV = 512
BAG = 32
ROWS_DEV = 1024
HOT_DEV = 64
C = 32
ROWS = 8192
TOKENS = 16384
VOCAB = 768
N_DP = 4
N_TABLE = 8


def touch_ends(values, stream_key, low, top_value):
    index_at = [jax.random.randint(jax.random.fold_in(stream_key, axis), (), 0, length) for axis, length in enumerate(values.shape)]
    widest = values.shape.index(max(values.shape))
    next_to = index_at[:widest] + [(index_at[widest] + 1) % values.shape[widest]] + index_at[widest + 1:]
    return values.at[tuple(index_at)].set(low).at[tuple(next_to)].set(top_value)


def levels(own_key, shape, shards, least, top_value):
    gain = 1.0
    for position, parts in shards:
        heights = jax.random.uniform(jax.random.fold_in(jax.random.fold_in(own_key, 6), position), (parts,), jnp.float32, least / len(shards), top_value / len(shards))
        gain = gain * jnp.repeat(jnp.exp(heights), shape[position] // parts).reshape((-1,) + (1,) * (len(shape) - 1 - position))
    return gain


def split_up(count, total, reach, slope):
    loads = [(1 << 20) // math.isqrt(grade ** slope) + 1 for grade in range(2, count + 1)]
    surplus, given = total - reach - (count - 1), [1] * (count - 1)
    while surplus > 0:
        free = [i for i in range(count - 1) if given[i] < reach]
        whole, budget = sum([loads[i] for i in free]), surplus
        for i in free:
            extra = min(reach - given[i], max(1, budget * loads[i] // whole), surplus)
            given[i] = given[i] + extra
            surplus = surplus - extra
    return np.array([reach] + given)


def uneven(rng, number_of, total, limit, skew):
    if number_of == 2:
        one = jax.random.randint(rng, (), max(1, total - limit), min(limit, total - 1) + 1)
        return jnp.stack([one, total - one])
    lengths = jnp.asarray(split_up(number_of, total, limit, skew), jnp.int32)
    couples = (number_of - 1) // 2
    source_of, receiver = lengths[1:1 + 2 * couples:2], lengths[2:2 + 2 * couples:2]
    margin = jnp.minimum(source_of - 1, limit - receiver)
    passed = jax.random.randint(jax.random.fold_in(rng, 1), (couples,), 0, 1 << 20) % (margin + 1)
    lengths = lengths.at[1:1 + 2 * couples:2].set(source_of - passed).at[2:2 + 2 * couples:2].set(receiver + passed)
    return lengths[jax.random.permutation(jax.random.fold_in(rng, 2), number_of)]


def bell_draw(own_key, extent, spread, limit, cuts=(), kind=jnp.bfloat16):
    entries = jax.random.normal(own_key, extent, jnp.float32) * spread
    if len(cuts) > 0:
        entries = levels(own_key, extent, cuts, -0.22, 0.18) * entries
    return jnp.clip(entries, min=-limit, max=limit).astype(kind)


def setup_inputs(seed: int = 0) -> dict:
    streams_of = jax.random.split(jax.random.key(seed), 10)
    bag_slots = touch_ends(jax.random.randint(streams_of[0], (TOKENS, BAG), -1, VOCAB), jax.random.fold_in(streams_of[0], 1), -1, VOCAB - 1).astype(jnp.int32)
    labels = jnp.clip(1.0 * jax.random.uniform(streams_of[1], (TOKENS,), jnp.float32) ** levels(streams_of[1], (TOKENS,), ((0, 32),), -0.2, 0.2), 0.0, 1.0)
    cold_ids = touch_ends(jax.random.randint(streams_of[2], (N_DP * N_TABLE, N_TABLE, C), 0, ROWS_DEV), jax.random.fold_in(streams_of[2], 1), 0, ROWS_DEV - 1).astype(jnp.int32)
    cold_count = jax.vmap(lambda own: uneven(own, N_TABLE, C * N_TABLE // 2, C, 2))(jax.random.split(streams_of[3], (N_DP * N_TABLE))).reshape((N_DP * N_TABLE, N_TABLE)).astype(jnp.int32)
    table = bell_draw(streams_of[4], (ROWS, E), 0.3, 1.8, ((0, 8),), jnp.float32)
    adagrad_sum = jnp.clip(jnp.exp(math.log(10.0) - 4.6051702 * jax.random.uniform(streams_of[5], (ROWS,), jnp.float32) ** levels(streams_of[5], (ROWS,), ((0, 8),), -0.2, 0.2)), 0.1, 10.0)
    hot_ids = touch_ends(jax.random.randint(streams_of[6], (N_TABLE * HOT_DEV,), 0, ROWS_DEV), jax.random.fold_in(streams_of[6], 1), 0, ROWS_DEV - 1).astype(jnp.int32)
    w_in = bell_draw(streams_of[7], (E, H), E ** -0.5, 0.375)
    w_out = bell_draw(streams_of[8], (H,), H ** -0.5, 0.09375)
    return {"bag_slots": bag_slots, "labels": labels, "cold_ids": cold_ids, "cold_count": cold_count, "table": table, "adagrad_sum": adagrad_sum, "hot_ids": hot_ids, "w_in": w_in, "w_out": w_out}


learning_rate = 0.3

def reference(bag_slots, labels, cold_ids, cold_count, table, adagrad_sum, hot_ids, w_in, w_out):
    readers = N_DP * N_TABLE
    hot_total = N_TABLE * HOT_DEV
    owner_base = jnp.arange(N_TABLE, dtype=jnp.int32) * ROWS_DEV
    hot_global = (jnp.repeat(owner_base, HOT_DEV) + hot_ids).astype(jnp.int32)
    table_bf = table.astype(jnp.bfloat16)
    slot_iota = jnp.arange(C, dtype=jnp.int32)
    w_out_f = w_out.astype(jnp.float32)

    def one_reader(grad, reader):
        slots = lax.dynamic_slice_in_dim(bag_slots, reader * B_DEV, B_DEV, 0)
        targets = lax.dynamic_slice_in_dim(labels, reader * B_DEV, B_DEV, 0)
        cold_global = (owner_base[:, None] + cold_ids[reader]).reshape(-1).astype(jnp.int32)
        cold_live = (slot_iota[None, :] < cold_count[reader][:, None]).reshape(-1)
        vocab_ids = jnp.concatenate([hot_global, cold_global])
        vocab_live = jnp.concatenate([jnp.ones((hot_total,), bool), cold_live])
        safe = jnp.maximum(slots, 0)
        entry_ids = vocab_ids[safe]
        entry_live = (slots >= 0) & vocab_live[safe]
        entry_rows = jnp.where(entry_live[..., None], table_bf[entry_ids].astype(jnp.float32), 0.0)
        pooled = lax.optimization_barrier(jnp.sum(entry_rows, axis=1)).astype(jnp.bfloat16)
        pre_act = jnp.dot(pooled, w_in, preferred_element_type=jnp.float32)
        hidden = jax.nn.relu(pre_act).astype(jnp.bfloat16)
        logit = jnp.dot(hidden, w_out, preferred_element_type=jnp.float32)
        dlogit = jax.nn.sigmoid(logit) - targets
        dhidden = (dlogit[:, None] * w_out_f[None, :] * (pre_act > 0)).astype(jnp.bfloat16)
        dpooled = jnp.dot(dhidden, w_in.T, preferred_element_type=jnp.float32).astype(jnp.bfloat16)
        contrib = jnp.where(entry_live[..., None], dpooled.astype(jnp.float32)[:, None, :], 0.0)
        grad = grad.at[entry_ids.reshape(-1)].add(contrib.reshape(-1, E))
        return (grad, None)
    grad, _ = lax.scan(one_reader, jnp.zeros((ROWS, E), jnp.float32), jnp.arange(readers, dtype=jnp.int32))
    new_sum = adagrad_sum + lax.optimization_barrier(jnp.mean(grad * grad, axis=1))
    new_table = table - learning_rate * grad / jnp.sqrt(new_sum)[:, None]
    return (new_table, new_sum)
```

```python
import functools

import jax
import jax.numpy as jnp
from jax import lax
from jax.experimental import pallas as pl
from jax.experimental.pallas import tpu as pltpu
from jax.sharding import PartitionSpec as P

learning_rate = 0.3
f32, bf16, i32 = jnp.float32, jnp.bfloat16, jnp.int32
VMEM = pl.BlockSpec(memory_space=pltpu.VMEM)
SMEM = pl.BlockSpec(memory_space=pltpu.SMEM)
FIELDS = 4
FIELD_BITS = 8
TAIL = 16


def call(body, outs, operands, scratch=(), in_specs=None, flops=0, moved=0):
    return pl.pallas_call(
        body,
        out_shape=outs,
        in_specs=in_specs or [VMEM] * len(operands),
        out_specs=jax.tree.map(lambda _: VMEM, outs),
        scratch_shapes=list(scratch),
        compiler_params=pltpu.CompilerParams(vmem_limit_bytes=48 * 1024 * 1024),
        cost_estimate=pl.CostEstimate(flops=flops, bytes_accessed=moved, transcendentals=0),
    )(*operands)


def lanes(pieces):
    return jnp.concatenate(pieces, axis=1)


def incidence_body(hot_dev, slot_cap, count_ref, slots_ref, inc_ref, inc_t_ref):
    vocab, batch = inc_t_ref.shape
    block = hot_dev + slot_cap
    owners = vocab // block
    field = vocab // FIELDS
    step = 128
    row = lax.broadcasted_iota(i32, (field, step), 0)
    for start in range(0, batch, step):
        slots = slots_ref[start:start + step, :].T
        cold = slots - owners * hot_dev
        hot_column = (slots // hot_dev) * block + slots % hot_dev
        cold_column = (cold // slot_cap) * block + hot_dev + cold % slot_cap
        column = jnp.where(cold < 0, hot_column, cold_column)
        key = jnp.where(slots < 0, -1, column % field)
        unit = jnp.left_shift(jnp.ones_like(slots), FIELD_BITS * (column // field))
        packed = jnp.zeros((field, step), i32)
        for entry in range(slots.shape[0]):
            packed += jnp.where(row == key[entry:entry + 1, :], unit[entry:entry + 1, :], 0)
        for k in range(FIELDS):
            part = jnp.right_shift(packed, FIELD_BITS * k) & (2**FIELD_BITS - 1)
            inc_t_ref[k * field:(k + 1) * field, start:start + step] = part.astype(f32).astype(bf16)
    place = lax.broadcasted_iota(i32, (block, batch), 0)
    for owner in range(owners):
        rows = pl.ds(owner * block, block)
        live = place < hot_dev + count_ref[0, owner]
        inc_t_ref[rows, :] = jnp.where(live, inc_t_ref[rows, :].astype(f32), 0.0).astype(bf16)
    inc_ref[...] = inc_t_ref[...].T


def serve_body(asked_ref, hot_ref, table_ref, out_ref, pick):
    owners, slot_cap = asked_ref.shape
    hot_dev = hot_ref.shape[1]
    rows = table_ref.shape[0]
    hot_column = jnp.broadcast_to(hot_ref[...], (8, hot_dev)).T[:, 0:1]
    asked = asked_ref[...].T
    pick[0:hot_dev, :] = (lax.broadcasted_iota(i32, (hot_dev, rows), 1) == hot_column).astype(f32).astype(bf16)
    row = lax.broadcasted_iota(i32, (slot_cap, rows), 1)
    for t in range(owners):
        at = hot_dev + t * slot_cap
        pick[at:at + slot_cap, :] = (row == asked[:, t:t + 1]).astype(f32).astype(bf16)
    picked = jnp.dot(pick[...], table_ref[...].astype(bf16), preferred_element_type=f32).astype(bf16)
    for t in range(owners):
        at = hot_dev + t * slot_cap
        out_ref[t, 0:hot_dev, :] = picked[0:hot_dev]
        out_ref[t, hot_dev:, :] = picked[at:at + slot_cap]


def top_body(labels_ref, inc_ref, inc_t_ref, rows_ref, w_in_ref, w_out_ref, out_ref, gated, dhidden):
    batch = inc_ref.shape[0]
    hidden_units = w_in_ref.shape[1]
    step = 512
    pooled = jnp.dot(inc_ref[...], rows_ref[...], preferred_element_type=f32).astype(bf16)
    total = jnp.zeros((batch, 128), f32)
    for start in range(0, hidden_units, step):
        cols = slice(start, start + step)
        pre_act = jnp.dot(pooled, w_in_ref[:, cols], preferred_element_type=f32)
        w_out = w_out_ref[:, cols].astype(f32)
        hidden = jnp.maximum(pre_act, 0.0).astype(bf16).astype(f32)
        gated[:, cols] = jnp.where(pre_act > 0, w_out, 0.0).astype(bf16)
        term = hidden * w_out
        for k in range(0, step, 128):
            total += term[:, k:k + 128]
    logit = jnp.sum(total, axis=1, keepdims=True)
    labels = labels_ref[...].T
    labels = jnp.concatenate([labels[:, k:k + 1] for k in range(labels.shape[1])], axis=0)
    dlogit = jax.nn.sigmoid(logit) - labels
    dhidden[...] = (dlogit * gated[...].astype(f32)).astype(bf16)
    dpooled = lax.dot_general(
        dhidden[...], w_in_ref[...], (((1,), (1,)), ((), ())), preferred_element_type=f32
    ).astype(bf16)
    out_ref[...] = jnp.dot(inc_t_ref[...], dpooled, preferred_element_type=f32).astype(bf16)


def collect_body(asked_ref, back_ref, out_ref):
    owners, slot_cap = asked_ref.shape
    hot_dev = back_ref.shape[1] - slot_cap
    out_ref[0:hot_dev, :] = jnp.sum(back_ref[:, 0:hot_dev, :].astype(f32), axis=0).astype(bf16)
    for t in range(owners):
        at = hot_dev + t * slot_cap
        out_ref[at:at + slot_cap, :] = back_ref[t, hot_dev:, :]
    asked = lanes([asked_ref[t:t + 1, :] for t in range(owners)])
    digit = lax.broadcasted_iota(i32, (TAIL, asked.shape[1]), 0)
    digits = jnp.where(digit == 0, asked >> 8, jnp.where(digit == 1, asked & 255, 0))
    out_ref[hot_dev + owners * slot_cap:, :] = digits.astype(f32).astype(bf16)


def adagrad(table, own_sum, grad):
    new_sum = own_sum + jnp.sum(grad * grad, axis=1, keepdims=True) * (1.0 / grad.shape[1])
    return table - grad * (learning_rate / jnp.sqrt(new_sum)), new_sum


def update_body(hot_ref, sum_ref, table_ref, *refs):
    groups = len(refs) - 4
    part_refs, (new_table_ref, new_sum_ref, held, sums) = refs[:groups], refs[groups:]
    hot_dev = hot_ref.shape[1]
    size = part_refs[0].shape[0]
    cold = size - hot_dev - TAIL
    rows, width = table_ref.shape
    me = lax.axis_index("dp")
    for s in range(groups):
        held[pl.ds(pl.multiple_of((me ^ s) * size, 16), size), :] = part_refs[s][...]
    hot = jnp.concatenate([held[g * size:g * size + hot_dev, :] for g in range(groups)], axis=0)
    hot_ids = lanes([hot_ref[...]] * groups)
    cold_ids = []
    for g in range(groups):
        digits = held[g * size + hot_dev + cold:(g + 1) * size, :].astype(f32).astype(i32)
        cold_ids.append(digits[0:1, :] * 256 + digits[1:2, :])
    own_sum = sum_ref[...].T
    step = 128
    for k in range(rows // step):
        at = slice(k * step, (k + 1) * step)

        def pick(ids):
            row = lax.broadcasted_iota(i32, (step, ids.shape[1]), 0) + k * step
            return (row == ids).astype(f32).astype(bf16)

        grad = jnp.dot(pick(hot_ids), hot, preferred_element_type=f32)
        for g in range(groups):
            part = held[g * size + hot_dev:g * size + hot_dev + cold, :]
            grad += jnp.dot(pick(cold_ids[g]), part, preferred_element_type=f32)
        new_table_ref[at, :], sums[:, k:k + 1] = adagrad(table_ref[at, :], own_sum[:, k:k + 1], grad)
    new_sum_ref[...] = sums[...].T


def dense_body(hot_ref, asked_ref, back_ref, out_ref):
    owners, slot_cap = asked_ref.shape
    hot_dev = hot_ref.shape[1]
    rows = out_ref.shape[0]

    def pick(ids):
        return (lax.broadcasted_iota(i32, (rows, ids.shape[1]), 0) == ids).astype(f32).astype(bf16)

    hot = jnp.sum(back_ref[:, 0:hot_dev, :].astype(f32), axis=0).astype(bf16)
    grad = jnp.dot(pick(hot_ref[...]), hot, preferred_element_type=f32)
    for t in range(owners):
        grad += jnp.dot(pick(asked_ref[t:t + 1, :]), back_ref[t, hot_dev:, :], preferred_element_type=f32)
    out_ref[...] = grad.astype(bf16)


def exchange(x):
    return lax.all_to_all(x, "table", split_axis=0, concat_axis=0, tiled=True)


def per_device(bag_slots, labels, cold_ids, cold_count, table, adagrad_sum, hot_ids, w_in, w_out):
    owners = lax.axis_size("table")
    groups = lax.axis_size("dp")
    hot_dev = hot_ids.shape[0]
    slot_cap = cold_ids.shape[2]
    batch = bag_slots.shape[0]
    rows, width = table.shape
    hidden_units = w_in.shape[1]
    block = hot_dev + slot_cap
    vocab = owners * block
    shape = jax.ShapeDtypeStruct

    hot_row = hot_ids.reshape(1, hot_dev)
    asked = exchange(cold_ids[0])
    inc, inc_t = call(
        functools.partial(incidence_body, hot_dev, slot_cap),
        (shape((batch, vocab), bf16), shape((vocab, batch), bf16)),
        (cold_count, bag_slots),
        in_specs=[SMEM, VMEM],
    )
    served = call(
        serve_body,
        shape((owners, block, width), bf16),
        (asked, hot_row, table),
        [pltpu.VMEM((hot_dev + owners * slot_cap, rows), bf16)],
    )
    fetched = exchange(served)
    slot_grad = call(
        top_body,
        shape((vocab, width), bf16),
        (labels.reshape(-1, 128), inc, inc_t, fetched.reshape(vocab, width), w_in, w_out.reshape(1, -1)),
        [pltpu.VMEM((batch, hidden_units), bf16), pltpu.VMEM((batch, hidden_units), bf16)],
    )
    returned = exchange(slot_grad.reshape(owners, block, width))
    size = hot_dev + owners * slot_cap + TAIL
    if groups & (groups - 1) == 0 and groups * size <= 2 * rows and owners * slot_cap == width:
        part = call(collect_body, shape((size, width), bf16), (asked, returned))
        parts = {0: part}
        bit = groups // 2
        while bit:
            swap = [(g, g ^ bit) for g in range(groups)]
            parts.update({s ^ bit: lax.ppermute(x, "dp", swap) for s, x in list(parts.items())})
            bit //= 2
        new_table, new_sum = call(
            update_body,
            (shape((rows, width), f32), shape((rows // 128, 128), f32)),
            (hot_row, adagrad_sum.reshape(-1, 128), table) + tuple(parts[s] for s in range(groups)),
            [pltpu.VMEM((groups * size, width), bf16), pltpu.VMEM((128, rows // 128), f32)],
        )
        return new_table, new_sum.reshape(rows)
    grad = call(dense_body, shape((rows, width), bf16), (hot_row, asked, returned))
    grad = lax.psum(grad, "dp").astype(f32)
    new_table, new_sum = adagrad(table, adagrad_sum[:, None], grad)
    return new_table, new_sum[:, 0]


def solution(mesh):
    placed = (
        P(("dp", "table"), None),
        P(("dp", "table")),
        P(("dp", "table"), None, None),
        P(("dp", "table"), None),
        P("table", None),
        P("table"),
        P("table"),
        P(),
        P(),
    )
    return jax.shard_map(
        per_device,
        mesh=mesh,
        in_specs=placed,
        out_specs=(P("table", None), P("table")),
        check_vma=False,
    )
```

```python
import functools

import jax
import jax.numpy as jnp
from jax import lax
from jax.experimental import pallas as pl
from jax.experimental.pallas import tpu as pltpu
from jax.sharding import PartitionSpec as P

learning_rate = 0.3
f32, bf16, i32 = jnp.float32, jnp.bfloat16, jnp.int32
VMEM = pl.BlockSpec(memory_space=pltpu.VMEM)
SMEM = pl.BlockSpec(memory_space=pltpu.SMEM)
FIELDS = 4
FIELD_BITS = 8
TAIL = 16


def call(body, outs, operands, scratch=(), in_specs=None, mib=12):
    return pl.pallas_call(
        body,
        out_shape=outs,
        in_specs=in_specs or [VMEM] * len(operands),
        out_specs=jax.tree.map(lambda _: VMEM, outs),
        scratch_shapes=list(scratch),
        compiler_params=pltpu.CompilerParams(vmem_limit_bytes=mib * 1024 * 1024),
    )(*operands)


def lanes(pieces):
    return jnp.concatenate(pieces, axis=1)


def one_hot(ids, shape, axis, start=0):
    return (lax.broadcasted_iota(i32, shape, axis) + start == ids).astype(f32).astype(bf16)


def incidence_body(hot_cols, slot_cap, count_ref, slots_ref, inc_ref, inc_t_ref):
    vocab, batch = inc_t_ref.shape
    field = vocab // FIELDS
    step = 128
    row = lax.broadcasted_iota(i32, (field, step), 0)
    for start in range(0, batch, step):
        slots = slots_ref[:, start:start + step]
        key = jnp.where(slots < 0, -1, slots % field)
        unit = jnp.left_shift(jnp.ones_like(slots), FIELD_BITS * (slots // field))
        packed = jnp.zeros((field, step), i32)
        for entry in range(slots.shape[0]):
            packed += jnp.where(row == key[entry:entry + 1, :], unit[entry:entry + 1, :], 0)
        for k in range(FIELDS):
            part = jnp.right_shift(packed, FIELD_BITS * k) & (2**FIELD_BITS - 1)
            inc_t_ref[k * field:(k + 1) * field, start:start + step] = part.astype(f32).astype(bf16)
    place = lax.broadcasted_iota(i32, (slot_cap, batch), 0)
    for owner in range((vocab - hot_cols) // slot_cap):
        rows = pl.ds(hot_cols + owner * slot_cap, slot_cap)
        inc_t_ref[rows, :] = jnp.where(place < count_ref[0, owner], inc_t_ref[rows, :].astype(f32), 0.0).astype(bf16)
    inc_ref[...] = inc_t_ref[...].T


def serve_hot_body(ids_ref, table_ref, out_ref, table_bf_ref):
    hot_dev = ids_ref.shape[1]
    table_bf_ref[...] = table_ref[...].astype(bf16)
    ids = jnp.broadcast_to(ids_ref[...], (8, hot_dev)).T[:, 0:1]
    pick = one_hot(ids, (hot_dev, table_ref.shape[0]), 1)
    picked = jnp.dot(pick, table_bf_ref[...], preferred_element_type=f32).astype(bf16)
    for t in range(out_ref.shape[0]):
        out_ref[t] = picked


def serve_cold_body(asked_ref, table_ref, out_ref, pick):
    owners, slot_cap = asked_ref.shape
    asked = asked_ref[...].T
    for t in range(owners):
        pick[t * slot_cap:(t + 1) * slot_cap, :] = one_hot(asked[:, t:t + 1], (slot_cap, table_ref.shape[0]), 1)
    out_ref[...] = jnp.dot(pick[...], table_ref[...], preferred_element_type=f32).astype(bf16)


def top_body(labels_ref, inc_ref, inc_t_ref, hot_ref, cold_ref, w_in_ref, w_out_ref, out_ref, gated, dhidden):
    batch = inc_ref.shape[0]
    hidden_units = w_in_ref.shape[1]
    owners, block, _ = out_ref.shape
    hot_cols = hot_ref.shape[0]
    hot_dev = hot_cols // owners
    slot_cap = block - hot_dev
    step = 512
    pooled = jnp.dot(inc_ref[:, 0:hot_cols], hot_ref[...], preferred_element_type=f32)
    pooled = (pooled + jnp.dot(inc_ref[:, hot_cols:], cold_ref[...], preferred_element_type=f32)).astype(bf16)
    logit = jnp.zeros((batch, 128), f32)
    for start in range(0, hidden_units, step):
        cols = slice(start, start + step)
        pre_act = jnp.dot(pooled, w_in_ref[:, cols], preferred_element_type=f32)
        hidden = jnp.maximum(pre_act, 0.0).astype(bf16)
        gated[:, cols] = jnp.where(pre_act > 0, w_out_ref[:, cols].astype(f32), 0.0).astype(bf16)
        w_out = jnp.broadcast_to(w_out_ref[:, cols], (128, step))
        logit += lax.dot_general(hidden, w_out, (((1,), (1,)), ((), ())), preferred_element_type=f32)
    labels = labels_ref[...].T
    labels = jnp.concatenate([labels[:, k:k + 1] for k in range(labels.shape[1])], axis=0)
    dlogit = jax.nn.sigmoid(logit) - labels
    for start in range(0, hidden_units, 128):
        cols = slice(start, start + 128)
        dhidden[:, cols] = (dlogit * gated[:, cols].astype(f32)).astype(bf16)
    dpooled = lax.dot_general(
        dhidden[...], w_in_ref[...], (((1,), (1,)), ((), ())), preferred_element_type=f32
    ).astype(bf16)
    grad = jnp.dot(inc_t_ref[...], dpooled, preferred_element_type=f32).astype(bf16)
    for t in range(owners):
        out_ref[t, 0:hot_dev, :] = grad[t * hot_dev:(t + 1) * hot_dev]
        out_ref[t, hot_dev:, :] = grad[hot_cols + t * slot_cap:hot_cols + (t + 1) * slot_cap]


def collect_body(asked_ref, back_ref, out_ref):
    owners, slot_cap = asked_ref.shape
    hot_dev = back_ref.shape[1] - slot_cap
    out_ref[0:hot_dev, :] = jnp.sum(back_ref[:, 0:hot_dev, :].astype(f32), axis=0).astype(bf16)
    for t in range(owners):
        at = hot_dev + t * slot_cap
        out_ref[at:at + slot_cap, :] = back_ref[t, hot_dev:, :]
    asked = lanes([asked_ref[t:t + 1, :] for t in range(owners)])
    digit = lax.broadcasted_iota(i32, (TAIL, asked.shape[1]), 0)
    digits = jnp.where(digit == 0, asked >> 8, jnp.where(digit == 1, asked & 255, 0))
    out_ref[hot_dev + owners * slot_cap:, :] = digits.astype(f32).astype(bf16)


def adagrad(table, own_sum, grad):
    new_sum = own_sum + jnp.sum(grad * grad, axis=1, keepdims=True) * (1.0 / grad.shape[1])
    return table - grad * (learning_rate / jnp.sqrt(new_sum)), new_sum


def update_body(hot_ref, sum_ref, table_ref, *refs):
    groups = len(refs) - 4
    part_refs, (new_table_ref, new_sum_ref, held, sums) = refs[:groups], refs[groups:]
    hot_dev = hot_ref.shape[1]
    size = part_refs[0].shape[0]
    cold = size - hot_dev - TAIL
    rows, width = table_ref.shape
    me = lax.axis_index("dp")
    for s in range(groups):
        held[pl.ds(pl.multiple_of((me ^ s) * size, 16), size), :] = part_refs[s][...]
    hot = jnp.concatenate([held[g * size:g * size + hot_dev, :] for g in range(groups)], axis=0)
    hot_ids = lanes([hot_ref[...]] * groups)
    cold_ids = []
    for g in range(groups):
        digits = held[g * size + hot_dev + cold:(g + 1) * size, :].astype(f32).astype(i32)
        cold_ids.append(digits[0:1, :] * 256 + digits[1:2, :])
    own_sum = sum_ref[...].T
    step = 128
    for k in range(rows // step):
        at = slice(k * step, (k + 1) * step)

        def pick(ids):
            row = lax.broadcasted_iota(i32, (step, ids.shape[1]), 0) + k * step
            return (row == ids).astype(f32).astype(bf16)

        grad = jnp.dot(pick(hot_ids), hot, preferred_element_type=f32)
        for g in range(groups):
            part = held[g * size + hot_dev:g * size + hot_dev + cold, :]
            grad += jnp.dot(pick(cold_ids[g]), part, preferred_element_type=f32)
        new_table_ref[at, :], sums[:, k:k + 1] = adagrad(table_ref[at, :], own_sum[:, k:k + 1], grad)
    new_sum_ref[...] = sums[...].T


def dense_body(hot_ref, asked_ref, back_ref, out_ref):
    owners, slot_cap = asked_ref.shape
    hot_dev = hot_ref.shape[1]
    rows = out_ref.shape[0]

    def pick(ids):
        return (lax.broadcasted_iota(i32, (rows, ids.shape[1]), 0) == ids).astype(f32).astype(bf16)

    hot = jnp.sum(back_ref[:, 0:hot_dev, :].astype(f32), axis=0).astype(bf16)
    grad = jnp.dot(pick(hot_ref[...]), hot, preferred_element_type=f32)
    for t in range(owners):
        grad += jnp.dot(pick(asked_ref[t:t + 1, :]), back_ref[t, hot_dev:, :], preferred_element_type=f32)
    out_ref[...] = grad.astype(bf16)


def exchange(x):
    return lax.all_to_all(x, "table", split_axis=0, concat_axis=0, tiled=True)


def per_device(bag_slots, labels, cold_ids, cold_count, table, adagrad_sum, hot_ids, w_in, w_out):
    owners = lax.axis_size("table")
    groups = lax.axis_size("dp")
    hot_dev = hot_ids.shape[0]
    slot_cap = cold_ids.shape[2]
    batch = bag_slots.shape[0]
    rows, width = table.shape
    hidden_units = w_in.shape[1]
    block = hot_dev + slot_cap
    vocab = owners * block
    shape = jax.ShapeDtypeStruct

    hot_row = hot_ids.reshape(1, hot_dev)
    asked = exchange(cold_ids[0])
    inc, inc_t = call(
        functools.partial(incidence_body, owners * hot_dev, slot_cap),
        (shape((batch, vocab), bf16), shape((vocab, batch), bf16)),
        (cold_count, bag_slots.T),
        in_specs=[SMEM, VMEM],
    )
    served_hot, table_bf = call(
        serve_hot_body,
        (shape((owners, hot_dev, width), bf16), shape((rows, width), bf16)),
        (hot_row, table),
    )
    hot_rows = exchange(served_hot).reshape(-1, width)
    served_cold = call(
        serve_cold_body,
        shape((owners * slot_cap, width), bf16),
        (asked, table_bf),
        [pltpu.VMEM((owners * slot_cap, rows), bf16)],
    )
    cold_rows = exchange(served_cold.reshape(owners, slot_cap, width)).reshape(-1, width)
    slot_grad = call(
        top_body,
        shape((owners, block, width), bf16),
        (labels.reshape(-1, 128), inc, inc_t, hot_rows, cold_rows, w_in, w_out.reshape(1, -1)),
        [pltpu.VMEM((batch, hidden_units), bf16), pltpu.VMEM((batch, hidden_units), bf16)],
        mib=24,
    )
    returned = exchange(slot_grad)
    size = hot_dev + owners * slot_cap + TAIL
    if groups & (groups - 1) == 0 and groups * size <= 2 * rows and owners * slot_cap == width:
        part = call(collect_body, shape((size, width), bf16), (asked, returned))
        parts = {0: part}
        bit = groups // 2
        while bit:
            swap = [(g, g ^ bit) for g in range(groups)]
            parts.update({s ^ bit: lax.ppermute(x, "dp", swap) for s, x in list(parts.items())})
            bit //= 2
        new_table, new_sum = call(
            update_body,
            (shape((rows, width), f32), shape((rows // 128, 128), f32)),
            (hot_row, adagrad_sum.reshape(-1, 128), table) + tuple(parts[s] for s in range(groups)),
            [pltpu.VMEM((groups * size, width), bf16), pltpu.VMEM((128, rows // 128), f32)],
        )
        return new_table, new_sum.reshape(rows)
    grad = call(dense_body, shape((rows, width), bf16), (hot_row, asked, returned))
    grad = lax.psum(grad, "dp").astype(f32)
    new_table, new_sum = adagrad(table, adagrad_sum[:, None], grad)
    return new_table, new_sum[:, 0]


def solution(mesh):
    placed = (
        P(("dp", "table"), None),
        P(("dp", "table")),
        P(("dp", "table"), None, None),
        P(("dp", "table"), None),
        P("table", None),
        P("table"),
        P("table"),
        P(),
        P(),
    )
    return jax.shard_map(
        per_device,
        mesh=mesh,
        in_specs=placed,
        out_specs=(P("table", None), P("table")),
        check_vma=False,
    )
```

```python
import functools

import jax
import jax.numpy as jnp
from jax import lax
from jax.experimental import pallas as pl
from jax.experimental.pallas import tpu as pltpu
from jax.sharding import PartitionSpec as P

learning_rate = 0.3
f32, bf16, i32 = jnp.float32, jnp.bfloat16, jnp.int32
VMEM = pl.BlockSpec(memory_space=pltpu.VMEM)
SMEM = pl.BlockSpec(memory_space=pltpu.SMEM)
FIELDS = 4
FIELD_BITS = 8
TAIL = 16


def call(body, outs, operands, scratch=(), in_specs=None, mib=12):
    return pl.pallas_call(
        body,
        out_shape=outs,
        in_specs=in_specs or [VMEM] * len(operands),
        out_specs=jax.tree.map(lambda _: VMEM, outs),
        scratch_shapes=list(scratch),
        compiler_params=pltpu.CompilerParams(vmem_limit_bytes=mib * 1024 * 1024),
    )(*operands)


def lanes(pieces):
    return jnp.concatenate(pieces, axis=1)


def one_hot(ids, shape, axis, start=0):
    return (lax.broadcasted_iota(i32, shape, axis) + start == ids).astype(f32).astype(bf16)


def incidence_body(hot_cols, slot_cap, count_ref, slots_ref, inc_ref, inc_t_ref):
    vocab, batch = inc_t_ref.shape
    field = vocab // FIELDS
    step = 128
    row = lax.broadcasted_iota(i32, (field, step), 0)
    for start in range(0, batch, step):
        slots = slots_ref[:, start:start + step]
        key = jnp.where(slots < 0, -1, slots % field)
        unit = jnp.left_shift(jnp.ones_like(slots), FIELD_BITS * (slots // field))
        packed = jnp.zeros((field, step), i32)
        for entry in range(slots.shape[0]):
            packed += jnp.where(row == key[entry:entry + 1, :], unit[entry:entry + 1, :], 0)
        for k in range(FIELDS):
            part = jnp.right_shift(packed, FIELD_BITS * k) & (2**FIELD_BITS - 1)
            inc_t_ref[k * field:(k + 1) * field, start:start + step] = part.astype(f32).astype(bf16)
    place = lax.broadcasted_iota(i32, (slot_cap, batch), 0)
    for owner in range((vocab - hot_cols) // slot_cap):
        rows = pl.ds(hot_cols + owner * slot_cap, slot_cap)
        inc_t_ref[rows, :] = jnp.where(place < count_ref[0, owner], inc_t_ref[rows, :].astype(f32), 0.0).astype(bf16)
    inc_ref[...] = inc_t_ref[...].T


def core():
    return lax.rem(lax.axis_index("dp"), 2)


def half_rows(owner, hot_dev, which):
    half = hot_dev // 2
    return pl.ds(pl.multiple_of(owner * hot_dev + which * half, half), half)


def pick_hot_body(ids_ref, table_ref, hot_ref, table_bf_ref):
    hot_dev = ids_ref.shape[1]
    table_bf_ref[...] = table_ref[...].astype(bf16)
    ids = jnp.broadcast_to(ids_ref[...], (8, hot_dev)).T[:, 0:1]
    pick = one_hot(ids, (hot_dev, table_ref.shape[0]), 1)
    hot_ref[...] = jnp.dot(pick, table_bf_ref[...], preferred_element_type=f32).astype(bf16)


def serve_body(asked_ref, hot_ref, table_ref, out_ref, pick):
    owners, slot_cap = asked_ref.shape
    hot_dev = hot_ref.shape[0]
    asked = asked_ref[...].T
    for t in range(owners):
        pick[t * slot_cap:(t + 1) * slot_cap, :] = one_hot(asked[:, t:t + 1], (slot_cap, table_ref.shape[0]), 1)
    picked = jnp.dot(pick[...], table_ref[...], preferred_element_type=f32).astype(bf16)
    hot = hot_ref[half_rows(0, hot_dev, core()), :]
    for t in range(owners):
        out_ref[t, 0:hot_dev // 2, :] = hot
        out_ref[t, hot_dev // 2:, :] = picked[t * slot_cap:(t + 1) * slot_cap]


def first_rows_body(rows_ref, out_ref):
    out_ref[...] = rows_ref[:, 0:out_ref.shape[1], :]


def top_body(labels_ref, inc_ref, inc_t_ref, own_ref, mate_ref, w_in_ref, w_out_ref, part_ref, send_ref, gated, rows):
    batch = inc_ref.shape[0]
    hidden_units, width = w_in_ref.shape[1], w_in_ref.shape[0]
    owners, half, _ = send_ref.shape
    hot_dev = 2 * half
    hot_cols = owners * hot_dev
    slot_cap = part_ref.shape[1] - half
    me = core()
    for t in range(owners):
        rows[half_rows(t, hot_dev, me), :] = own_ref[t, 0:half, :]
        rows[half_rows(t, hot_dev, 1 - me), :] = mate_ref[t, 0:half, :]
        rows[hot_cols + t * slot_cap:hot_cols + (t + 1) * slot_cap, :] = own_ref[t, half:, :]
    labels = labels_ref[...].T
    labels = jnp.concatenate([labels[:, k:k + 1] for k in range(labels.shape[1])], axis=0)
    pooled = jnp.dot(inc_ref[...], rows[...], preferred_element_type=f32).astype(bf16)
    size, step, wide = batch // 2, 512, 2048
    dpooled = []
    for at in range(0, batch, size):
        samples = slice(at, at + size)
        total = jnp.zeros((size, 128), f32)
        for start in range(0, hidden_units, step):
            cols = slice(start, start + step)
            pre_act = jnp.dot(pooled[samples], w_in_ref[:, cols], preferred_element_type=f32)
            w_out = w_out_ref[:, cols].astype(f32)
            gated[samples, cols] = jnp.where(pre_act > 0, w_out, 0.0).astype(bf16)
            term = jnp.maximum(pre_act, 0.0).astype(bf16).astype(f32) * w_out
            for k in range(0, step, 128):
                total += term[:, k:k + 128]
        logit = jnp.sum(total, axis=1, keepdims=True)
        dlogit = jnp.broadcast_to(jax.nn.sigmoid(logit) - labels[samples], (size, 128))
        grad = jnp.zeros((size, width), f32)
        for start in range(0, hidden_units, wide):
            dhidden = lanes([
                (dlogit * gated[samples, k:k + 128].astype(f32)).astype(bf16) for k in range(start, start + wide, 128)
            ])
            grad += lax.dot_general(
                dhidden, w_in_ref[:, start:start + wide], (((1,), (1,)), ((), ())), preferred_element_type=f32
            )
        dpooled.append(grad.astype(bf16))
    dpooled = jnp.concatenate(dpooled, axis=0)
    rows[...] = jnp.dot(inc_t_ref[...], dpooled, preferred_element_type=f32).astype(bf16)
    for t in range(owners):
        send_ref[t] = rows[half_rows(t, hot_dev, 1 - me), :]
        part_ref[t, 0:half, :] = rows[half_rows(t, hot_dev, me), :]
        part_ref[t, half:, :] = rows[hot_cols + t * slot_cap:hot_cols + (t + 1) * slot_cap, :]


def add_hot_body(part_ref, got_ref, out_ref):
    half = got_ref.shape[1]
    out_ref[:, 0:half, :] = (part_ref[:, 0:half, :].astype(f32) + got_ref[...].astype(f32)).astype(bf16)
    out_ref[:, half:, :] = part_ref[:, half:, :]


def collect_body(asked_ref, back_ref, out_ref):
    owners, slot_cap = asked_ref.shape
    half = back_ref.shape[1] - slot_cap
    out_ref[0:half, :] = jnp.sum(back_ref[:, 0:half, :].astype(f32), axis=0).astype(bf16)
    for t in range(owners):
        out_ref[half + t * slot_cap:half + (t + 1) * slot_cap, :] = back_ref[t, half:, :]
    asked = lanes([asked_ref[t:t + 1, :] for t in range(owners)])
    digit = lax.broadcasted_iota(i32, (TAIL, asked.shape[1]), 0)
    digits = jnp.where(digit == 0, asked >> 8, jnp.where(digit == 1, asked & 255, 0))
    out_ref[half + owners * slot_cap:, :] = digits.astype(f32).astype(bf16)


def hot_half(hot_ref, which):
    half = hot_ref.shape[1] // 2
    return jnp.where(which == 0, hot_ref[:, 0:half], hot_ref[:, half:])


def row_grads(which, hot_ref, part_refs, held, put, rows):
    size = part_refs[0].shape[0]
    half = hot_ref.shape[1] // 2
    me = lax.div(lax.axis_index("dp"), 2)
    count = len(part_refs)
    for s in range(count):
        held[pl.ds(pl.multiple_of((me ^ s) * size, 16), size), :] = part_refs[s][...]
    hot = jnp.concatenate([held[g * size:g * size + half, :] for g in range(count)], axis=0)
    ids = [lanes([hot_half(hot_ref, which)] * count)]
    parts = [hot]
    for g in range(count):
        digits = held[(g + 1) * size - TAIL:(g + 1) * size, :].astype(f32).astype(i32)
        ids.append(digits[0:1, :] * 256 + digits[1:2, :])
        parts.append(held[g * size + half:(g + 1) * size - TAIL, :])
    step = 128
    for start in range(0, rows, step):
        grad = 0.0
        for k in range(len(ids)):
            pick = one_hot(ids[k], (step, ids[k].shape[1]), 0, start)
            grad += jnp.dot(pick, parts[k], preferred_element_type=f32)
        put(slice(start, start + step), grad)


def own_grad_body(hot_ref, *refs):
    part_refs, (out_ref, held) = refs[:-2], refs[-2:]

    def put(at, grad):
        out_ref[at, :] = grad

    row_grads(core(), hot_ref, part_refs, held, put, out_ref.shape[0])


def adagrad(table, own_sum, grad):
    new_sum = own_sum + jnp.sum(grad * grad, axis=1, keepdims=True) * (1.0 / grad.shape[1])
    return table - grad * (learning_rate / jnp.sqrt(new_sum)), new_sum


def update_body(hot_ref, sum_ref, table_ref, grad_ref, *refs):
    part_refs, (new_table_ref, new_sum_ref, held, sums) = refs[:-4], refs[-4:]
    own_sum = sum_ref[...].T

    def put(at, grad):
        k = at.start // 128
        new_table_ref[at, :], sums[:, k:k + 1] = adagrad(
            table_ref[at, :], own_sum[:, k:k + 1], grad_ref[at, :] + grad
        )

    row_grads(1 - core(), hot_ref, part_refs, held, put, table_ref.shape[0])
    new_sum_ref[...] = sums[...].T


def dense_body(hot_ref, asked_ref, back_ref, out_ref):
    owners, slot_cap = asked_ref.shape
    half = back_ref.shape[1] - slot_cap
    rows = out_ref.shape[0]
    hot = jnp.sum(back_ref[:, 0:half, :].astype(f32), axis=0).astype(bf16)
    grad = jnp.dot(one_hot(hot_half(hot_ref, core()), (rows, half), 0), hot, preferred_element_type=f32)
    for t in range(owners):
        pick = one_hot(asked_ref[t:t + 1, :], (rows, slot_cap), 0)
        grad += jnp.dot(pick, back_ref[t, half:, :], preferred_element_type=f32)
    out_ref[...] = grad.astype(bf16)


def exchange(x):
    return lax.all_to_all(x, "table", split_axis=0, concat_axis=0, tiled=True)


def swap(x, bit):
    return lax.ppermute(x, "dp", [(g, g ^ bit) for g in range(lax.axis_size("dp"))])


def per_device(bag_slots, labels, cold_ids, cold_count, table, adagrad_sum, hot_ids, w_in, w_out):
    owners = lax.axis_size("table")
    groups = lax.axis_size("dp")
    hot_dev = hot_ids.shape[0]
    slot_cap = cold_ids.shape[2]
    batch = bag_slots.shape[0]
    rows, width = table.shape
    hidden_units = w_in.shape[1]
    half = hot_dev // 2
    vocab = owners * (hot_dev + slot_cap)
    shape = jax.ShapeDtypeStruct

    hot_row = hot_ids.reshape(1, hot_dev)
    asked = exchange(cold_ids[0])
    inc, inc_t = call(
        functools.partial(incidence_body, owners * hot_dev, slot_cap),
        (shape((batch, vocab), bf16), shape((vocab, batch), bf16)),
        (cold_count, bag_slots.T),
        in_specs=[SMEM, VMEM],
    )
    hot, table_bf = call(pick_hot_body, (shape((hot_dev, width), bf16), shape((rows, width), bf16)), (hot_row, table))
    served = call(
        serve_body,
        shape((owners, half + slot_cap, width), bf16),
        (asked, hot, table_bf),
        [pltpu.VMEM((owners * slot_cap, rows), bf16)],
    )
    own_rows, inc, inc_t = lax.optimization_barrier((exchange(served), inc, inc_t))
    mate_rows = swap(call(first_rows_body, shape((owners, half, width), bf16), (own_rows,)), 1)
    part, to_mate = call(
        top_body,
        (shape((owners, half + slot_cap, width), bf16), shape((owners, half, width), bf16)),
        (labels.reshape(-1, 128), inc, inc_t, own_rows, mate_rows, w_in, w_out.reshape(1, -1)),
        [pltpu.VMEM((batch, hidden_units), bf16), pltpu.VMEM((vocab, width), bf16)],
        mib=24,
    )
    summed = call(add_hot_body, shape(part.shape, bf16), (part, swap(to_mate, 1)))
    returned = exchange(summed)
    size = half + owners * slot_cap + TAIL
    if groups & (groups - 1) == 0 and groups * size <= 2 * rows and owners * slot_cap == width:
        parts = {0: call(collect_body, shape((size, width), bf16), (asked, returned))}
        bit = groups // 2
        while bit > 1:
            parts.update({s ^ bit: swap(x, bit) for s, x in list(parts.items())})
            bit //= 2
        near = [parts[2 * y] for y in range(groups // 2)]
        far = [swap(x, 1) for x in near]
        held = pltpu.VMEM((groups // 2 * size, width), bf16)
        grad = call(own_grad_body, shape((rows, width), f32), (hot_row, *near), [held])
        new_table, new_sum = call(
            update_body,
            (shape((rows, width), f32), shape((rows // 128, 128), f32)),
            (hot_row, adagrad_sum.reshape(-1, 128), table, grad, *far),
            [held, pltpu.VMEM((128, rows // 128), f32)],
        )
        return new_table, new_sum.reshape(rows)
    grad = call(dense_body, shape((rows, width), bf16), (hot_row, asked, returned))
    grad = lax.psum(grad, "dp").astype(f32)
    new_table, new_sum = adagrad(table, adagrad_sum[:, None], grad)
    return new_table, new_sum[:, 0]


def solution(mesh):
    placed = (
        P(("dp", "table"), None),
        P(("dp", "table")),
        P(("dp", "table"), None, None),
        P(("dp", "table"), None),
        P("table", None),
        P("table"),
        P("table"),
        P(),
        P(),
    )
    return jax.shard_map(
        per_device,
        mesh=mesh,
        in_specs=placed,
        out_specs=(P("table", None), P("table")),
        check_vma=False,
    )
```

```python
import functools

import jax
import jax.numpy as jnp
from jax import lax
from jax.experimental import pallas as pl
from jax.experimental.pallas import tpu as pltpu
from jax.sharding import PartitionSpec as P

learning_rate = 0.3
f32, bf16, i32 = jnp.float32, jnp.bfloat16, jnp.int32
VMEM = pl.BlockSpec(memory_space=pltpu.VMEM)
ANY = pl.BlockSpec(memory_space=pl.ANY)
SMEM = pl.BlockSpec(memory_space=pltpu.SMEM)
FIELDS = 4
FIELD_BITS = 8
TAIL = 16


def call(body, outs, operands, scratch=(), in_specs=None, out_specs=None, mib=12):
    return pl.pallas_call(
        body,
        out_shape=outs,
        in_specs=in_specs or [VMEM] * len(operands),
        out_specs=out_specs or jax.tree.map(lambda _: VMEM, outs),
        scratch_shapes=list(scratch),
        compiler_params=pltpu.CompilerParams(vmem_limit_bytes=mib * 1024 * 1024),
    )(*operands)


def lanes(pieces):
    return jnp.concatenate(pieces, axis=1)


def one_hot(ids, shape, axis, start=0):
    return (lax.broadcasted_iota(i32, shape, axis) + start == ids).astype(f32).astype(bf16)


def incidence_body(hot_cols, slot_cap, count_ref, slots_ref, inc_ref, inc_t_ref):
    vocab, batch = inc_t_ref.shape
    field = vocab // FIELDS
    step = 128
    row = lax.broadcasted_iota(i32, (field, step), 0)
    for start in range(0, batch, step):
        slots = slots_ref[:, start:start + step]
        key = jnp.where(slots < 0, -1, slots % field)
        unit = jnp.left_shift(jnp.ones_like(slots), FIELD_BITS * (slots // field))
        packed = jnp.zeros((field, step), i32)
        for entry in range(slots.shape[0]):
            packed += jnp.where(row == key[entry:entry + 1, :], unit[entry:entry + 1, :], 0)
        for k in range(FIELDS):
            part = jnp.right_shift(packed, FIELD_BITS * k) & (2**FIELD_BITS - 1)
            inc_t_ref[k * field:(k + 1) * field, start:start + step] = part.astype(f32).astype(bf16)
    place = lax.broadcasted_iota(i32, (slot_cap, batch), 0)
    for owner in range((vocab - hot_cols) // slot_cap):
        rows = pl.ds(hot_cols + owner * slot_cap, slot_cap)
        inc_t_ref[rows, :] = jnp.where(place < count_ref[0, owner], inc_t_ref[rows, :].astype(f32), 0.0).astype(bf16)
    inc_ref[...] = inc_t_ref[...].T


def core():
    return lax.rem(lax.axis_index("dp"), 2)


def half_rows(owner, hot_dev, which):
    half = hot_dev // 2
    return pl.ds(pl.multiple_of(owner * hot_dev + which * half, half), half)


def pick_hot_body(ids_ref, table_ref, hot_ref, table_bf_ref):
    hot_dev = ids_ref.shape[1]
    table_bf_ref[...] = table_ref[...].astype(bf16)
    ids = jnp.broadcast_to(ids_ref[...], (8, hot_dev)).T[:, 0:1]
    pick = one_hot(ids, (hot_dev, table_ref.shape[0]), 1)
    hot_ref[...] = jnp.dot(pick, table_bf_ref[...], preferred_element_type=f32).astype(bf16)


def serve_body(asked_ref, hot_ref, table_ref, out_ref, pick, hot, cold, sems):
    owners, slot_cap = asked_ref.shape
    half = hot.shape[0]
    hot[...] = hot_ref[half_rows(0, 2 * half, core()), :]
    copies = [pltpu.make_async_copy(hot, out_ref.at[t, 0:half], sems.at[t]) for t in range(owners)]
    for copy in copies:
        copy.start()
    asked = asked_ref[...].T
    for t in range(owners):
        pick[t * slot_cap:(t + 1) * slot_cap, :] = one_hot(asked[:, t:t + 1], (slot_cap, table_ref.shape[0]), 1)
    cold[...] = jnp.dot(pick[...], table_ref[...], preferred_element_type=f32).astype(bf16)
    for t in range(owners):
        rows = cold.at[t * slot_cap:(t + 1) * slot_cap]
        copies.append(pltpu.make_async_copy(rows, out_ref.at[t, half:half + slot_cap], sems.at[owners + t]))
        copies[-1].start()
    for copy in copies:
        copy.wait()


def first_rows_body(rows_ref, out_ref):
    out_ref[...] = rows_ref[:, 0:out_ref.shape[1], :]


def top_body(labels_ref, inc_ref, own_ref, mate_ref, w_in_ref, w_out_ref, out_ref, gated, rows):
    batch = inc_ref.shape[0]
    hidden_units, width = w_in_ref.shape[1], w_in_ref.shape[0]
    owners, half, _ = mate_ref.shape
    hot_dev = 2 * half
    hot_cols = owners * hot_dev
    slot_cap = own_ref.shape[1] - half
    me = core()
    for t in range(owners):
        rows[half_rows(t, hot_dev, me), :] = own_ref[t, 0:half, :]
        rows[half_rows(t, hot_dev, 1 - me), :] = mate_ref[t, 0:half, :]
        rows[hot_cols + t * slot_cap:hot_cols + (t + 1) * slot_cap, :] = own_ref[t, half:, :]
    labels = labels_ref[...].T
    labels = jnp.concatenate([labels[:, k:k + 1] for k in range(labels.shape[1])], axis=0)
    pooled = jnp.dot(inc_ref[...], rows[...], preferred_element_type=f32).astype(bf16)
    size, step, wide = batch // 2, 512, 2048
    for at in range(0, batch, size):
        samples = slice(at, at + size)
        total = jnp.zeros((size, 128), f32)
        for start in range(0, hidden_units, step):
            cols = slice(start, start + step)
            pre_act = jnp.dot(pooled[samples], w_in_ref[:, cols], preferred_element_type=f32)
            w_out = w_out_ref[:, cols].astype(f32)
            gated[samples, cols] = jnp.where(pre_act > 0, w_out, 0.0).astype(bf16)
            term = jnp.maximum(pre_act, 0.0).astype(bf16).astype(f32) * w_out
            for k in range(0, step, 128):
                total += term[:, k:k + 128]
        logit = jnp.sum(total, axis=1, keepdims=True)
        dlogit = jnp.broadcast_to(jax.nn.sigmoid(logit) - labels[samples], (size, 128))
        grad = jnp.zeros((size, width), f32)
        for start in range(0, hidden_units, wide):
            dhidden = lanes([
                (dlogit * gated[samples, k:k + 128].astype(f32)).astype(bf16) for k in range(start, start + wide, 128)
            ])
            grad += lax.dot_general(
                dhidden, w_in_ref[:, start:start + wide], (((1,), (1,)), ((), ())), preferred_element_type=f32
            )
        out_ref[samples, :] = grad.astype(bf16)


def slot_grads_body(inc_t_ref, dpooled_ref, part_ref, send_ref, rows):
    owners, half, _ = send_ref.shape
    hot_dev = 2 * half
    hot_cols = owners * hot_dev
    slot_cap = part_ref.shape[1] - half
    me = core()
    rows[...] = jnp.dot(inc_t_ref[...], dpooled_ref[...], preferred_element_type=f32).astype(bf16)
    for t in range(owners):
        send_ref[t] = rows[half_rows(t, hot_dev, 1 - me), :]
        part_ref[t, 0:half, :] = rows[half_rows(t, hot_dev, me), :]
        part_ref[t, half:, :] = rows[hot_cols + t * slot_cap:hot_cols + (t + 1) * slot_cap, :]


def add_hot_body(part_ref, got_ref, out_ref):
    half = got_ref.shape[1]
    out_ref[:, 0:half, :] = (part_ref[:, 0:half, :].astype(f32) + got_ref[...].astype(f32)).astype(bf16)
    out_ref[:, half:, :] = part_ref[:, half:, :]


def collect_body(asked_ref, back_ref, out_ref):
    owners, slot_cap = asked_ref.shape
    half = back_ref.shape[1] - slot_cap
    out_ref[0:half, :] = jnp.sum(back_ref[:, 0:half, :].astype(f32), axis=0).astype(bf16)
    for t in range(owners):
        out_ref[half + t * slot_cap:half + (t + 1) * slot_cap, :] = back_ref[t, half:, :]
    asked = lanes([asked_ref[t:t + 1, :] for t in range(owners)])
    digit = lax.broadcasted_iota(i32, (TAIL, asked.shape[1]), 0)
    digits = jnp.where(digit == 0, asked >> 8, jnp.where(digit == 1, asked & 255, 0))
    out_ref[half + owners * slot_cap:, :] = digits.astype(f32).astype(bf16)


def hot_half(hot_ref, which):
    half = hot_ref.shape[1] // 2
    return jnp.where(which == 0, hot_ref[:, 0:half], hot_ref[:, half:])


def row_grads(which, hot_ref, part_refs, held, put, rows):
    size = part_refs[0].shape[0]
    half = hot_ref.shape[1] // 2
    me = lax.div(lax.axis_index("dp"), 2)
    count = len(part_refs)
    for s in range(count):
        held[pl.ds(pl.multiple_of((me ^ s) * size, 16), size), :] = part_refs[s][...]
    hot = jnp.concatenate([held[g * size:g * size + half, :] for g in range(count)], axis=0)
    ids = [lanes([hot_half(hot_ref, which)] * count)]
    parts = [hot]
    for g in range(count):
        digits = held[(g + 1) * size - TAIL:(g + 1) * size, :].astype(f32).astype(i32)
        ids.append(digits[0:1, :] * 256 + digits[1:2, :])
        parts.append(held[g * size + half:(g + 1) * size - TAIL, :])
    step = 128
    for start in range(0, rows, step):
        grad = 0.0
        for k in range(len(ids)):
            pick = one_hot(ids[k], (step, ids[k].shape[1]), 0, start)
            grad += jnp.dot(pick, parts[k], preferred_element_type=f32)
        put(slice(start, start + step), grad)


def own_grad_body(hot_ref, *refs):
    part_refs, (out_ref, held) = refs[:-2], refs[-2:]

    def put(at, grad):
        out_ref[at, :] = grad

    row_grads(core(), hot_ref, part_refs, held, put, out_ref.shape[0])


def adagrad(table, own_sum, grad):
    new_sum = own_sum + jnp.sum(grad * grad, axis=1, keepdims=True) * (1.0 / grad.shape[1])
    return table - grad * (learning_rate / jnp.sqrt(new_sum)), new_sum


def update_body(hot_ref, sum_ref, table_ref, grad_ref, *refs):
    part_refs, (new_table_ref, new_sum_ref, held, sums, staged, sems) = refs[:-6], refs[-6:]
    own_sum = sum_ref[...].T
    copies = []

    def put(at, grad):
        k = at.start // 128
        staged[at, :], sums[:, k:k + 1] = adagrad(table_ref[at, :], own_sum[:, k:k + 1], grad_ref[at, :] + grad)
        copies.append(pltpu.make_async_copy(staged.at[at], new_table_ref.at[at], sems.at[k]))
        copies[k].start()

    row_grads(1 - core(), hot_ref, part_refs, held, put, table_ref.shape[0])
    new_sum_ref[...] = sums[...].T
    for copy in copies:
        copy.wait()


def dense_body(hot_ref, asked_ref, back_ref, out_ref):
    owners, slot_cap = asked_ref.shape
    half = back_ref.shape[1] - slot_cap
    rows = out_ref.shape[0]
    hot = jnp.sum(back_ref[:, 0:half, :].astype(f32), axis=0).astype(bf16)
    grad = jnp.dot(one_hot(hot_half(hot_ref, core()), (rows, half), 0), hot, preferred_element_type=f32)
    for t in range(owners):
        pick = one_hot(asked_ref[t:t + 1, :], (rows, slot_cap), 0)
        grad += jnp.dot(pick, back_ref[t, half:, :], preferred_element_type=f32)
    out_ref[...] = grad.astype(bf16)


def exchange(x):
    return lax.all_to_all(x, "table", split_axis=0, concat_axis=0, tiled=True)


def swap(x, bit):
    return lax.ppermute(x, "dp", [(g, g ^ bit) for g in range(lax.axis_size("dp"))])


def per_device(bag_slots, labels, cold_ids, cold_count, table, adagrad_sum, hot_ids, w_in, w_out):
    owners = lax.axis_size("table")
    groups = lax.axis_size("dp")
    hot_dev = hot_ids.shape[0]
    slot_cap = cold_ids.shape[2]
    batch = bag_slots.shape[0]
    rows, width = table.shape
    hidden_units = w_in.shape[1]
    half = hot_dev // 2
    vocab = owners * (hot_dev + slot_cap)
    shape = jax.ShapeDtypeStruct

    hot_row = hot_ids.reshape(1, hot_dev)
    asked = exchange(cold_ids[0])
    inc, inc_t = call(
        functools.partial(incidence_body, owners * hot_dev, slot_cap),
        (shape((batch, vocab), bf16), shape((vocab, batch), bf16)),
        (cold_count, bag_slots.T),
        in_specs=[SMEM, VMEM],
    )
    hot, table_bf = call(pick_hot_body, (shape((hot_dev, width), bf16), shape((rows, width), bf16)), (hot_row, table))
    served = call(
        serve_body,
        shape((owners, half + slot_cap, width), bf16),
        (asked, hot, table_bf),
        [
            pltpu.VMEM((owners * slot_cap, rows), bf16),
            pltpu.VMEM((half, width), bf16),
            pltpu.VMEM((owners * slot_cap, width), bf16),
            pltpu.SemaphoreType.DMA((2 * owners,)),
        ],
        out_specs=ANY,
    )
    own_rows, inc, inc_t = lax.optimization_barrier((exchange(served), inc, inc_t))
    mate_rows = swap(call(first_rows_body, shape((owners, half, width), bf16), (own_rows,)), 1)
    dpooled = call(
        top_body,
        shape((batch, width), bf16),
        (labels.reshape(-1, 128), inc, own_rows, mate_rows, w_in, w_out.reshape(1, -1)),
        [pltpu.VMEM((batch, hidden_units), bf16), pltpu.VMEM((vocab, width), bf16)],
        mib=24,
    )
    part, to_mate = call(
        slot_grads_body,
        (shape((owners, half + slot_cap, width), bf16), shape((owners, half, width), bf16)),
        (inc_t, dpooled),
        [pltpu.VMEM((vocab, width), bf16)],
    )
    summed = call(add_hot_body, shape(part.shape, bf16), (part, swap(to_mate, 1)))
    returned = exchange(summed)
    size = half + owners * slot_cap + TAIL
    if groups & (groups - 1) == 0 and groups * size <= 2 * rows and owners * slot_cap == width:
        parts = {0: call(collect_body, shape((size, width), bf16), (asked, returned))}
        bit = groups // 2
        while bit > 1:
            parts.update({s ^ bit: swap(x, bit) for s, x in list(parts.items())})
            bit //= 2
        near = [parts[2 * y] for y in range(groups // 2)]
        far = [swap(x, 1) for x in near]
        held = pltpu.VMEM((groups // 2 * size, width), bf16)
        grad = call(own_grad_body, shape((rows, width), f32), (hot_row, *near), [held])
        new_table, new_sum = call(
            update_body,
            (shape((rows, width), f32), shape((rows // 128, 128), f32)),
            (hot_row, adagrad_sum.reshape(-1, 128), table, grad, *far),
            [
                held,
                pltpu.VMEM((128, rows // 128), f32),
                pltpu.VMEM((rows, width), f32),
                pltpu.SemaphoreType.DMA((rows // 128,)),
            ],
            out_specs=(ANY, VMEM),
        )
        return new_table, new_sum.reshape(rows)
    grad = call(dense_body, shape((rows, width), bf16), (hot_row, asked, returned))
    grad = lax.psum(grad, "dp").astype(f32)
    new_table, new_sum = adagrad(table, adagrad_sum[:, None], grad)
    return new_table, new_sum[:, 0]


def solution(mesh):
    placed = (
        P(("dp", "table"), None),
        P(("dp", "table")),
        P(("dp", "table"), None, None),
        P(("dp", "table"), None),
        P("table", None),
        P("table"),
        P("table"),
        P(),
        P(),
    )
    return jax.shard_map(
        per_device,
        mesh=mesh,
        in_specs=placed,
        out_specs=(P("table", None), P("table")),
        check_vma=False,
    )
```

```python
import functools

import jax
import jax.numpy as jnp
from jax import lax
from jax.experimental import pallas as pl
from jax.experimental.pallas import tpu as pltpu
from jax.sharding import PartitionSpec as P

learning_rate = 0.3
f32, bf16, i32 = jnp.float32, jnp.bfloat16, jnp.int32
VMEM = pl.BlockSpec(memory_space=pltpu.VMEM)
HBM = pl.BlockSpec(memory_space=pltpu.HBM)
SMEM = pl.BlockSpec(memory_space=pltpu.SMEM)
FIELDS = 4
FIELD_BITS = 8
TAIL = 16


def call(body, outs, operands, scratch=(), in_specs=None, out_specs=None, mib=12):
    return pl.pallas_call(
        body,
        out_shape=outs,
        in_specs=in_specs or [VMEM] * len(operands),
        out_specs=out_specs or jax.tree.map(lambda _: VMEM, outs),
        scratch_shapes=list(scratch),
        compiler_params=pltpu.CompilerParams(vmem_limit_bytes=mib * 1024 * 1024),
    )(*operands)


def lanes(pieces):
    return jnp.concatenate(pieces, axis=1)


def one_hot(ids, shape, axis, start=0):
    return (lax.broadcasted_iota(i32, shape, axis) + start == ids).astype(f32).astype(bf16)


def incidence_body(hot_cols, slot_cap, count_ref, slots_ref, inc_t_ref):
    vocab, batch = inc_t_ref.shape
    field = vocab // FIELDS
    step = 128
    row = lax.broadcasted_iota(i32, (field, step), 0)
    for start in range(0, batch, step):
        slots = slots_ref[:, start:start + step]
        key = jnp.where(slots < 0, -1, slots % field)
        unit = jnp.left_shift(jnp.ones_like(slots), FIELD_BITS * (slots // field))
        packed = jnp.zeros((field, step), i32)
        for entry in range(slots.shape[0]):
            packed += jnp.where(row == key[entry:entry + 1, :], unit[entry:entry + 1, :], 0)
        for k in range(FIELDS):
            part = jnp.right_shift(packed, FIELD_BITS * k) & (2**FIELD_BITS - 1)
            inc_t_ref[k * field:(k + 1) * field, start:start + step] = part.astype(f32).astype(bf16)
    place = lax.broadcasted_iota(i32, (slot_cap, batch), 0)
    for owner in range((vocab - hot_cols) // slot_cap):
        rows = pl.ds(hot_cols + owner * slot_cap, slot_cap)
        inc_t_ref[rows, :] = jnp.where(place < count_ref[0, owner], inc_t_ref[rows, :].astype(f32), 0.0).astype(bf16)


def transpose_body(x_ref, out_ref):
    out_ref[...] = x_ref[...].T


def core():
    return lax.rem(lax.axis_index("dp"), 2)


def half_rows(owner, hot_dev, which):
    half = hot_dev // 2
    return pl.ds(pl.multiple_of(owner * hot_dev + which * half, half), half)


def pick_hot_body(ids_ref, table_ref, hot_ref, table_bf_ref, ids, table, sems):
    copies = [pltpu.make_async_copy(ids_ref, ids, sems.at[0]), pltpu.make_async_copy(table_ref, table, sems.at[1])]
    for copy in copies:
        copy.start()
    for copy in copies:
        copy.wait()
    hot_dev = ids.shape[1]
    table_bf_ref[...] = table[...].astype(bf16)
    column = jnp.broadcast_to(ids[...], (8, hot_dev)).T[:, 0:1]
    pick = one_hot(column, (hot_dev, table.shape[0]), 1)
    hot_ref[...] = jnp.dot(pick, table_bf_ref[...], preferred_element_type=f32).astype(bf16)


def serve_body(asked_ref, hot_ref, table_ref, out_ref, pick, staged, sem):
    owners, slot_cap = asked_ref.shape
    hot_dev = hot_ref.shape[0]
    asked = asked_ref[...].T
    for t in range(owners):
        pick[t * slot_cap:(t + 1) * slot_cap, :] = one_hot(asked[:, t:t + 1], (slot_cap, table_ref.shape[0]), 1)
    picked = jnp.dot(pick[...], table_ref[...], preferred_element_type=f32).astype(bf16)
    hot = hot_ref[half_rows(0, hot_dev, core()), :]
    for t in range(owners):
        staged[t, 0:hot_dev // 2, :] = hot
        staged[t, hot_dev // 2:, :] = picked[t * slot_cap:(t + 1) * slot_cap]
    copy = pltpu.make_async_copy(staged, out_ref, sem)
    copy.start()
    copy.wait()


def first_rows_body(rows_ref, out_ref):
    out_ref[...] = rows_ref[:, 0:out_ref.shape[1], :]


def top_body(labels_ref, inc_ref, own_ref, mate_ref, w_in_ref, w_out_ref, out_ref, gated, rows):
    batch = inc_ref.shape[0]
    hidden_units, width = w_in_ref.shape[1], w_in_ref.shape[0]
    owners, half, _ = mate_ref.shape
    hot_dev = 2 * half
    hot_cols = owners * hot_dev
    slot_cap = own_ref.shape[1] - half
    me = core()
    for t in range(owners):
        rows[half_rows(t, hot_dev, me), :] = own_ref[t, 0:half, :]
        rows[half_rows(t, hot_dev, 1 - me), :] = mate_ref[t, 0:half, :]
        rows[hot_cols + t * slot_cap:hot_cols + (t + 1) * slot_cap, :] = own_ref[t, half:, :]
    labels = labels_ref[...].T
    labels = jnp.concatenate([labels[:, k:k + 1] for k in range(labels.shape[1])], axis=0)
    pooled = jnp.dot(inc_ref[...], rows[...], preferred_element_type=f32).astype(bf16)
    size, step, wide = batch // 2, 512, 2048
    for at in range(0, batch, size):
        samples = slice(at, at + size)
        total = jnp.zeros((size, 128), f32)
        for start in range(0, hidden_units, step):
            cols = slice(start, start + step)
            pre_act = jnp.dot(pooled[samples], w_in_ref[:, cols], preferred_element_type=f32)
            w_out = w_out_ref[:, cols].astype(f32)
            gated[samples, cols] = jnp.where(pre_act > 0, w_out, 0.0).astype(bf16)
            term = jnp.maximum(pre_act, 0.0).astype(bf16).astype(f32) * w_out
            for k in range(0, step, 128):
                total += term[:, k:k + 128]
        logit = jnp.sum(total, axis=1, keepdims=True)
        dlogit = jnp.broadcast_to(jax.nn.sigmoid(logit) - labels[samples], (size, 128))
        grad = jnp.zeros((size, width), f32)
        for start in range(0, hidden_units, wide):
            dhidden = lanes([
                (dlogit * gated[samples, k:k + 128].astype(f32)).astype(bf16) for k in range(start, start + wide, 128)
            ])
            grad += lax.dot_general(
                dhidden, w_in_ref[:, start:start + wide], (((1,), (1,)), ((), ())), preferred_element_type=f32
            )
        out_ref[samples, :] = grad.astype(bf16)


def slot_grads_body(inc_t_ref, dpooled_ref, part_ref, send_ref, rows):
    owners, half, _ = send_ref.shape
    hot_dev = 2 * half
    hot_cols = owners * hot_dev
    slot_cap = part_ref.shape[1] - half
    me = core()
    rows[...] = jnp.dot(inc_t_ref[...], dpooled_ref[...], preferred_element_type=f32).astype(bf16)
    for t in range(owners):
        send_ref[t] = rows[half_rows(t, hot_dev, 1 - me), :]
        part_ref[t, 0:half, :] = rows[half_rows(t, hot_dev, me), :]
        part_ref[t, half:, :] = rows[hot_cols + t * slot_cap:hot_cols + (t + 1) * slot_cap, :]


def add_hot_body(part_ref, got_ref, out_ref):
    half = got_ref.shape[1]
    out_ref[:, 0:half, :] = (part_ref[:, 0:half, :].astype(f32) + got_ref[...].astype(f32)).astype(bf16)
    out_ref[:, half:, :] = part_ref[:, half:, :]


def collect_body(asked_ref, back_ref, out_ref):
    owners, slot_cap = asked_ref.shape
    half = back_ref.shape[1] - slot_cap
    out_ref[0:half, :] = jnp.sum(back_ref[:, 0:half, :].astype(f32), axis=0).astype(bf16)
    for t in range(owners):
        out_ref[half + t * slot_cap:half + (t + 1) * slot_cap, :] = back_ref[t, half:, :]
    asked = lanes([asked_ref[t:t + 1, :] for t in range(owners)])
    digit = lax.broadcasted_iota(i32, (TAIL, asked.shape[1]), 0)
    digits = jnp.where(digit == 0, asked >> 8, jnp.where(digit == 1, asked & 255, 0))
    out_ref[half + owners * slot_cap:, :] = digits.astype(f32).astype(bf16)


def hot_half(hot_ref, which):
    half = hot_ref.shape[1] // 2
    return jnp.where(which == 0, hot_ref[:, 0:half], hot_ref[:, half:])


def row_grads(which, hot_ref, part_refs, held, put, rows):
    size = part_refs[0].shape[0]
    half = hot_ref.shape[1] // 2
    me = lax.div(lax.axis_index("dp"), 2)
    count = len(part_refs)
    for s in range(count):
        held[pl.ds(pl.multiple_of((me ^ s) * size, 16), size), :] = part_refs[s][...]
    hot = jnp.concatenate([held[g * size:g * size + half, :] for g in range(count)], axis=0)
    ids = [lanes([hot_half(hot_ref, which)] * count)]
    parts = [hot]
    for g in range(count):
        digits = held[(g + 1) * size - TAIL:(g + 1) * size, :].astype(f32).astype(i32)
        ids.append(digits[0:1, :] * 256 + digits[1:2, :])
        parts.append(held[g * size + half:(g + 1) * size - TAIL, :])
    step = 128
    for start in range(0, rows, step):
        grad = 0.0
        for k in range(len(ids)):
            pick = one_hot(ids[k], (step, ids[k].shape[1]), 0, start)
            grad += jnp.dot(pick, parts[k], preferred_element_type=f32)
        put(slice(start, start + step), grad)


def own_grad_body(hot_ref, *refs):
    part_refs, (out_ref, held) = refs[:-2], refs[-2:]

    def put(at, grad):
        out_ref[at, :] = grad

    row_grads(core(), hot_ref, part_refs, held, put, out_ref.shape[0])


def adagrad(table, own_sum, grad):
    new_sum = own_sum + jnp.sum(grad * grad, axis=1, keepdims=True) * (1.0 / grad.shape[1])
    return table - grad * (learning_rate / jnp.sqrt(new_sum)), new_sum


def update_body(hot_ref, sum_ref, table_ref, grad_ref, *refs):
    part_refs, (new_table_ref, new_sum_ref, held, sums, staged, sems) = refs[:-6], refs[-6:]
    own_sum = sum_ref[...].T
    piece = table_ref.shape[0] // 2
    copies = []

    def put(at, grad):
        k = at.start // 128
        staged[at, :], sums[:, k:k + 1] = adagrad(table_ref[at, :], own_sum[:, k:k + 1], grad_ref[at, :] + grad)
        if at.stop % piece == 0:
            done = slice(at.stop - piece, at.stop)
            copies.append(pltpu.make_async_copy(staged.at[done], new_table_ref.at[done], sems.at[len(copies)]))
            copies[-1].start()

    row_grads(1 - core(), hot_ref, part_refs, held, put, table_ref.shape[0])
    new_sum_ref[...] = sums[...].T
    for copy in copies:
        copy.wait()


def dense_body(hot_ref, asked_ref, back_ref, out_ref):
    owners, slot_cap = asked_ref.shape
    half = back_ref.shape[1] - slot_cap
    rows = out_ref.shape[0]
    hot = jnp.sum(back_ref[:, 0:half, :].astype(f32), axis=0).astype(bf16)
    grad = jnp.dot(one_hot(hot_half(hot_ref, core()), (rows, half), 0), hot, preferred_element_type=f32)
    for t in range(owners):
        pick = one_hot(asked_ref[t:t + 1, :], (rows, slot_cap), 0)
        grad += jnp.dot(pick, back_ref[t, half:, :], preferred_element_type=f32)
    out_ref[...] = grad.astype(bf16)


def exchange(x):
    return lax.all_to_all(x, "table", split_axis=0, concat_axis=0, tiled=True)


def swap(x, bit):
    return lax.ppermute(x, "dp", [(g, g ^ bit) for g in range(lax.axis_size("dp"))])


def per_device(bag_slots, labels, cold_ids, cold_count, table, adagrad_sum, hot_ids, w_in, w_out):
    owners = lax.axis_size("table")
    groups = lax.axis_size("dp")
    hot_dev = hot_ids.shape[0]
    slot_cap = cold_ids.shape[2]
    batch = bag_slots.shape[0]
    rows, width = table.shape
    hidden_units = w_in.shape[1]
    half = hot_dev // 2
    vocab = owners * (hot_dev + slot_cap)
    shape = jax.ShapeDtypeStruct

    hot_row = hot_ids.reshape(1, hot_dev)
    asked = exchange(cold_ids[0])
    inc_t = call(
        functools.partial(incidence_body, owners * hot_dev, slot_cap),
        shape((vocab, batch), bf16),
        (cold_count, bag_slots.T),
        in_specs=[SMEM, VMEM],
    )
    inc = call(transpose_body, shape((batch, vocab), bf16), (inc_t,))
    hot, table_bf = call(
        pick_hot_body,
        (shape((hot_dev, width), bf16), shape((rows, width), bf16)),
        (hot_row, table),
        [pltpu.VMEM((1, hot_dev), i32), pltpu.VMEM((rows, width), f32), pltpu.SemaphoreType.DMA((2,))],
        in_specs=[HBM, HBM],
    )
    served = call(
        serve_body,
        shape((owners, half + slot_cap, width), bf16),
        (asked, hot, table_bf),
        [
            pltpu.VMEM((owners * slot_cap, rows), bf16),
            pltpu.VMEM((owners, half + slot_cap, width), bf16),
            pltpu.SemaphoreType.DMA,
        ],
        out_specs=HBM,
    )
    own_rows, inc, inc_t = lax.optimization_barrier((exchange(served), inc, inc_t))
    mate_rows = swap(call(first_rows_body, shape((owners, half, width), bf16), (own_rows,)), 1)
    dpooled = call(
        top_body,
        shape((batch, width), bf16),
        (labels.reshape(-1, 128), inc, own_rows, mate_rows, w_in, w_out.reshape(1, -1)),
        [pltpu.VMEM((batch, hidden_units), bf16), pltpu.VMEM((vocab, width), bf16)],
        mib=24,
    )
    part, to_mate = call(
        slot_grads_body,
        (shape((owners, half + slot_cap, width), bf16), shape((owners, half, width), bf16)),
        (inc_t, dpooled),
        [pltpu.VMEM((vocab, width), bf16)],
    )
    summed = call(add_hot_body, shape(part.shape, bf16), (part, swap(to_mate, 1)))
    returned = exchange(summed)
    size = half + owners * slot_cap + TAIL
    if groups & (groups - 1) == 0 and groups * size <= 2 * rows and owners * slot_cap == width:
        parts = {0: call(collect_body, shape((size, width), bf16), (asked, returned))}
        bit = groups // 2
        while bit > 1:
            parts.update({s ^ bit: swap(x, bit) for s, x in list(parts.items())})
            bit //= 2
        near = [parts[2 * y] for y in range(groups // 2)]
        far = [swap(x, 1) for x in near]
        held = pltpu.VMEM((groups // 2 * size, width), bf16)
        grad = call(own_grad_body, shape((rows, width), f32), (hot_row, *near), [held])
        new_table, new_sum = call(
            update_body,
            (shape((rows, width), f32), shape((rows // 128, 128), f32)),
            (hot_row, adagrad_sum.reshape(-1, 128), table, grad, *far),
            [
                held,
                pltpu.VMEM((128, rows // 128), f32),
                pltpu.VMEM((rows, width), f32),
                pltpu.SemaphoreType.DMA((2,)),
            ],
            out_specs=(HBM, VMEM),
        )
        return new_table, new_sum.reshape(rows)
    grad = call(dense_body, shape((rows, width), bf16), (hot_row, asked, returned))
    grad = lax.psum(grad, "dp").astype(f32)
    new_table, new_sum = adagrad(table, adagrad_sum[:, None], grad)
    return new_table, new_sum[:, 0]


def solution(mesh):
    placed = (
        P(("dp", "table"), None),
        P(("dp", "table")),
        P(("dp", "table"), None, None),
        P(("dp", "table"), None),
        P("table", None),
        P("table"),
        P("table"),
        P(),
        P(),
    )
    return jax.shard_map(
        per_device,
        mesh=mesh,
        in_specs=placed,
        out_specs=(P("table", None), P("table")),
        check_vma=False,
    )
```

```python
import functools
import math

import jax
import jax.numpy as jnp
from jax import lax
from jax.experimental import pallas as pl
from jax.experimental.pallas import tpu as pltpu
from jax.sharding import PartitionSpec as P

learning_rate = 0.3
f32, bf16, i32 = jnp.float32, jnp.bfloat16, jnp.int32
VMEM = pl.BlockSpec(memory_space=pltpu.VMEM)
HBM = pl.BlockSpec(memory_space=pltpu.HBM)
SMEM = pl.BlockSpec(memory_space=pltpu.SMEM)
FIELDS = 4
FIELD_BITS = 8
TAIL = 16


def call(body, outs, operands, scratch=(), in_specs=None, out_specs=None):
    held = jax.tree.leaves((outs, operands)) + [x for x in scratch if getattr(x, "memory_space", None) == pltpu.VMEM]
    limit = sum(math.prod(x.shape) * jnp.dtype(x.dtype).itemsize for x in held) + 4 * 1024 * 1024
    return pl.pallas_call(
        body,
        out_shape=outs,
        in_specs=in_specs or [VMEM] * len(operands),
        out_specs=out_specs or jax.tree.map(lambda _: VMEM, outs),
        scratch_shapes=list(scratch),
        compiler_params=pltpu.CompilerParams(vmem_limit_bytes=limit),
    )(*operands)


def lanes(pieces):
    return jnp.concatenate(pieces, axis=1)


def one_hot(ids, shape, axis, start=0):
    return (lax.broadcasted_iota(i32, shape, axis) + start == ids).astype(f32).astype(bf16)


def incidence_body(hot_cols, slot_cap, count_ref, slots_ref, inc_t_ref):
    vocab, batch = inc_t_ref.shape
    field = vocab // FIELDS
    step = 128
    row = lax.broadcasted_iota(i32, (field, step), 0)
    for start in range(0, batch, step):
        slots = slots_ref[:, start:start + step]
        key = jnp.where(slots < 0, -1, slots % field)
        unit = jnp.left_shift(jnp.ones_like(slots), FIELD_BITS * (slots // field))
        packed = jnp.zeros((field, step), i32)
        for entry in range(slots.shape[0]):
            packed += jnp.where(row == key[entry:entry + 1, :], unit[entry:entry + 1, :], 0)
        for k in range(FIELDS):
            part = jnp.right_shift(packed, FIELD_BITS * k) & (2**FIELD_BITS - 1)
            inc_t_ref[k * field:(k + 1) * field, start:start + step] = part.astype(f32).astype(bf16)
    place = lax.broadcasted_iota(i32, (slot_cap, batch), 0)
    for owner in range((vocab - hot_cols) // slot_cap):
        rows = pl.ds(hot_cols + owner * slot_cap, slot_cap)
        inc_t_ref[rows, :] = jnp.where(place < count_ref[0, owner], inc_t_ref[rows, :].astype(f32), 0.0).astype(bf16)


def transpose_body(x_ref, out_ref):
    out_ref[...] = x_ref[...].T


def core():
    return lax.rem(lax.axis_index("dp"), 2)


def half_rows(owner, hot_dev, which):
    half = hot_dev // 2
    return pl.ds(pl.multiple_of(owner * hot_dev + which * half, half), half)


def pick_hot_body(ids_ref, table_ref, hot_ref, table_bf_ref, ids, table, sems):
    copies = [pltpu.make_async_copy(ids_ref, ids, sems.at[0]), pltpu.make_async_copy(table_ref, table, sems.at[1])]
    for copy in copies:
        copy.start()
    for copy in copies:
        copy.wait()
    hot_dev = ids.shape[1]
    table_bf_ref[...] = table[...].astype(bf16)
    column = jnp.broadcast_to(ids[...], (8, hot_dev)).T[:, 0:1]
    pick = one_hot(column, (hot_dev, table.shape[0]), 1)
    hot_ref[...] = jnp.dot(pick, table_bf_ref[...], preferred_element_type=f32).astype(bf16)


def serve_body(asked_ref, hot_ref, table_ref, out_ref, pick, staged, sem):
    owners, slot_cap = asked_ref.shape
    hot_dev = hot_ref.shape[0]
    asked = asked_ref[...].T
    for t in range(owners):
        pick[t * slot_cap:(t + 1) * slot_cap, :] = one_hot(asked[:, t:t + 1], (slot_cap, table_ref.shape[0]), 1)
    picked = jnp.dot(pick[...], table_ref[...], preferred_element_type=f32).astype(bf16)
    hot = hot_ref[half_rows(0, hot_dev, core()), :]
    for t in range(owners):
        staged[t, 0:hot_dev // 2, :] = hot
        staged[t, hot_dev // 2:, :] = picked[t * slot_cap:(t + 1) * slot_cap]
    copy = pltpu.make_async_copy(staged, out_ref, sem)
    copy.start()
    copy.wait()


def first_rows_body(rows_ref, out_ref):
    out_ref[...] = rows_ref[:, 0:out_ref.shape[1], :]


def top_body(labels_ref, inc_ref, own_ref, mate_ref, w_in_ref, w_out_ref, out_ref, gated, rows):
    batch = inc_ref.shape[0]
    hidden_units, width = w_in_ref.shape[1], w_in_ref.shape[0]
    owners, half, _ = mate_ref.shape
    hot_dev = 2 * half
    hot_cols = owners * hot_dev
    slot_cap = own_ref.shape[1] - half
    me = core()
    for t in range(owners):
        rows[half_rows(t, hot_dev, me), :] = own_ref[t, 0:half, :]
        rows[half_rows(t, hot_dev, 1 - me), :] = mate_ref[t, 0:half, :]
        rows[hot_cols + t * slot_cap:hot_cols + (t + 1) * slot_cap, :] = own_ref[t, half:, :]
    labels = labels_ref[...].T
    labels = jnp.concatenate([labels[:, k:k + 1] for k in range(labels.shape[1])], axis=0)
    pooled = jnp.dot(inc_ref[...], rows[...], preferred_element_type=f32).astype(bf16)
    size, step, wide = batch // 2, 512, 2048
    w_out = w_out_ref[...].astype(f32)
    w_out = [lanes([w_out[k:k + 1, :] for k in range(r, r + step // 128)]) for r in range(0, hidden_units // 128, step // 128)]
    for at in range(0, batch, size):
        samples = slice(at, at + size)
        total = jnp.zeros((size, 128), f32)
        for start in range(0, hidden_units, step):
            cols = slice(start, start + step)
            pre_act = jnp.dot(pooled[samples], w_in_ref[:, cols], preferred_element_type=f32)
            own = w_out[start // step]
            gated[samples, cols] = jnp.where(pre_act > 0, own, 0.0).astype(bf16)
            term = jnp.maximum(pre_act, 0.0).astype(bf16).astype(f32) * own
            for k in range(0, step, 128):
                total += term[:, k:k + 128]
        logit = jnp.sum(total, axis=1, keepdims=True)
        dlogit = jnp.broadcast_to(jax.nn.sigmoid(logit) - labels[samples], (size, 128))
        grad = jnp.zeros((size, width), f32)
        for start in range(0, hidden_units, wide):
            dhidden = lanes([
                (dlogit * gated[samples, k:k + 128].astype(f32)).astype(bf16) for k in range(start, start + wide, 128)
            ])
            grad += lax.dot_general(
                dhidden, w_in_ref[:, start:start + wide], (((1,), (1,)), ((), ())), preferred_element_type=f32
            )
        out_ref[samples, :] = grad.astype(bf16)


def slot_grads_body(inc_t_ref, dpooled_ref, part_ref, send_ref, rows):
    owners, half, _ = send_ref.shape
    hot_dev = 2 * half
    hot_cols = owners * hot_dev
    slot_cap = part_ref.shape[1] - half
    me = core()
    rows[...] = jnp.dot(inc_t_ref[...], dpooled_ref[...], preferred_element_type=f32).astype(bf16)
    for t in range(owners):
        send_ref[t] = rows[half_rows(t, hot_dev, 1 - me), :]
        part_ref[t, 0:half, :] = rows[half_rows(t, hot_dev, me), :]
        part_ref[t, half:, :] = rows[hot_cols + t * slot_cap:hot_cols + (t + 1) * slot_cap, :]


def add_hot_body(part_ref, got_ref, out_ref):
    half = got_ref.shape[1]
    out_ref[:, 0:half, :] = (part_ref[:, 0:half, :].astype(f32) + got_ref[...].astype(f32)).astype(bf16)
    out_ref[:, half:, :] = part_ref[:, half:, :]


def collect_body(asked_ref, back_ref, out_ref):
    owners, slot_cap = asked_ref.shape
    half = back_ref.shape[1] - slot_cap
    out_ref[0:half, :] = jnp.sum(back_ref[:, 0:half, :].astype(f32), axis=0).astype(bf16)
    for t in range(owners):
        out_ref[half + t * slot_cap:half + (t + 1) * slot_cap, :] = back_ref[t, half:, :]
    asked = lanes([asked_ref[t:t + 1, :] for t in range(owners)])
    digit = lax.broadcasted_iota(i32, (TAIL, asked.shape[1]), 0)
    digits = jnp.where(digit == 0, asked >> 8, jnp.where(digit == 1, asked & 255, 0))
    out_ref[half + owners * slot_cap:, :] = digits.astype(f32).astype(bf16)


def hot_half(hot_ref, which):
    half = hot_ref.shape[1] // 2
    return jnp.where(which == 0, hot_ref[:, 0:half], hot_ref[:, half:])


def row_grads(which, hot_ref, part_refs, held, put, rows):
    size = part_refs[0].shape[0]
    half = hot_ref.shape[1] // 2
    me = lax.div(lax.axis_index("dp"), 2)
    count = len(part_refs)
    for s in range(count):
        held[pl.ds(pl.multiple_of((me ^ s) * size, 16), size), :] = part_refs[s][...]
    hot = jnp.concatenate([held[g * size:g * size + half, :] for g in range(count)], axis=0)
    ids = [lanes([hot_half(hot_ref, which)] * count)]
    parts = [hot]
    for g in range(count):
        digits = held[(g + 1) * size - TAIL:(g + 1) * size, :].astype(f32).astype(i32)
        ids.append(digits[0:1, :] * 256 + digits[1:2, :])
        parts.append(held[g * size + half:(g + 1) * size - TAIL, :])
    step = 128
    for start in range(0, rows, step):
        grad = 0.0
        for k in range(len(ids)):
            pick = one_hot(ids[k], (step, ids[k].shape[1]), 0, start)
            grad += jnp.dot(pick, parts[k], preferred_element_type=f32)
        put(slice(start, start + step), grad)


def own_grad_body(hot_ref, *refs):
    part_refs, (out_ref, held) = refs[:-2], refs[-2:]

    def put(at, grad):
        out_ref[at, :] = grad

    row_grads(core(), hot_ref, part_refs, held, put, out_ref.shape[0])


def update_body(hot_ref, sum_ref, table_ref, grad_ref, *refs):
    part_refs, (new_table_ref, new_sum_ref, held, squares, grads, staged, sums, sems) = refs[:-8], refs[-8:]
    rows, width = table_ref.shape
    step = 128

    def put(at, grad):
        grad = grad_ref[at, :] + grad
        grads[at, :] = grad
        squares[:, at.start // step:at.stop // step] = jnp.sum(grad * grad, axis=1, keepdims=True)

    row_grads(1 - core(), hot_ref, part_refs, held, put, rows)
    new_sum = sum_ref[...] + squares[...].T * (1.0 / width)
    sums[...] = new_sum
    copies = [pltpu.make_async_copy(sums, new_sum_ref, sems.at[0])]
    copies[0].start()
    scale = (learning_rate / jnp.sqrt(new_sum)).T
    for start in range(0, rows, step):
        at = slice(start, start + step)
        k = start // step
        staged[at, :] = table_ref[at, :] - grads[at, :] * scale[:, k:k + 1]
        if at.stop % (rows // 2) == 0:
            done = slice(at.stop - rows // 2, at.stop)
            copies.append(pltpu.make_async_copy(staged.at[done], new_table_ref.at[done], sems.at[len(copies)]))
            copies[-1].start()
    for copy in copies:
        copy.wait()


def dense_body(hot_ref, asked_ref, back_ref, out_ref):
    owners, slot_cap = asked_ref.shape
    half = back_ref.shape[1] - slot_cap
    rows = out_ref.shape[0]
    hot = jnp.sum(back_ref[:, 0:half, :].astype(f32), axis=0).astype(bf16)
    grad = jnp.dot(one_hot(hot_half(hot_ref, core()), (rows, half), 0), hot, preferred_element_type=f32)
    for t in range(owners):
        pick = one_hot(asked_ref[t:t + 1, :], (rows, slot_cap), 0)
        grad += jnp.dot(pick, back_ref[t, half:, :], preferred_element_type=f32)
    out_ref[...] = grad.astype(bf16)


def exchange(x):
    return lax.all_to_all(x, "table", split_axis=0, concat_axis=0, tiled=True)


def swap(x, bit):
    return lax.ppermute(x, "dp", [(g, g ^ bit) for g in range(lax.axis_size("dp"))])


def per_device(bag_slots, labels, cold_ids, cold_count, table, adagrad_sum, hot_ids, w_in, w_out):
    owners = lax.axis_size("table")
    groups = lax.axis_size("dp")
    hot_dev = hot_ids.shape[0]
    slot_cap = cold_ids.shape[2]
    batch = bag_slots.shape[0]
    rows, width = table.shape
    hidden_units = w_in.shape[1]
    half = hot_dev // 2
    vocab = owners * (hot_dev + slot_cap)
    shape = jax.ShapeDtypeStruct

    hot_row = hot_ids.reshape(1, hot_dev)
    asked = exchange(cold_ids[0])
    inc_t = call(
        functools.partial(incidence_body, owners * hot_dev, slot_cap),
        shape((vocab, batch), bf16),
        (cold_count, bag_slots.T),
        in_specs=[SMEM, VMEM],
    )
    inc = call(transpose_body, shape((batch, vocab), bf16), (inc_t,))
    hot, table_bf = call(
        pick_hot_body,
        (shape((hot_dev, width), bf16), shape((rows, width), bf16)),
        (hot_row, table),
        [pltpu.VMEM((1, hot_dev), i32), pltpu.VMEM((rows, width), f32), pltpu.SemaphoreType.DMA((2,))],
        in_specs=[HBM, HBM],
    )
    served = call(
        serve_body,
        shape((owners, half + slot_cap, width), bf16),
        (asked, hot, table_bf),
        [
            pltpu.VMEM((owners * slot_cap, rows), bf16),
            pltpu.VMEM((owners, half + slot_cap, width), bf16),
            pltpu.SemaphoreType.DMA,
        ],
        out_specs=HBM,
    )
    own_rows, inc, inc_t = lax.optimization_barrier((exchange(served), inc, inc_t))
    mate_rows = swap(call(first_rows_body, shape((owners, half, width), bf16), (own_rows,)), 1)
    dpooled = call(
        top_body,
        shape((batch, width), bf16),
        (labels.reshape(-1, 128), inc, own_rows, mate_rows, w_in, w_out.reshape(-1, 128)),
        [pltpu.VMEM((batch, hidden_units), bf16), pltpu.VMEM((vocab, width), bf16)],
    )
    part, to_mate = call(
        slot_grads_body,
        (shape((owners, half + slot_cap, width), bf16), shape((owners, half, width), bf16)),
        (inc_t, dpooled),
        [pltpu.VMEM((vocab, width), bf16)],
    )
    summed = call(add_hot_body, shape(part.shape, bf16), (part, swap(to_mate, 1)))
    returned = exchange(summed)
    size = half + owners * slot_cap + TAIL
    if groups & (groups - 1) == 0 and groups * size <= 2 * rows and owners * slot_cap == width:
        parts = {0: call(collect_body, shape((size, width), bf16), (asked, returned))}
        bit = groups // 2
        while bit > 1:
            parts.update({s ^ bit: swap(x, bit) for s, x in list(parts.items())})
            bit //= 2
        near = [parts[2 * y] for y in range(groups // 2)]
        far = [swap(x, 1) for x in near]
        held = pltpu.VMEM((groups // 2 * size, width), bf16)
        grad = call(own_grad_body, shape((rows, width), f32), (hot_row, *near), [held])
        new_table, new_sum = call(
            update_body,
            (shape((rows, width), f32), shape((rows // 128, 128), f32)),
            (hot_row, adagrad_sum.reshape(-1, 128), table, grad, *far),
            [
                held,
                pltpu.VMEM((128, rows // 128), f32),
                pltpu.VMEM((rows, width), f32),
                pltpu.VMEM((rows, width), f32),
                pltpu.VMEM((rows // 128, 128), f32),
                pltpu.SemaphoreType.DMA((3,)),
            ],
            out_specs=(HBM, HBM),
        )
        return new_table, new_sum.reshape(rows)
    grad = call(dense_body, shape((rows, width), bf16), (hot_row, asked, returned))
    grad = lax.psum(grad, "dp").astype(f32)
    new_sum = adagrad_sum + jnp.mean(grad * grad, axis=1)
    return table - learning_rate * grad / jnp.sqrt(new_sum)[:, None], new_sum


def solution(mesh):
    placed = (
        P(("dp", "table"), None),
        P(("dp", "table")),
        P(("dp", "table"), None, None),
        P(("dp", "table"), None),
        P("table", None),
        P("table"),
        P("table"),
        P(),
        P(),
    )
    return jax.shard_map(
        per_device,
        mesh=mesh,
        in_specs=placed,
        out_specs=(P("table", None), P("table")),
        check_vma=False,
    )
```

```python
import functools
import math

import jax
import jax.numpy as jnp
from jax import lax
from jax.experimental import pallas as pl
from jax.experimental.pallas import tpu as pltpu
from jax.sharding import PartitionSpec as P

learning_rate = 0.3
f32, bf16, i32 = jnp.float32, jnp.bfloat16, jnp.int32
VMEM = pl.BlockSpec(memory_space=pltpu.VMEM)
HBM = pl.BlockSpec(memory_space=pltpu.HBM)
SMEM = pl.BlockSpec(memory_space=pltpu.SMEM)
FIELDS = 4
FIELD_BITS = 8
TAIL = 16


def call(body, outs, operands, scratch=(), in_specs=None, out_specs=None):
    held = jax.tree.leaves((outs, operands)) + [x for x in scratch if getattr(x, "memory_space", None) == pltpu.VMEM]
    limit = sum(math.prod(x.shape) * jnp.dtype(x.dtype).itemsize for x in held) + 4 * 1024 * 1024
    return pl.pallas_call(
        body,
        out_shape=outs,
        in_specs=in_specs or [VMEM] * len(operands),
        out_specs=out_specs or jax.tree.map(lambda _: VMEM, outs),
        scratch_shapes=list(scratch),
        compiler_params=pltpu.CompilerParams(vmem_limit_bytes=limit),
    )(*operands)


def lanes(pieces):
    return jnp.concatenate(pieces, axis=1)


def one_hot(ids, shape, axis, start=0):
    return (lax.broadcasted_iota(i32, shape, axis) + start == ids).astype(f32).astype(bf16)


def incidence_body(hot_cols, slot_cap, count_ref, slots_ref, out_ref, inc_t_ref):
    vocab, batch = inc_t_ref.shape
    field = vocab // FIELDS
    step = 128
    row = lax.broadcasted_iota(i32, (field, step), 0)
    for start in range(0, batch, step):
        slots = slots_ref[:, start:start + step]
        key = jnp.where(slots < 0, -1, slots % field)
        unit = jnp.left_shift(jnp.ones_like(slots), FIELD_BITS * (slots // field))
        packed = jnp.zeros((field, step), i32)
        for entry in range(slots.shape[0]):
            packed += jnp.where(row == key[entry:entry + 1, :], unit[entry:entry + 1, :], 0)
        for k in range(FIELDS):
            part = jnp.right_shift(packed, FIELD_BITS * k) & (2**FIELD_BITS - 1)
            inc_t_ref[k * field:(k + 1) * field, start:start + step] = part.astype(f32).astype(bf16)
    place = lax.broadcasted_iota(i32, (slot_cap, batch), 0)
    for owner in range((vocab - hot_cols) // slot_cap):
        rows = pl.ds(hot_cols + owner * slot_cap, slot_cap)
        inc_t_ref[rows, :] = jnp.where(place < count_ref[0, owner], inc_t_ref[rows, :].astype(f32), 0.0).astype(bf16)
    out_ref[...] = inc_t_ref[...].T


def core():
    return lax.rem(lax.axis_index("dp"), 2)


def half_rows(owner, hot_dev, which):
    half = hot_dev // 2
    return pl.ds(pl.multiple_of(owner * hot_dev + which * half, half), half)


def pick_hot_body(ids_ref, table_ref, hot_ref, table_bf_ref, ids, table, sems):
    copies = [pltpu.make_async_copy(ids_ref, ids, sems.at[0]), pltpu.make_async_copy(table_ref, table, sems.at[1])]
    for copy in copies:
        copy.start()
    for copy in copies:
        copy.wait()
    hot_dev = ids.shape[1]
    table_bf_ref[...] = table[...].astype(bf16)
    column = jnp.broadcast_to(ids[...], (8, hot_dev)).T[:, 0:1]
    pick = one_hot(column, (hot_dev, table.shape[0]), 1)
    hot_ref[...] = jnp.dot(pick, table_bf_ref[...], preferred_element_type=f32).astype(bf16)


def serve_body(asked_ref, hot_ref, table_ref, out_ref, pick, staged, sem):
    owners, slot_cap = asked_ref.shape
    hot_dev = hot_ref.shape[0]
    asked = asked_ref[...].T
    for t in range(owners):
        pick[t * slot_cap:(t + 1) * slot_cap, :] = one_hot(asked[:, t:t + 1], (slot_cap, table_ref.shape[0]), 1)
    picked = jnp.dot(pick[...], table_ref[...], preferred_element_type=f32).astype(bf16)
    hot = hot_ref[half_rows(0, hot_dev, core()), :]
    for t in range(owners):
        staged[t, 0:hot_dev // 2, :] = hot
        staged[t, hot_dev // 2:, :] = picked[t * slot_cap:(t + 1) * slot_cap]
    copy = pltpu.make_async_copy(staged, out_ref, sem)
    copy.start()
    copy.wait()


def first_rows_body(rows_ref, out_ref):
    out_ref[...] = rows_ref[:, 0:out_ref.shape[1], :]


def top_body(labels_ref, inc_ref, own_ref, mate_ref, w_in_ref, w_out_ref, out_ref, gated, rows, pooled, total, dlogit):
    batch = inc_ref.shape[0]
    hidden_units, width = w_in_ref.shape[1], w_in_ref.shape[0]
    owners, half, _ = mate_ref.shape
    hot_dev = 2 * half
    hot_cols = owners * hot_dev
    slot_cap = own_ref.shape[1] - half
    me = core()
    step, wide = 512, 2048

    def stage(body):
        pl.when(me >= 0)(body)

    @stage
    def pool():
        for t in range(owners):
            rows[half_rows(t, hot_dev, me), :] = own_ref[t, 0:half, :]
            rows[half_rows(t, hot_dev, 1 - me), :] = mate_ref[t, 0:half, :]
            rows[hot_cols + t * slot_cap:hot_cols + (t + 1) * slot_cap, :] = own_ref[t, half:, :]
        pooled[...] = jnp.dot(inc_ref[...], rows[...], preferred_element_type=f32).astype(bf16)

    @stage
    def forward():
        w_out = w_out_ref[...].astype(f32)
        acc = jnp.zeros((batch, 128), f32)
        for start in range(0, hidden_units, step):
            cols = slice(start, start + step)
            pre_act = jnp.dot(pooled[...], w_in_ref[:, cols], preferred_element_type=f32)
            own = lanes([w_out[k:k + 1, :] for k in range(start // 128, (start + step) // 128)])
            gated[:, cols] = jnp.where(pre_act > 0, own, 0.0).astype(bf16)
            term = jnp.maximum(pre_act, 0.0).astype(bf16).astype(f32) * own
            for k in range(0, step, 128):
                acc += term[:, k:k + 128]
        total[...] = acc

    @stage
    def backward():
        blocks = batch // 128
        logit = lanes([jnp.sum(total[k * 128:(k + 1) * 128, :], axis=1, keepdims=True) for k in range(blocks)])
        delta = jax.nn.sigmoid(logit) - labels_ref[...].T
        for k in range(blocks):
            dlogit[k * 128:(k + 1) * 128, :] = jnp.broadcast_to(delta[:, k:k + 1], (128, 128))
        grad = jnp.zeros((batch, width), f32)
        for start in range(0, hidden_units, wide):
            dhidden = lanes([
                (dlogit[...] * gated[:, k:k + 128].astype(f32)).astype(bf16) for k in range(start, start + wide, 128)
            ])
            grad += lax.dot_general(
                dhidden, w_in_ref[:, start:start + wide], (((1,), (1,)), ((), ())), preferred_element_type=f32
            )
        out_ref[...] = grad.astype(bf16)


def slot_grads_body(inc_ref, dpooled_ref, part_ref, send_ref, rows):
    owners, half, _ = send_ref.shape
    hot_dev = 2 * half
    hot_cols = owners * hot_dev
    slot_cap = part_ref.shape[1] - half
    me = core()
    rows[...] = jnp.dot(inc_ref[...].T, dpooled_ref[...], preferred_element_type=f32).astype(bf16)
    for t in range(owners):
        send_ref[t] = rows[half_rows(t, hot_dev, 1 - me), :]
        part_ref[t, 0:half, :] = rows[half_rows(t, hot_dev, me), :]
        part_ref[t, half:, :] = rows[hot_cols + t * slot_cap:hot_cols + (t + 1) * slot_cap, :]


def add_hot_body(part_ref, got_ref, out_ref):
    half = got_ref.shape[1]
    out_ref[:, 0:half, :] = (part_ref[:, 0:half, :].astype(f32) + got_ref[...].astype(f32)).astype(bf16)
    out_ref[:, half:, :] = part_ref[:, half:, :]


def collect_body(asked_ref, back_ref, out_ref):
    owners, slot_cap = asked_ref.shape
    half = back_ref.shape[1] - slot_cap
    out_ref[0:half, :] = jnp.sum(back_ref[:, 0:half, :].astype(f32), axis=0).astype(bf16)
    for t in range(owners):
        out_ref[half + t * slot_cap:half + (t + 1) * slot_cap, :] = back_ref[t, half:, :]
    asked = lanes([asked_ref[t:t + 1, :] for t in range(owners)])
    digit = lax.broadcasted_iota(i32, (TAIL, asked.shape[1]), 0)
    digits = jnp.where(digit == 0, asked >> 8, jnp.where(digit == 1, asked & 255, 0))
    out_ref[half + owners * slot_cap:, :] = digits.astype(f32).astype(bf16)


def hot_half(hot_ref, which):
    half = hot_ref.shape[1] // 2
    return jnp.where(which == 0, hot_ref[:, 0:half], hot_ref[:, half:])


def row_grads(which, hot_ref, part_refs, held, put, pieces):
    size = part_refs[0].shape[0]
    half = hot_ref.shape[1] // 2
    me = lax.div(lax.axis_index("dp"), 2)
    count = len(part_refs)
    for s in range(count):
        held[pl.ds(pl.multiple_of((me ^ s) * size, 16), size), :] = part_refs[s][...]
    hot = jnp.concatenate([held[g * size:g * size + half, :] for g in range(count)], axis=0)
    ids = [lanes([hot_half(hot_ref, which)] * count)]
    parts = [hot]
    for g in range(count):
        digits = held[(g + 1) * size - TAIL:(g + 1) * size, :].astype(f32).astype(i32)
        ids.append(digits[0:1, :] * 256 + digits[1:2, :])
        parts.append(held[g * size + half:(g + 1) * size - TAIL, :])
    step = 128
    for piece, done in pieces:
        for start in range(piece.start, piece.stop, step):
            grad = 0.0
            for k in range(len(ids)):
                pick = one_hot(ids[k], (step, ids[k].shape[1]), 0, start)
                grad += jnp.dot(pick, parts[k], preferred_element_type=f32)
            put(slice(start, start + step), grad)
        done(piece)


def own_grad_body(hot_ref, *refs):
    part_refs, (out_ref, held) = refs[:-2], refs[-2:]

    def put(at, grad):
        out_ref[at, :] = grad

    row_grads(core(), hot_ref, part_refs, held, put, [(slice(0, out_ref.shape[0]), lambda piece: None)])


def update_body(hot_ref, sum_ref, table_ref, grad_ref, *refs):
    part_refs, (new_table_ref, new_sum_ref, held, squares, grads, staged, sums, sems) = refs[:-8], refs[-8:]
    rows, width = table_ref.shape
    step = 128

    def put(at, grad):
        grad = grad_ref[at, :] + grad
        grads[at, :] = grad
        squares[:, at.start // step:at.stop // step] = jnp.sum(grad * grad, axis=1, keepdims=True)

    copies = []

    def done(piece):
        lines = slice(piece.start // step, piece.stop // step)
        new_sum = sum_ref[lines, :] + squares[:, lines].T * (1.0 / width)
        sums[lines, :] = new_sum
        scale = (learning_rate / jnp.sqrt(new_sum)).T
        for start in range(piece.start, piece.stop, step):
            at = slice(start, start + step)
            k = (start - piece.start) // step
            staged[at, :] = table_ref[at, :] - grads[at, :] * scale[:, k:k + 1]
        copies.append(pltpu.make_async_copy(staged.at[piece], new_table_ref.at[piece], sems.at[len(copies)]))
        copies[-1].start()

    middle = rows // 2
    row_grads(1 - core(), hot_ref, part_refs, held, put, [(slice(0, middle), done), (slice(middle, rows), done)])
    copies.append(pltpu.make_async_copy(sums, new_sum_ref, sems.at[len(copies)]))
    copies[-1].start()
    for copy in copies:
        copy.wait()


def dense_body(hot_ref, asked_ref, back_ref, out_ref):
    owners, slot_cap = asked_ref.shape
    half = back_ref.shape[1] - slot_cap
    rows = out_ref.shape[0]
    hot = jnp.sum(back_ref[:, 0:half, :].astype(f32), axis=0).astype(bf16)
    grad = jnp.dot(one_hot(hot_half(hot_ref, core()), (rows, half), 0), hot, preferred_element_type=f32)
    for t in range(owners):
        pick = one_hot(asked_ref[t:t + 1, :], (rows, slot_cap), 0)
        grad += jnp.dot(pick, back_ref[t, half:, :], preferred_element_type=f32)
    out_ref[...] = grad.astype(bf16)


def exchange(x):
    return lax.all_to_all(x, "table", split_axis=0, concat_axis=0, tiled=True)


def swap(x, bit):
    return lax.ppermute(x, "dp", [(g, g ^ bit) for g in range(lax.axis_size("dp"))])


def per_device(bag_slots, labels, cold_ids, cold_count, table, adagrad_sum, hot_ids, w_in, w_out):
    owners = lax.axis_size("table")
    groups = lax.axis_size("dp")
    hot_dev = hot_ids.shape[0]
    slot_cap = cold_ids.shape[2]
    batch = bag_slots.shape[0]
    rows, width = table.shape
    hidden_units = w_in.shape[1]
    half = hot_dev // 2
    vocab = owners * (hot_dev + slot_cap)
    shape = jax.ShapeDtypeStruct

    hot_row = hot_ids.reshape(1, hot_dev)
    asked = exchange(cold_ids[0])
    inc = call(
        functools.partial(incidence_body, owners * hot_dev, slot_cap),
        shape((batch, vocab), bf16),
        (cold_count, bag_slots.T),
        [pltpu.VMEM((vocab, batch), bf16)],
        in_specs=[SMEM, VMEM],
    )
    hot, table_bf = call(
        pick_hot_body,
        (shape((hot_dev, width), bf16), shape((rows, width), bf16)),
        (hot_row, table),
        [pltpu.VMEM((1, hot_dev), i32), pltpu.VMEM((rows, width), f32), pltpu.SemaphoreType.DMA((2,))],
        in_specs=[HBM, HBM],
    )
    served = call(
        serve_body,
        shape((owners, half + slot_cap, width), bf16),
        (asked, hot, table_bf),
        [
            pltpu.VMEM((owners * slot_cap, rows), bf16),
            pltpu.VMEM((owners, half + slot_cap, width), bf16),
            pltpu.SemaphoreType.DMA,
        ],
        out_specs=HBM,
    )
    own_rows, inc = lax.optimization_barrier((exchange(served), inc))
    mate_rows = swap(call(first_rows_body, shape((owners, half, width), bf16), (own_rows,)), 1)
    dpooled = call(
        top_body,
        shape((batch, width), bf16),
        (labels.reshape(-1, 128), inc, own_rows, mate_rows, w_in, w_out.reshape(-1, 128)),
        [
            pltpu.VMEM((batch, hidden_units), bf16),
            pltpu.VMEM((vocab, width), bf16),
            pltpu.VMEM((batch, width), bf16),
            pltpu.VMEM((batch, 128), f32),
            pltpu.VMEM((batch, 128), f32),
        ],
    )
    part, to_mate = call(
        slot_grads_body,
        (shape((owners, half + slot_cap, width), bf16), shape((owners, half, width), bf16)),
        (inc, dpooled),
        [pltpu.VMEM((vocab, width), bf16)],
    )
    summed = call(add_hot_body, shape(part.shape, bf16), (part, swap(to_mate, 1)))
    returned = exchange(summed)
    size = half + owners * slot_cap + TAIL
    if groups & (groups - 1) == 0 and groups * size <= 2 * rows and owners * slot_cap == width:
        parts = {0: call(collect_body, shape((size, width), bf16), (asked, returned))}
        bit = groups // 2
        while bit > 1:
            parts.update({s ^ bit: swap(x, bit) for s, x in list(parts.items())})
            bit //= 2
        near = [parts[2 * y] for y in range(groups // 2)]
        far = [swap(x, 1) for x in near]
        held = pltpu.VMEM((groups // 2 * size, width), bf16)
        grad = call(own_grad_body, shape((rows, width), f32), (hot_row, *near), [held])
        new_table, new_sum = call(
            update_body,
            (shape((rows, width), f32), shape((rows // 128, 128), f32)),
            (hot_row, adagrad_sum.reshape(-1, 128), table, grad, *far),
            [
                held,
                pltpu.VMEM((128, rows // 128), f32),
                pltpu.VMEM((rows, width), f32),
                pltpu.VMEM((rows, width), f32),
                pltpu.VMEM((rows // 128, 128), f32),
                pltpu.SemaphoreType.DMA((3,)),
            ],
            out_specs=(HBM, HBM),
        )
        return new_table, new_sum.reshape(rows)
    grad = call(dense_body, shape((rows, width), bf16), (hot_row, asked, returned))
    grad = lax.psum(grad, "dp").astype(f32)
    new_sum = adagrad_sum + jnp.mean(grad * grad, axis=1)
    return table - learning_rate * grad / jnp.sqrt(new_sum)[:, None], new_sum


def solution(mesh):
    placed = (
        P(("dp", "table"), None),
        P(("dp", "table")),
        P(("dp", "table"), None, None),
        P(("dp", "table"), None),
        P("table", None),
        P("table"),
        P("table"),
        P(),
        P(),
    )
    return jax.shard_map(
        per_device,
        mesh=mesh,
        in_specs=placed,
        out_specs=(P("table", None), P("table")),
        check_vma=False,
    )
```

```python
import functools
import math

import jax
import jax.numpy as jnp
from jax import lax
from jax.experimental import pallas as pl
from jax.experimental.pallas import tpu as pltpu
from jax.sharding import PartitionSpec as P

learning_rate = 0.3
f32, bf16, i32 = jnp.float32, jnp.bfloat16, jnp.int32
VMEM = pl.BlockSpec(memory_space=pltpu.VMEM)
HBM = pl.BlockSpec(memory_space=pltpu.HBM)
SMEM = pl.BlockSpec(memory_space=pltpu.SMEM)
FIELDS = 4
FIELD_BITS = 8
TAIL = 16


def call(body, outs, operands, scratch=(), in_specs=None, out_specs=None):
    held = jax.tree.leaves((outs, operands)) + [x for x in scratch if getattr(x, "memory_space", None) == pltpu.VMEM]
    limit = sum(math.prod(x.shape) * jnp.dtype(x.dtype).itemsize for x in held) + 4 * 1024 * 1024
    return pl.pallas_call(
        body,
        out_shape=outs,
        in_specs=in_specs or [VMEM] * len(operands),
        out_specs=out_specs or jax.tree.map(lambda _: VMEM, outs),
        scratch_shapes=list(scratch),
        compiler_params=pltpu.CompilerParams(vmem_limit_bytes=limit),
    )(*operands)


def lanes(pieces):
    return jnp.concatenate(pieces, axis=1)


def one_hot(ids, shape, axis, start=0):
    return (lax.broadcasted_iota(i32, shape, axis) + start == ids).astype(f32).astype(bf16)


def incidence_body(hot_cols, slot_cap, count_ref, slots_ref, out_ref, inc_t_ref):
    vocab, batch = inc_t_ref.shape
    field = vocab // FIELDS
    step = 128
    row = lax.broadcasted_iota(i32, (field, step), 0)
    for start in range(0, batch, step):
        slots = slots_ref[:, start:start + step]
        key = jnp.where(slots < 0, -1, slots % field)
        unit = jnp.left_shift(jnp.ones_like(slots), FIELD_BITS * (slots // field))
        packed = jnp.zeros((field, step), i32)
        for entry in range(slots.shape[0]):
            packed += jnp.where(row == key[entry:entry + 1, :], unit[entry:entry + 1, :], 0)
        for k in range(FIELDS):
            part = jnp.right_shift(packed, FIELD_BITS * k) & (2**FIELD_BITS - 1)
            inc_t_ref[k * field:(k + 1) * field, start:start + step] = part.astype(f32).astype(bf16)
    place = lax.broadcasted_iota(i32, (slot_cap, batch), 0)
    for owner in range((vocab - hot_cols) // slot_cap):
        rows = pl.ds(hot_cols + owner * slot_cap, slot_cap)
        inc_t_ref[rows, :] = jnp.where(place < count_ref[0, owner], inc_t_ref[rows, :].astype(f32), 0.0).astype(bf16)
    out_ref[...] = inc_t_ref[...].T


def core():
    return lax.rem(lax.axis_index("dp"), 2)


def half_rows(owner, hot_dev, which):
    half = hot_dev // 2
    return pl.ds(pl.multiple_of(owner * hot_dev + which * half, half), half)


def pick_hot_body(ids_ref, table_ref, hot_ref, table_bf_ref, ids, table, sems):
    copies = [pltpu.make_async_copy(ids_ref, ids, sems.at[0]), pltpu.make_async_copy(table_ref, table, sems.at[1])]
    for copy in copies:
        copy.start()
    for copy in copies:
        copy.wait()
    hot_dev = ids.shape[1]
    table_bf_ref[...] = table[...].astype(bf16)
    column = jnp.broadcast_to(ids[...], (8, hot_dev)).T[:, 0:1]
    pick = one_hot(column, (hot_dev, table.shape[0]), 1)
    hot_ref[...] = jnp.dot(pick, table_bf_ref[...], preferred_element_type=f32).astype(bf16)


def serve_body(asked_ref, hot_ref, table_ref, out_ref, pick, staged, sem):
    owners, slot_cap = asked_ref.shape
    hot_dev = hot_ref.shape[0]
    asked = asked_ref[...].T
    for t in range(owners):
        pick[t * slot_cap:(t + 1) * slot_cap, :] = one_hot(asked[:, t:t + 1], (slot_cap, table_ref.shape[0]), 1)
    picked = jnp.dot(pick[...], table_ref[...], preferred_element_type=f32).astype(bf16)
    hot = hot_ref[half_rows(0, hot_dev, core()), :]
    for t in range(owners):
        staged[t, 0:hot_dev // 2, :] = hot
        staged[t, hot_dev // 2:, :] = picked[t * slot_cap:(t + 1) * slot_cap]
    copy = pltpu.make_async_copy(staged, out_ref, sem)
    copy.start()
    copy.wait()


def first_rows_body(rows_ref, out_ref):
    out_ref[...] = rows_ref[:, 0:out_ref.shape[1], :]


def top_body(labels_ref, inc_ref, own_ref, mate_ref, w_in_ref, w_out_ref, out_ref, gated, rows, pooled, total, dlogit):
    batch = inc_ref.shape[0]
    hidden_units, width = w_in_ref.shape[1], w_in_ref.shape[0]
    owners, half, _ = mate_ref.shape
    hot_dev = 2 * half
    hot_cols = owners * hot_dev
    slot_cap = own_ref.shape[1] - half
    me = core()
    size, step, wide = batch // 2, 512, 2048
    blocks = [slice(at, at + size) for at in range(0, batch, size)]
    for t in range(owners):
        rows[half_rows(t, hot_dev, me), :] = own_ref[t, 0:half, :]
        rows[half_rows(t, hot_dev, 1 - me), :] = mate_ref[t, 0:half, :]
        rows[hot_cols + t * slot_cap:hot_cols + (t + 1) * slot_cap, :] = own_ref[t, half:, :]
    pooled[...] = jnp.dot(inc_ref[...], rows[...], preferred_element_type=f32).astype(bf16)
    w_out = w_out_ref[...].astype(f32)
    for samples in blocks:
        acc = jnp.zeros((size, 128), f32)
        for start in range(0, hidden_units, step):
            cols = slice(start, start + step)
            pre_act = jnp.dot(pooled[samples, :], w_in_ref[:, cols], preferred_element_type=f32)
            own = lanes([w_out[k:k + 1, :] for k in range(start // 128, (start + step) // 128)])
            gated[samples, cols] = jnp.where(pre_act > 0, own, 0.0).astype(bf16)
            term = jnp.maximum(pre_act, 0.0).astype(bf16).astype(f32) * own
            for k in range(0, step, 128):
                acc += term[:, k:k + 128]
        total[samples, :] = acc
    lines = [slice(at, at + 128) for at in range(0, batch, 128)]
    logit = lanes([jnp.sum(total[line, :], axis=1, keepdims=True) for line in lines])
    delta = jax.nn.sigmoid(logit) - labels_ref[...].T
    for k, line in enumerate(lines):
        dlogit[line, :] = jnp.broadcast_to(delta[:, k:k + 1], (128, 128))
    for samples in blocks:
        scale = dlogit[samples, :]
        grad = jnp.zeros((size, width), f32)
        for start in range(0, hidden_units, wide):
            dhidden = lanes([
                (scale * gated[samples, k:k + 128].astype(f32)).astype(bf16) for k in range(start, start + wide, 128)
            ])
            grad += lax.dot_general(
                dhidden, w_in_ref[:, start:start + wide], (((1,), (1,)), ((), ())), preferred_element_type=f32
            )
        out_ref[samples, :] = grad.astype(bf16)


def slot_grads_body(inc_ref, dpooled_ref, part_ref, send_ref, rows):
    owners, half, _ = send_ref.shape
    hot_dev = 2 * half
    hot_cols = owners * hot_dev
    slot_cap = part_ref.shape[1] - half
    me = core()
    rows[...] = jnp.dot(inc_ref[...].T, dpooled_ref[...], preferred_element_type=f32).astype(bf16)
    for t in range(owners):
        send_ref[t] = rows[half_rows(t, hot_dev, 1 - me), :]
        part_ref[t, 0:half, :] = rows[half_rows(t, hot_dev, me), :]
        part_ref[t, half:, :] = rows[hot_cols + t * slot_cap:hot_cols + (t + 1) * slot_cap, :]


def add_hot_body(part_ref, got_ref, out_ref):
    half = got_ref.shape[1]
    out_ref[:, 0:half, :] = (part_ref[:, 0:half, :].astype(f32) + got_ref[...].astype(f32)).astype(bf16)
    out_ref[:, half:, :] = part_ref[:, half:, :]


def collect_body(asked_ref, back_ref, out_ref):
    owners, slot_cap = asked_ref.shape
    half = back_ref.shape[1] - slot_cap
    out_ref[0:half, :] = jnp.sum(back_ref[:, 0:half, :].astype(f32), axis=0).astype(bf16)
    for t in range(owners):
        out_ref[half + t * slot_cap:half + (t + 1) * slot_cap, :] = back_ref[t, half:, :]
    asked = lanes([asked_ref[t:t + 1, :] for t in range(owners)])
    digit = lax.broadcasted_iota(i32, (TAIL, asked.shape[1]), 0)
    digits = jnp.where(digit == 0, asked >> 8, jnp.where(digit == 1, asked & 255, 0))
    out_ref[half + owners * slot_cap:, :] = digits.astype(f32).astype(bf16)


def hot_half(hot_ref, which):
    half = hot_ref.shape[1] // 2
    return jnp.where(which == 0, hot_ref[:, 0:half], hot_ref[:, half:])


def row_grads(which, hot_ref, part_refs, held, put, rows):
    size = part_refs[0].shape[0]
    half = hot_ref.shape[1] // 2
    me = lax.div(lax.axis_index("dp"), 2)
    count = len(part_refs)
    for s in range(count):
        held[pl.ds(pl.multiple_of((me ^ s) * size, 16), size), :] = part_refs[s][...]
    hot = jnp.concatenate([held[g * size:g * size + half, :] for g in range(count)], axis=0)
    ids = [lanes([hot_half(hot_ref, which)] * count)]
    parts = [hot]
    for g in range(count):
        digits = held[(g + 1) * size - TAIL:(g + 1) * size, :].astype(f32).astype(i32)
        ids.append(digits[0:1, :] * 256 + digits[1:2, :])
        parts.append(held[g * size + half:(g + 1) * size - TAIL, :])
    step = 128
    for start in range(0, rows, step):
        grad = 0.0
        for k in range(len(ids)):
            pick = one_hot(ids[k], (step, ids[k].shape[1]), 0, start)
            grad += jnp.dot(pick, parts[k], preferred_element_type=f32)
        put(slice(start, start + step), grad)


def own_grad_body(hot_ref, *refs):
    part_refs, (out_ref, held) = refs[:-2], refs[-2:]

    def put(at, grad):
        out_ref[at, :] = grad

    row_grads(core(), hot_ref, part_refs, held, put, out_ref.shape[0])


def update_body(hot_ref, sum_ref, table_ref, grad_ref, *refs):
    part_refs, (new_table_ref, new_sum_ref, held, squares, grads, staged, sums, sems) = refs[:-8], refs[-8:]
    rows, width = table_ref.shape
    step = 128

    def put(at, grad):
        grad = grad_ref[at, :] + grad
        grads[at, :] = grad
        squares[:, at.start // step:at.stop // step] = jnp.sum(grad * grad, axis=1, keepdims=True)

    row_grads(1 - core(), hot_ref, part_refs, held, put, rows)
    new_sum = sum_ref[...] + squares[...].T * (1.0 / width)
    sums[...] = new_sum
    scale = (learning_rate / jnp.sqrt(new_sum)).T
    for start in range(0, rows, step):
        at = slice(start, start + step)
        k = start // step
        staged[at, :] = table_ref[at, :] - grads[at, :] * scale[:, k:k + 1]
    copies = [
        pltpu.make_async_copy(staged, new_table_ref, sems.at[0]),
        pltpu.make_async_copy(sums, new_sum_ref, sems.at[1]),
    ]
    for copy in copies:
        copy.start()
    for copy in copies:
        copy.wait()


def dense_body(hot_ref, asked_ref, back_ref, out_ref):
    owners, slot_cap = asked_ref.shape
    half = back_ref.shape[1] - slot_cap
    rows = out_ref.shape[0]
    hot = jnp.sum(back_ref[:, 0:half, :].astype(f32), axis=0).astype(bf16)
    grad = jnp.dot(one_hot(hot_half(hot_ref, core()), (rows, half), 0), hot, preferred_element_type=f32)
    for t in range(owners):
        pick = one_hot(asked_ref[t:t + 1, :], (rows, slot_cap), 0)
        grad += jnp.dot(pick, back_ref[t, half:, :], preferred_element_type=f32)
    out_ref[...] = grad.astype(bf16)


def exchange(x):
    return lax.all_to_all(x, "table", split_axis=0, concat_axis=0, tiled=True)


def swap(x, bit):
    return lax.ppermute(x, "dp", [(g, g ^ bit) for g in range(lax.axis_size("dp"))])


def per_device(bag_slots, labels, cold_ids, cold_count, table, adagrad_sum, hot_ids, w_in, w_out):
    owners = lax.axis_size("table")
    groups = lax.axis_size("dp")
    hot_dev = hot_ids.shape[0]
    slot_cap = cold_ids.shape[2]
    batch = bag_slots.shape[0]
    rows, width = table.shape
    hidden_units = w_in.shape[1]
    half = hot_dev // 2
    vocab = owners * (hot_dev + slot_cap)
    shape = jax.ShapeDtypeStruct

    hot_row = hot_ids.reshape(1, hot_dev)
    asked = exchange(cold_ids[0])
    inc = call(
        functools.partial(incidence_body, owners * hot_dev, slot_cap),
        shape((batch, vocab), bf16),
        (cold_count, bag_slots.T),
        [pltpu.VMEM((vocab, batch), bf16)],
        in_specs=[SMEM, VMEM],
    )
    hot, table_bf = call(
        pick_hot_body,
        (shape((hot_dev, width), bf16), shape((rows, width), bf16)),
        (hot_row, table),
        [pltpu.VMEM((1, hot_dev), i32), pltpu.VMEM((rows, width), f32), pltpu.SemaphoreType.DMA((2,))],
        in_specs=[HBM, HBM],
    )
    served = call(
        serve_body,
        shape((owners, half + slot_cap, width), bf16),
        (asked, hot, table_bf),
        [
            pltpu.VMEM((owners * slot_cap, rows), bf16),
            pltpu.VMEM((owners, half + slot_cap, width), bf16),
            pltpu.SemaphoreType.DMA,
        ],
        out_specs=HBM,
    )
    own_rows, inc = lax.optimization_barrier((exchange(served), inc))
    mate_rows = swap(call(first_rows_body, shape((owners, half, width), bf16), (own_rows,)), 1)
    dpooled = call(
        top_body,
        shape((batch, width), bf16),
        (labels.reshape(-1, 128), inc, own_rows, mate_rows, w_in, w_out.reshape(-1, 128)),
        [
            pltpu.VMEM((batch, hidden_units), bf16),
            pltpu.VMEM((vocab, width), bf16),
            pltpu.VMEM((batch, width), bf16),
            pltpu.VMEM((batch, 128), f32),
            pltpu.VMEM((batch, 128), f32),
        ],
    )
    part, to_mate = call(
        slot_grads_body,
        (shape((owners, half + slot_cap, width), bf16), shape((owners, half, width), bf16)),
        (inc, dpooled),
        [pltpu.VMEM((vocab, width), bf16)],
    )
    summed = call(add_hot_body, shape(part.shape, bf16), (part, swap(to_mate, 1)))
    returned = exchange(summed)
    size = half + owners * slot_cap + TAIL
    if groups & (groups - 1) == 0 and groups * size <= 2 * rows and owners * slot_cap == width:
        parts = {0: call(collect_body, shape((size, width), bf16), (asked, returned))}
        bit = groups // 2
        while bit > 1:
            parts.update({s ^ bit: swap(x, bit) for s, x in list(parts.items())})
            bit //= 2
        near = [parts[2 * y] for y in range(groups // 2)]
        far = [swap(x, 1) for x in near]
        held = pltpu.VMEM((groups // 2 * size, width), bf16)
        grad = call(own_grad_body, shape((rows, width), f32), (hot_row, *near), [held])
        new_table, new_sum = call(
            update_body,
            (shape((rows, width), f32), shape((rows // 128, 128), f32)),
            (hot_row, adagrad_sum.reshape(-1, 128), table, grad, *far),
            [
                held,
                pltpu.VMEM((128, rows // 128), f32),
                pltpu.VMEM((rows, width), f32),
                pltpu.VMEM((rows, width), f32),
                pltpu.VMEM((rows // 128, 128), f32),
                pltpu.SemaphoreType.DMA((2,)),
            ],
            out_specs=(HBM, HBM),
        )
        return new_table, new_sum.reshape(rows)
    grad = call(dense_body, shape((rows, width), bf16), (hot_row, asked, returned))
    grad = lax.psum(grad, "dp").astype(f32)
    new_sum = adagrad_sum + jnp.mean(grad * grad, axis=1)
    return table - learning_rate * grad / jnp.sqrt(new_sum)[:, None], new_sum


def solution(mesh):
    placed = (
        P(("dp", "table"), None),
        P(("dp", "table")),
        P(("dp", "table"), None, None),
        P(("dp", "table"), None),
        P("table", None),
        P("table"),
        P("table"),
        P(),
        P(),
    )
    return jax.shard_map(
        per_device,
        mesh=mesh,
        in_specs=placed,
        out_specs=(P("table", None), P("table")),
        check_vma=False,
    )
```

```python
import functools
import math

import jax
import jax.numpy as jnp
from jax import lax
from jax.experimental import pallas as pl
from jax.experimental.pallas import tpu as pltpu
from jax.sharding import PartitionSpec as P

learning_rate = 0.3
f32, bf16, i32 = jnp.float32, jnp.bfloat16, jnp.int32
VMEM = pl.BlockSpec(memory_space=pltpu.VMEM)
HBM = pl.BlockSpec(memory_space=pltpu.HBM)
SMEM = pl.BlockSpec(memory_space=pltpu.SMEM)
FIELDS = 4
FIELD_BITS = 8
TAIL = 16


def call(body, outs, operands, scratch=(), in_specs=None, out_specs=None):
    held = jax.tree.leaves((outs, operands)) + [x for x in scratch if getattr(x, "memory_space", None) == pltpu.VMEM]
    limit = sum(math.prod(x.shape) * jnp.dtype(x.dtype).itemsize for x in held) + 4 * 1024 * 1024
    return pl.pallas_call(
        body,
        out_shape=outs,
        in_specs=in_specs or [VMEM] * len(operands),
        out_specs=out_specs or jax.tree.map(lambda _: VMEM, outs),
        scratch_shapes=list(scratch),
        compiler_params=pltpu.CompilerParams(vmem_limit_bytes=limit),
    )(*operands)


def lanes(pieces):
    return jnp.concatenate(pieces, axis=1)


def one_hot(ids, shape, axis, start=0):
    return (lax.broadcasted_iota(i32, shape, axis) + start == ids).astype(f32).astype(bf16)


def incidence_body(hot_dev, slot_cap, count_ref, slots_ref, out_ref, inc_t_ref):
    vocab, batch = inc_t_ref.shape
    owners = vocab // (hot_dev + slot_cap)
    half = hot_dev // 2
    hot_cols = owners * hot_dev
    me = core()
    field = vocab // FIELDS
    step = 128
    row = lax.broadcasted_iota(i32, (field, step), 0)
    for start in range(0, batch, step):
        slots = slots_ref[:, start:start + step]
        place = slots % hot_dev
        hot = jnp.where(place // half == me, 0, owners * half) + (slots // hot_dev) * half + place % half
        column = jnp.where(slots < hot_cols, hot, slots)
        key = jnp.where(slots < 0, -1, column % field)
        unit = jnp.left_shift(jnp.ones_like(slots), FIELD_BITS * (column // field))
        packed = jnp.zeros((field, step), i32)
        for entry in range(slots.shape[0]):
            packed += jnp.where(row == key[entry:entry + 1, :], unit[entry:entry + 1, :], 0)
        for k in range(FIELDS):
            part = jnp.right_shift(packed, FIELD_BITS * k) & (2**FIELD_BITS - 1)
            inc_t_ref[k * field:(k + 1) * field, start:start + step] = part.astype(f32).astype(bf16)
    place = lax.broadcasted_iota(i32, (slot_cap, batch), 0)
    for owner in range(owners):
        rows = pl.ds(hot_cols + owner * slot_cap, slot_cap)
        inc_t_ref[rows, :] = jnp.where(place < count_ref[0, owner], inc_t_ref[rows, :].astype(f32), 0.0).astype(bf16)
    out_ref[...] = inc_t_ref[...].T


def core():
    return lax.rem(lax.axis_index("dp"), 2)


def pick_hot_body(ids_ref, table_ref, hot_ref, table_bf_ref, ids, table, sems):
    copies = [pltpu.make_async_copy(ids_ref, ids, sems.at[0]), pltpu.make_async_copy(table_ref, table, sems.at[1])]
    for copy in copies:
        copy.start()
    for copy in copies:
        copy.wait()
    hot_dev = ids.shape[1]
    table_bf_ref[...] = table[...].astype(bf16)
    column = jnp.broadcast_to(ids[...], (8, hot_dev)).T[:, 0:1]
    pick = one_hot(column, (hot_dev, table.shape[0]), 1)
    hot_ref[...] = jnp.dot(pick, table_bf_ref[...], preferred_element_type=f32).astype(bf16)


def serve_body(asked_ref, hot_ref, table_ref, out_ref, pick, staged, sem):
    owners, slot_cap = asked_ref.shape
    hot_dev = hot_ref.shape[0]
    asked = asked_ref[...].T
    for t in range(owners):
        pick[t * slot_cap:(t + 1) * slot_cap, :] = one_hot(asked[:, t:t + 1], (slot_cap, table_ref.shape[0]), 1)
    picked = jnp.dot(pick[...], table_ref[...], preferred_element_type=f32).astype(bf16)
    half = hot_dev // 2
    hot = hot_ref[pl.ds(pl.multiple_of(core() * half, half), half), :]
    for t in range(owners):
        staged[t, 0:half, :] = hot
        staged[t, half:, :] = picked[t * slot_cap:(t + 1) * slot_cap]
    copy = pltpu.make_async_copy(staged, out_ref, sem)
    copy.start()
    copy.wait()


def first_rows_body(rows_ref, out_ref):
    out_ref[...] = rows_ref[:, 0:out_ref.shape[1], :]


def top_body(labels_ref, inc_ref, own_ref, mate_ref, w_in_ref, w_out_ref, out_ref, hidden, rows, pooled, total, dlogit):
    batch = inc_ref.shape[0]
    hidden_units, width = w_in_ref.shape[1], w_in_ref.shape[0]
    owners, half, _ = mate_ref.shape
    hot_half = owners * half
    slot_cap = own_ref.shape[1] - half
    size, step, wide = batch // 2, 512, 2048
    blocks = [slice(at, at + size) for at in range(0, batch, size)]
    rows[hot_half:2 * hot_half, :] = mate_ref[...].reshape(hot_half, width)
    for t in range(owners):
        rows[t * half:(t + 1) * half, :] = own_ref[t, 0:half, :]
        rows[2 * hot_half + t * slot_cap:2 * hot_half + (t + 1) * slot_cap, :] = own_ref[t, half:, :]
    pooled[...] = jnp.dot(inc_ref[...], rows[...], preferred_element_type=f32).astype(bf16)
    w_out = w_out_ref[...].astype(f32)
    for samples in blocks:
        acc = jnp.zeros((size, 128), f32)
        for start in range(0, hidden_units, step):
            cols = slice(start, start + step)
            pre_act = jnp.dot(pooled[samples, :], w_in_ref[:, cols], preferred_element_type=f32)
            own = lanes([w_out[k:k + 1, :] for k in range(start // 128, (start + step) // 128)])
            act = jnp.maximum(pre_act, 0.0).astype(bf16)
            hidden[samples, cols] = act
            term = act.astype(f32) * own
            for k in range(0, step, 128):
                acc += term[:, k:k + 128]
        total[samples, :] = acc
    lines = [slice(at, at + 128) for at in range(0, batch, 128)]
    logit = lanes([jnp.sum(total[line, :], axis=1, keepdims=True) for line in lines])
    delta = jax.nn.sigmoid(logit) - labels_ref[...].T
    for k, line in enumerate(lines):
        dlogit[line, :] = jnp.broadcast_to(delta[:, k:k + 1], (128, 128))
    for samples in blocks:
        scale = dlogit[samples, :]
        grad = jnp.zeros((size, width), f32)
        for start in range(0, hidden_units, wide):
            dhidden = lanes([
                jnp.where(
                    hidden[samples, k:k + 128].astype(f32) > 0, scale * w_out[k // 128:k // 128 + 1, :], 0.0
                ).astype(bf16)
                for k in range(start, start + wide, 128)
            ])
            grad += lax.dot_general(
                dhidden, w_in_ref[:, start:start + wide], (((1,), (1,)), ((), ())), preferred_element_type=f32
            )
        out_ref[samples, :] = grad.astype(bf16)


def mate_grads_body(inc_ref, dpooled_ref, out_ref):
    hot_half = out_ref.shape[0]
    out_ref[...] = jnp.dot(
        inc_ref[:, hot_half:2 * hot_half].T, dpooled_ref[...], preferred_element_type=f32
    ).astype(bf16)


def own_grads_body(inc_ref, dpooled_ref, hot_ref, cold_ref):
    hot_half = hot_ref.shape[0]
    dpooled = dpooled_ref[...]
    hot_ref[...] = jnp.dot(inc_ref[:, 0:hot_half].T, dpooled, preferred_element_type=f32)
    cold_ref[...] = jnp.dot(inc_ref[:, 2 * hot_half:].T, dpooled, preferred_element_type=f32).astype(bf16)


def pack_grads_body(hot_ref, got_ref, cold_ref, out_ref):
    owners, half, width = got_ref.shape
    hot = hot_ref[...] + got_ref[...].reshape(owners * half, width).astype(f32)
    slot_cap = out_ref.shape[1] - half
    for t in range(owners):
        out_ref[t, 0:half, :] = hot[t * half:(t + 1) * half].astype(bf16)
        out_ref[t, half:, :] = cold_ref[t * slot_cap:(t + 1) * slot_cap, :]


def collect_body(asked_ref, back_ref, out_ref):
    owners, slot_cap = asked_ref.shape
    half = back_ref.shape[1] - slot_cap
    out_ref[0:half, :] = jnp.sum(back_ref[:, 0:half, :].astype(f32), axis=0).astype(bf16)
    for t in range(owners):
        out_ref[half + t * slot_cap:half + (t + 1) * slot_cap, :] = back_ref[t, half:, :]
    asked = lanes([asked_ref[t:t + 1, :] for t in range(owners)])
    digit = lax.broadcasted_iota(i32, (TAIL, asked.shape[1]), 0)
    digits = jnp.where(digit == 0, asked >> 8, jnp.where(digit == 1, asked & 255, 0))
    out_ref[half + owners * slot_cap:, :] = digits.astype(f32).astype(bf16)


def hot_half(hot_ref, which):
    half = hot_ref.shape[1] // 2
    return jnp.where(which == 0, hot_ref[:, 0:half], hot_ref[:, half:])


def row_grads(which, hot_ref, part_refs, held, put, rows):
    size = part_refs[0].shape[0]
    half = hot_ref.shape[1] // 2
    me = lax.div(lax.axis_index("dp"), 2)
    count = len(part_refs)
    for s in range(count):
        held[pl.ds(pl.multiple_of((me ^ s) * size, 16), size), :] = part_refs[s][...]
    hot = jnp.concatenate([held[g * size:g * size + half, :] for g in range(count)], axis=0)
    ids = [lanes([hot_half(hot_ref, which)] * count)]
    parts = [hot]
    for g in range(count):
        digits = held[(g + 1) * size - TAIL:(g + 1) * size, :].astype(f32).astype(i32)
        ids.append(digits[0:1, :] * 256 + digits[1:2, :])
        parts.append(held[g * size + half:(g + 1) * size - TAIL, :])
    step = 128
    for start in range(0, rows, step):
        grad = 0.0
        for k in range(len(ids)):
            pick = one_hot(ids[k], (step, ids[k].shape[1]), 0, start)
            grad += jnp.dot(pick, parts[k], preferred_element_type=f32)
        put(slice(start, start + step), grad)


def own_grad_body(hot_ref, *refs):
    part_refs, (out_ref, held) = refs[:-2], refs[-2:]

    def put(at, grad):
        out_ref[at, :] = grad

    row_grads(core(), hot_ref, part_refs, held, put, out_ref.shape[0])


def update_body(hot_ref, sum_ref, table_ref, grad_ref, *refs):
    part_refs, (new_table_ref, new_sum_ref, held, squares, grads, staged, sums, sems) = refs[:-8], refs[-8:]
    rows, width = table_ref.shape
    step = 128

    def put(at, grad):
        grad = grad_ref[at, :] + grad
        grads[at, :] = grad
        squares[:, at.start // step:at.stop // step] = jnp.sum(grad * grad, axis=1, keepdims=True)

    row_grads(1 - core(), hot_ref, part_refs, held, put, rows)
    new_sum = sum_ref[...] + squares[...].T * (1.0 / width)
    sums[...] = new_sum
    scale = (learning_rate / jnp.sqrt(new_sum)).T
    for start in range(0, rows, step):
        at = slice(start, start + step)
        k = start // step
        staged[at, :] = table_ref[at, :] - grads[at, :] * scale[:, k:k + 1]
    copies = [
        pltpu.make_async_copy(staged, new_table_ref, sems.at[0]),
        pltpu.make_async_copy(sums, new_sum_ref, sems.at[1]),
    ]
    for copy in copies:
        copy.start()
    for copy in copies:
        copy.wait()


def dense_body(hot_ref, asked_ref, back_ref, out_ref):
    owners, slot_cap = asked_ref.shape
    half = back_ref.shape[1] - slot_cap
    rows = out_ref.shape[0]
    hot = jnp.sum(back_ref[:, 0:half, :].astype(f32), axis=0).astype(bf16)
    grad = jnp.dot(one_hot(hot_half(hot_ref, core()), (rows, half), 0), hot, preferred_element_type=f32)
    for t in range(owners):
        pick = one_hot(asked_ref[t:t + 1, :], (rows, slot_cap), 0)
        grad += jnp.dot(pick, back_ref[t, half:, :], preferred_element_type=f32)
    out_ref[...] = grad.astype(bf16)


def exchange(x):
    return lax.all_to_all(x, "table", split_axis=0, concat_axis=0, tiled=True)


def swap(x, bit):
    return lax.ppermute(x, "dp", [(g, g ^ bit) for g in range(lax.axis_size("dp"))])


def per_device(bag_slots, labels, cold_ids, cold_count, table, adagrad_sum, hot_ids, w_in, w_out):
    owners = lax.axis_size("table")
    groups = lax.axis_size("dp")
    hot_dev = hot_ids.shape[0]
    slot_cap = cold_ids.shape[2]
    batch = bag_slots.shape[0]
    rows, width = table.shape
    hidden_units = w_in.shape[1]
    half = hot_dev // 2
    vocab = owners * (hot_dev + slot_cap)
    shape = jax.ShapeDtypeStruct

    hot_row = hot_ids.reshape(1, hot_dev)
    asked = exchange(cold_ids[0])
    inc = call(
        functools.partial(incidence_body, hot_dev, slot_cap),
        shape((batch, vocab), bf16),
        (cold_count, bag_slots.T),
        [pltpu.VMEM((vocab, batch), bf16)],
        in_specs=[SMEM, VMEM],
    )
    hot, table_bf = call(
        pick_hot_body,
        (shape((hot_dev, width), bf16), shape((rows, width), bf16)),
        (hot_row, table),
        [pltpu.VMEM((1, hot_dev), i32), pltpu.VMEM((rows, width), f32), pltpu.SemaphoreType.DMA((2,))],
        in_specs=[HBM, HBM],
    )
    served = call(
        serve_body,
        shape((owners, half + slot_cap, width), bf16),
        (asked, hot, table_bf),
        [
            pltpu.VMEM((owners * slot_cap, rows), bf16),
            pltpu.VMEM((owners, half + slot_cap, width), bf16),
            pltpu.SemaphoreType.DMA,
        ],
        out_specs=HBM,
    )
    own_rows, inc = lax.optimization_barrier((exchange(served), inc))
    mate_rows = swap(call(first_rows_body, shape((owners, half, width), bf16), (own_rows,)), 1)
    dpooled = call(
        top_body,
        shape((batch, width), bf16),
        (labels.reshape(-1, 128), inc, own_rows, mate_rows, w_in, w_out.reshape(-1, 128)),
        [
            pltpu.VMEM((batch, hidden_units), bf16),
            pltpu.VMEM((vocab, width), bf16),
            pltpu.VMEM((batch, width), bf16),
            pltpu.VMEM((batch, 128), f32),
            pltpu.VMEM((batch, 128), f32),
        ],
    )
    hot_half = owners * half
    to_mate = call(mate_grads_body, shape((hot_half, width), bf16), (inc, dpooled))
    got = swap(to_mate.reshape(owners, half, width), 1)
    hot_grads, cold_grads = call(
        own_grads_body,
        (shape((hot_half, width), f32), shape((owners * slot_cap, width), bf16)),
        (inc, dpooled),
    )
    summed = call(pack_grads_body, shape((owners, half + slot_cap, width), bf16), (hot_grads, got, cold_grads))
    returned = exchange(summed)
    size = half + owners * slot_cap + TAIL
    if groups & (groups - 1) == 0 and groups * size <= 2 * rows and owners * slot_cap == width:
        parts = {0: call(collect_body, shape((size, width), bf16), (asked, returned))}
        bit = groups // 2
        while bit > 1:
            parts.update({s ^ bit: swap(x, bit) for s, x in list(parts.items())})
            bit //= 2
        near = [parts[2 * y] for y in range(groups // 2)]
        far = [swap(x, 1) for x in near]
        held = pltpu.VMEM((groups // 2 * size, width), bf16)
        grad = call(own_grad_body, shape((rows, width), f32), (hot_row, *near), [held])
        new_table, new_sum = call(
            update_body,
            (shape((rows, width), f32), shape((rows // 128, 128), f32)),
            (hot_row, adagrad_sum.reshape(-1, 128), table, grad, *far),
            [
                held,
                pltpu.VMEM((128, rows // 128), f32),
                pltpu.VMEM((rows, width), f32),
                pltpu.VMEM((rows, width), f32),
                pltpu.VMEM((rows // 128, 128), f32),
                pltpu.SemaphoreType.DMA((2,)),
            ],
            out_specs=(HBM, HBM),
        )
        return new_table, new_sum.reshape(rows)
    grad = call(dense_body, shape((rows, width), bf16), (hot_row, asked, returned))
    grad = lax.psum(grad, "dp").astype(f32)
    new_sum = adagrad_sum + jnp.mean(grad * grad, axis=1)
    return table - learning_rate * grad / jnp.sqrt(new_sum)[:, None], new_sum


def solution(mesh):
    placed = (
        P(("dp", "table"), None),
        P(("dp", "table")),
        P(("dp", "table"), None, None),
        P(("dp", "table"), None),
        P("table", None),
        P("table"),
        P("table"),
        P(),
        P(),
    )
    return jax.shard_map(
        per_device,
        mesh=mesh,
        in_specs=placed,
        out_specs=(P("table", None), P("table")),
        check_vma=False,
    )
```

```python
import functools
import math

import jax
import jax.numpy as jnp
from jax import lax
from jax.experimental import pallas as pl
from jax.experimental.pallas import tpu as pltpu
from jax.sharding import PartitionSpec as P

learning_rate = 0.3
f32, bf16, i32 = jnp.float32, jnp.bfloat16, jnp.int32
VMEM = pl.BlockSpec(memory_space=pltpu.VMEM)
HBM = pl.BlockSpec(memory_space=pltpu.HBM)
SMEM = pl.BlockSpec(memory_space=pltpu.SMEM)
FIELDS = 4
FIELD_BITS = 8
TAIL = 16


def call(body, outs, operands, scratch=(), in_specs=None, out_specs=None):
    held = jax.tree.leaves((outs, operands)) + [x for x in scratch if getattr(x, "memory_space", None) == pltpu.VMEM]
    limit = sum(math.prod(x.shape) * jnp.dtype(x.dtype).itemsize for x in held) + 4 * 1024 * 1024
    return pl.pallas_call(
        body,
        out_shape=outs,
        in_specs=in_specs or [VMEM] * len(operands),
        out_specs=out_specs or jax.tree.map(lambda _: VMEM, outs),
        scratch_shapes=list(scratch),
        compiler_params=pltpu.CompilerParams(vmem_limit_bytes=limit),
    )(*operands)


def lanes(pieces):
    return jnp.concatenate(pieces, axis=1)


def one_hot(ids, shape, axis, start=0):
    return (lax.broadcasted_iota(i32, shape, axis) + start == ids).astype(f32).astype(bf16)


def count_body(hot_dev, count_ref, slots_ref, packed_ref):
    field, batch = packed_ref.shape
    owners = count_ref.shape[1]
    slot_cap = FIELDS * field // owners - hot_dev
    half = hot_dev // 2
    hot_cols = owners * hot_dev
    me = core()
    step = 128
    row = lax.broadcasted_iota(i32, (field, step), 0)
    for start in range(0, batch, step):
        slots = slots_ref[:, start:start + step]
        place = slots % hot_dev
        hot = jnp.where(place // half == me, 0, owners * half) + (slots // hot_dev) * half + place % half
        column = jnp.where(slots < hot_cols, hot, slots)
        cold = slots - hot_cols
        live = slots >= 0
        for t in range(owners):
            at = cold - t * slot_cap
            live = live & ((at < count_ref[0, t]) | (at >= slot_cap))
        key = jnp.where(live, column % field, -1)
        unit = jnp.left_shift(jnp.ones_like(slots), FIELD_BITS * (column // field))
        packed = jnp.zeros((field, step), i32)
        for entry in range(slots.shape[0]):
            packed += jnp.where(row == key[entry:entry + 1, :], unit[entry:entry + 1, :], 0)
        packed_ref[:, start:start + step] = packed


def incidence_body(packed_ref, out_ref, inc_t_ref):
    field = packed_ref.shape[0]
    for k in range(FIELDS):
        part = jnp.right_shift(packed_ref[...], FIELD_BITS * k) & (2**FIELD_BITS - 1)
        inc_t_ref[k * field:(k + 1) * field, :] = part.astype(f32).astype(bf16)
    out_ref[...] = inc_t_ref[...].T


def core():
    return lax.rem(lax.axis_index("dp"), 2)


def pick_hot_body(ids_ref, table_ref, hot_ref, table_bf_ref, ids, table, sems):
    copies = [pltpu.make_async_copy(ids_ref, ids, sems.at[0]), pltpu.make_async_copy(table_ref, table, sems.at[1])]
    for copy in copies:
        copy.start()
    for copy in copies:
        copy.wait()
    hot_dev = ids.shape[1]
    table_bf_ref[...] = table[...].astype(bf16)
    column = jnp.broadcast_to(ids[...], (8, hot_dev)).T[:, 0:1]
    pick = one_hot(column, (hot_dev, table.shape[0]), 1)
    hot_ref[...] = jnp.dot(pick, table_bf_ref[...], preferred_element_type=f32).astype(bf16)


def serve_body(asked_ref, hot_ref, table_ref, out_ref, pick):
    owners, slot_cap = asked_ref.shape
    half = hot_ref.shape[0] // 2
    asked = asked_ref[...].T
    for t in range(owners):
        pick[t * slot_cap:(t + 1) * slot_cap, :] = one_hot(asked[:, t:t + 1], (slot_cap, table_ref.shape[0]), 1)
    picked = jnp.dot(pick[...], table_ref[...], preferred_element_type=f32).astype(bf16)
    hot = hot_ref[pl.ds(pl.multiple_of(core() * half, half), half), :]
    for t in range(owners):
        out_ref[t, 0:half, :] = hot
        out_ref[t, half:, :] = picked[t * slot_cap:(t + 1) * slot_cap]


def first_rows_body(rows_ref, out_ref):
    out_ref[...] = rows_ref[:, 0:out_ref.shape[1], :]


def top_body(labels_ref, inc_ref, own_ref, mate_ref, w_in_ref, w_out_ref, out_ref, hidden, rows, pooled, total, dlogit):
    batch = inc_ref.shape[0]
    hidden_units, width = w_in_ref.shape[1], w_in_ref.shape[0]
    owners, half, _ = mate_ref.shape
    hot_half = owners * half
    slot_cap = own_ref.shape[1] - half
    size, step, wide = batch // 2, 512, 2048
    blocks = [slice(at, at + size) for at in range(0, batch, size)]
    rows[hot_half:2 * hot_half, :] = mate_ref[...].reshape(hot_half, width)
    for t in range(owners):
        rows[t * half:(t + 1) * half, :] = own_ref[t, 0:half, :]
        rows[2 * hot_half + t * slot_cap:2 * hot_half + (t + 1) * slot_cap, :] = own_ref[t, half:, :]
    pooled[...] = jnp.dot(inc_ref[...], rows[...], preferred_element_type=f32).astype(bf16)
    w_out = w_out_ref[...].astype(f32)
    for samples in blocks:
        acc = jnp.zeros((size, 128), f32)
        for start in range(0, hidden_units, step):
            cols = slice(start, start + step)
            pre_act = jnp.dot(pooled[samples, :], w_in_ref[:, cols], preferred_element_type=f32)
            own = lanes([w_out[k:k + 1, :] for k in range(start // 128, (start + step) // 128)])
            act = jnp.maximum(pre_act, 0.0).astype(bf16)
            hidden[samples, cols] = act
            term = act.astype(f32) * own
            for k in range(0, step, 128):
                acc += term[:, k:k + 128]
        total[samples, :] = acc
    lines = [slice(at, at + 128) for at in range(0, batch, 128)]
    logit = lanes([jnp.sum(total[line, :], axis=1, keepdims=True) for line in lines])
    delta = jax.nn.sigmoid(logit) - labels_ref[...].T
    for k, line in enumerate(lines):
        dlogit[line, :] = jnp.broadcast_to(delta[:, k:k + 1], (128, 128))
    for samples in blocks:
        scale = dlogit[samples, :]
        grad = jnp.zeros((size, width), f32)
        for start in range(0, hidden_units, wide):
            dhidden = lanes([
                jnp.where(
                    hidden[samples, k:k + 128].astype(f32) > 0, scale * w_out[k // 128:k // 128 + 1, :], 0.0
                ).astype(bf16)
                for k in range(start, start + wide, 128)
            ])
            grad += lax.dot_general(
                dhidden, w_in_ref[:, start:start + wide], (((1,), (1,)), ((), ())), preferred_element_type=f32
            )
        out_ref[samples, :] = grad.astype(bf16)


def mate_grads_body(inc_ref, dpooled_ref, out_ref):
    hot_half = out_ref.shape[0]
    out_ref[...] = jnp.dot(
        inc_ref[:, hot_half:2 * hot_half].T, dpooled_ref[...], preferred_element_type=f32
    ).astype(bf16)


def own_grads_body(inc_ref, dpooled_ref, hot_ref, cold_ref):
    hot_half = hot_ref.shape[0]
    dpooled = dpooled_ref[...]
    hot_ref[...] = jnp.dot(inc_ref[:, 0:hot_half].T, dpooled, preferred_element_type=f32)
    cold_ref[...] = jnp.dot(inc_ref[:, 2 * hot_half:].T, dpooled, preferred_element_type=f32).astype(bf16)


def pack_grads_body(hot_ref, got_ref, cold_ref, out_ref):
    owners, half, width = got_ref.shape
    hot = hot_ref[...] + got_ref[...].reshape(owners * half, width).astype(f32)
    slot_cap = out_ref.shape[1] - half
    for t in range(owners):
        out_ref[t, 0:half, :] = hot[t * half:(t + 1) * half].astype(bf16)
        out_ref[t, half:, :] = cold_ref[t * slot_cap:(t + 1) * slot_cap, :]


def collect_body(asked_ref, back_ref, out_ref):
    owners, slot_cap = asked_ref.shape
    half = back_ref.shape[1] - slot_cap
    out_ref[0:half, :] = jnp.sum(back_ref[:, 0:half, :].astype(f32), axis=0).astype(bf16)
    for t in range(owners):
        out_ref[half + t * slot_cap:half + (t + 1) * slot_cap, :] = back_ref[t, half:, :]
    asked = lanes([asked_ref[t:t + 1, :] for t in range(owners)])
    digit = lax.broadcasted_iota(i32, (TAIL, asked.shape[1]), 0)
    digits = jnp.where(digit == 0, asked >> 8, jnp.where(digit == 1, asked & 255, 0))
    out_ref[half + owners * slot_cap:, :] = digits.astype(f32).astype(bf16)


def hot_half(hot_ref, which):
    half = hot_ref.shape[1] // 2
    return jnp.where(which == 0, hot_ref[:, 0:half], hot_ref[:, half:])


def row_grads(which, hot_ref, part_refs, held, put, rows):
    size = part_refs[0].shape[0]
    half = hot_ref.shape[1] // 2
    me = lax.div(lax.axis_index("dp"), 2)
    count = len(part_refs)
    for s in range(count):
        held[pl.ds(pl.multiple_of((me ^ s) * size, 16), size), :] = part_refs[s][...]
    hot = jnp.concatenate([held[g * size:g * size + half, :] for g in range(count)], axis=0)
    ids = [lanes([hot_half(hot_ref, which)] * count)]
    parts = [hot]
    for g in range(count):
        digits = held[(g + 1) * size - TAIL:(g + 1) * size, :].astype(f32).astype(i32)
        ids.append(digits[0:1, :] * 256 + digits[1:2, :])
        parts.append(held[g * size + half:(g + 1) * size - TAIL, :])
    step = 128
    for start in range(0, rows, step):
        grad = 0.0
        for k in range(len(ids)):
            pick = one_hot(ids[k], (step, ids[k].shape[1]), 0, start)
            grad += jnp.dot(pick, parts[k], preferred_element_type=f32)
        put(slice(start, start + step), grad)


def own_grad_body(hot_ref, *refs):
    part_refs, (out_ref, held) = refs[:-2], refs[-2:]

    def put(at, grad):
        out_ref[at, :] = grad

    row_grads(core(), hot_ref, part_refs, held, put, out_ref.shape[0])


def update_body(hot_ref, sum_ref, table_ref, grad_ref, *refs):
    part_refs, (new_table_ref, new_sum_ref, held, squares, grads, staged, sums, sems) = refs[:-8], refs[-8:]
    rows, width = table_ref.shape
    step = 128

    def put(at, grad):
        grad = grad_ref[at, :] + grad
        grads[at, :] = grad
        square = grad * grad
        square = sum(square[:, k:k + 128] for k in range(0, width, 128)).T
        squares[at.start // step:at.stop // step, :] = jnp.sum(square, axis=0, keepdims=True)

    row_grads(1 - core(), hot_ref, part_refs, held, put, rows)
    new_sum = sum_ref[...] + squares[...] * (1.0 / width)
    sums[...] = new_sum
    scale = (learning_rate / jnp.sqrt(new_sum)).T
    for start in range(0, rows, step):
        at = slice(start, start + step)
        k = start // step
        staged[at, :] = table_ref[at, :] - grads[at, :] * scale[:, k:k + 1]
    copies = [
        pltpu.make_async_copy(staged, new_table_ref, sems.at[0]),
        pltpu.make_async_copy(sums, new_sum_ref, sems.at[1]),
    ]
    for copy in copies:
        copy.start()
    for copy in copies:
        copy.wait()


def dense_body(hot_ref, asked_ref, back_ref, out_ref):
    owners, slot_cap = asked_ref.shape
    half = back_ref.shape[1] - slot_cap
    rows = out_ref.shape[0]
    hot = jnp.sum(back_ref[:, 0:half, :].astype(f32), axis=0).astype(bf16)
    grad = jnp.dot(one_hot(hot_half(hot_ref, core()), (rows, half), 0), hot, preferred_element_type=f32)
    for t in range(owners):
        pick = one_hot(asked_ref[t:t + 1, :], (rows, slot_cap), 0)
        grad += jnp.dot(pick, back_ref[t, half:, :], preferred_element_type=f32)
    out_ref[...] = grad.astype(bf16)


def exchange(x):
    return lax.all_to_all(x, "table", split_axis=0, concat_axis=0, tiled=True)


def swap(x, bit):
    return lax.ppermute(x, "dp", [(g, g ^ bit) for g in range(lax.axis_size("dp"))])


def per_device(bag_slots, labels, cold_ids, cold_count, table, adagrad_sum, hot_ids, w_in, w_out):
    owners = lax.axis_size("table")
    groups = lax.axis_size("dp")
    hot_dev = hot_ids.shape[0]
    slot_cap = cold_ids.shape[2]
    batch = bag_slots.shape[0]
    rows, width = table.shape
    hidden_units = w_in.shape[1]
    half = hot_dev // 2
    vocab = owners * (hot_dev + slot_cap)
    shape = jax.ShapeDtypeStruct

    hot_row = hot_ids.reshape(1, hot_dev)
    asked = exchange(cold_ids[0])
    packed = call(
        functools.partial(count_body, hot_dev),
        shape((vocab // FIELDS, batch), i32),
        (cold_count, bag_slots.T),
        in_specs=[SMEM, VMEM],
    )
    asked, packed = lax.optimization_barrier((asked, packed))
    hot, table_bf = call(
        pick_hot_body,
        (shape((hot_dev, width), bf16), shape((rows, width), bf16)),
        (hot_row, table),
        [pltpu.VMEM((1, hot_dev), i32), pltpu.VMEM((rows, width), f32), pltpu.SemaphoreType.DMA((2,))],
        in_specs=[HBM, HBM],
    )
    served = call(
        serve_body,
        shape((owners, half + slot_cap, width), bf16),
        (asked, hot, table_bf),
        [pltpu.VMEM((owners * slot_cap, rows), bf16)],
    )
    own_rows = exchange(served)
    first_rows = call(first_rows_body, shape((owners, half, width), bf16), (own_rows,))
    first_rows, packed = lax.optimization_barrier((first_rows, packed))
    mate_rows = swap(first_rows, 1)
    inc = call(incidence_body, shape((batch, vocab), bf16), (packed,), [pltpu.VMEM((vocab, batch), bf16)])
    dpooled = call(
        top_body,
        shape((batch, width), bf16),
        (labels.reshape(-1, 128), inc, own_rows, mate_rows, w_in, w_out.reshape(-1, 128)),
        [
            pltpu.VMEM((batch, hidden_units), bf16),
            pltpu.VMEM((vocab, width), bf16),
            pltpu.VMEM((batch, width), bf16),
            pltpu.VMEM((batch, 128), f32),
            pltpu.VMEM((batch, 128), f32),
        ],
    )
    hot_half = owners * half
    to_mate = call(mate_grads_body, shape((hot_half, width), bf16), (inc, dpooled))
    got = swap(to_mate.reshape(owners, half, width), 1)
    hot_grads, cold_grads = call(
        own_grads_body,
        (shape((hot_half, width), f32), shape((owners * slot_cap, width), bf16)),
        (inc, dpooled),
    )
    summed = call(pack_grads_body, shape((owners, half + slot_cap, width), bf16), (hot_grads, got, cold_grads))
    returned = exchange(summed)
    size = half + owners * slot_cap + TAIL
    if groups & (groups - 1) == 0 and groups * size <= 2 * rows and owners * slot_cap == width:
        parts = {0: call(collect_body, shape((size, width), bf16), (asked, returned))}
        bit = groups // 2
        while bit > 1:
            parts.update({s ^ bit: swap(x, bit) for s, x in list(parts.items())})
            bit //= 2
        near = [parts[2 * y] for y in range(groups // 2)]
        far = [swap(x, 1) for x in near]
        held = pltpu.VMEM((groups // 2 * size, width), bf16)
        grad = call(own_grad_body, shape((rows, width), f32), (hot_row, *near), [held])
        new_table, new_sum = call(
            update_body,
            (shape((rows, width), f32), shape((rows // 128, 128), f32)),
            (hot_row, adagrad_sum.reshape(-1, 128), table, grad, *far),
            [
                held,
                pltpu.VMEM((rows // 128, 128), f32),
                pltpu.VMEM((rows, width), f32),
                pltpu.VMEM((rows, width), f32),
                pltpu.VMEM((rows // 128, 128), f32),
                pltpu.SemaphoreType.DMA((2,)),
            ],
            out_specs=(HBM, HBM),
        )
        return new_table, new_sum.reshape(rows)
    grad = call(dense_body, shape((rows, width), bf16), (hot_row, asked, returned))
    grad = lax.psum(grad, "dp").astype(f32)
    new_sum = adagrad_sum + jnp.mean(grad * grad, axis=1)
    return table - learning_rate * grad / jnp.sqrt(new_sum)[:, None], new_sum


def solution(mesh):
    placed = (
        P(("dp", "table"), None),
        P(("dp", "table")),
        P(("dp", "table"), None, None),
        P(("dp", "table"), None),
        P("table", None),
        P("table"),
        P("table"),
        P(),
        P(),
    )
    return jax.shard_map(
        per_device,
        mesh=mesh,
        in_specs=placed,
        out_specs=(P("table", None), P("table")),
        check_vma=False,
    )
```

```python
import functools
import math

import jax
import jax.numpy as jnp
from jax import lax
from jax.experimental import pallas as pl
from jax.experimental.pallas import tpu as pltpu
from jax.sharding import PartitionSpec as P

learning_rate = 0.3
f32, bf16, i32 = jnp.float32, jnp.bfloat16, jnp.int32
VMEM = pl.BlockSpec(memory_space=pltpu.VMEM)
HBM = pl.BlockSpec(memory_space=pltpu.HBM)
SMEM = pl.BlockSpec(memory_space=pltpu.SMEM)
FIELDS = 4
FIELD_BITS = 8
TAIL = 16


def call(body, outs, operands, scratch=(), in_specs=None, out_specs=None):
    held = jax.tree.leaves((outs, operands)) + [x for x in scratch if getattr(x, "memory_space", None) == pltpu.VMEM]
    limit = sum(math.prod(x.shape) * jnp.dtype(x.dtype).itemsize for x in held) + 4 * 1024 * 1024
    return pl.pallas_call(
        body,
        out_shape=outs,
        in_specs=in_specs or [VMEM] * len(operands),
        out_specs=out_specs or jax.tree.map(lambda _: VMEM, outs),
        scratch_shapes=list(scratch),
        compiler_params=pltpu.CompilerParams(vmem_limit_bytes=limit),
    )(*operands)


def lanes(pieces):
    return jnp.concatenate(pieces, axis=1)


def one_hot(ids, shape, axis, start=0):
    return (lax.broadcasted_iota(i32, shape, axis) + start == ids).astype(f32).astype(bf16)


def incidence_body(hot_dev, slot_cap, count_ref, slots_ref, out_ref, inc_t_ref):
    vocab, batch = inc_t_ref.shape
    owners = vocab // (hot_dev + slot_cap)
    half = hot_dev // 2
    hot_cols = owners * hot_dev
    me = core()
    field = vocab // FIELDS
    step = 128
    row = lax.broadcasted_iota(i32, (field, step), 0)
    for start in range(0, batch, step):
        slots = slots_ref[:, start:start + step]
        place = slots % hot_dev
        hot = jnp.where(place // half == me, 0, owners * half) + (slots // hot_dev) * half + place % half
        column = jnp.where(slots < hot_cols, hot, slots)
        key = jnp.where(slots < 0, -1, column % field)
        unit = jnp.left_shift(jnp.ones_like(slots), FIELD_BITS * (column // field))
        packed = jnp.zeros((field, step), i32)
        for entry in range(slots.shape[0]):
            packed += jnp.where(row == key[entry:entry + 1, :], unit[entry:entry + 1, :], 0)
        for k in range(FIELDS):
            part = jnp.right_shift(packed, FIELD_BITS * k) & (2**FIELD_BITS - 1)
            inc_t_ref[k * field:(k + 1) * field, start:start + step] = part.astype(f32).astype(bf16)
    place = lax.broadcasted_iota(i32, (slot_cap, batch), 0)
    for owner in range(owners):
        rows = pl.ds(hot_cols + owner * slot_cap, slot_cap)
        inc_t_ref[rows, :] = jnp.where(place < count_ref[0, owner], inc_t_ref[rows, :].astype(f32), 0.0).astype(bf16)
    out_ref[...] = inc_t_ref[...].T


def core():
    return lax.rem(lax.axis_index("dp"), 2)


def pick_hot_body(ids_ref, table_ref, hot_ref, table_bf_ref, ids, table, sems):
    copies = [pltpu.make_async_copy(ids_ref, ids, sems.at[0]), pltpu.make_async_copy(table_ref, table, sems.at[1])]
    for copy in copies:
        copy.start()
    for copy in copies:
        copy.wait()
    hot_dev = ids.shape[1]
    table_bf_ref[...] = table[...].astype(bf16)
    column = jnp.broadcast_to(ids[...], (8, hot_dev)).T[:, 0:1]
    pick = one_hot(column, (hot_dev, table.shape[0]), 1)
    hot_ref[...] = jnp.dot(pick, table_bf_ref[...], preferred_element_type=f32).astype(bf16)


def serve_body(asked_ref, hot_ref, table_ref, out_ref, pick, staged, sem):
    owners, slot_cap = asked_ref.shape
    hot_dev = hot_ref.shape[0]
    asked = asked_ref[...].T
    for t in range(owners):
        pick[t * slot_cap:(t + 1) * slot_cap, :] = one_hot(asked[:, t:t + 1], (slot_cap, table_ref.shape[0]), 1)
    picked = jnp.dot(pick[...], table_ref[...], preferred_element_type=f32).astype(bf16)
    half = hot_dev // 2
    hot = hot_ref[pl.ds(pl.multiple_of(core() * half, half), half), :]
    for t in range(owners):
        staged[t, 0:half, :] = hot
        staged[t, half:, :] = picked[t * slot_cap:(t + 1) * slot_cap]
    copy = pltpu.make_async_copy(staged, out_ref, sem)
    copy.start()
    copy.wait()


def first_rows_body(rows_ref, out_ref):
    out_ref[...] = rows_ref[:, 0:out_ref.shape[1], :]


def top_body(labels_ref, inc_ref, own_ref, mate_ref, w_in_ref, w_out_ref, out_ref, hidden, rows, pooled, total, dlogit):
    batch = inc_ref.shape[0]
    hidden_units, width = w_in_ref.shape[1], w_in_ref.shape[0]
    owners, half, _ = mate_ref.shape
    hot_half = owners * half
    slot_cap = own_ref.shape[1] - half
    size, step, wide = batch // 2, 512, 1024
    blocks = [slice(at, at + size) for at in range(0, batch, size)]
    rows[hot_half:2 * hot_half, :] = mate_ref[...].reshape(hot_half, width)
    for t in range(owners):
        rows[t * half:(t + 1) * half, :] = own_ref[t, 0:half, :]
        rows[2 * hot_half + t * slot_cap:2 * hot_half + (t + 1) * slot_cap, :] = own_ref[t, half:, :]
    pooled[...] = jnp.dot(inc_ref[...], rows[...], preferred_element_type=f32).astype(bf16)
    w_out = w_out_ref[...].astype(f32)
    for samples in blocks:
        acc = jnp.zeros((size, 128), f32)
        for start in range(0, hidden_units, step):
            cols = slice(start, start + step)
            pre_act = jnp.dot(pooled[samples, :], w_in_ref[:, cols], preferred_element_type=f32)
            own = lanes([w_out[k:k + 1, :] for k in range(start // 128, (start + step) // 128)])
            act = jnp.maximum(pre_act.astype(bf16), jnp.zeros((), bf16))
            hidden[samples, cols] = act
            term = act.astype(f32) * own
            for k in range(0, step, 128):
                acc += term[:, k:k + 128]
        total[samples, :] = acc
    lines = [slice(at, at + 128) for at in range(0, batch, 128)]
    logit = lanes([jnp.sum(total[line, :], axis=1, keepdims=True) for line in lines])
    delta = jax.nn.sigmoid(logit) - labels_ref[...].T
    for k, line in enumerate(lines):
        dlogit[line, :] = jnp.broadcast_to(delta[:, k:k + 1], (128, 128))
    for samples in blocks:
        scale = dlogit[samples, :]
        grad = jnp.zeros((size, width), f32)
        for start in range(0, hidden_units, wide):
            dhidden = lanes([
                jnp.where(
                    hidden[samples, k:k + 128].astype(f32) > 0, scale * w_out[k // 128:k // 128 + 1, :], 0.0
                ).astype(bf16)
                for k in range(start, start + wide, 128)
            ])
            grad += lax.dot_general(
                dhidden, w_in_ref[:, start:start + wide], (((1,), (1,)), ((), ())), preferred_element_type=f32
            )
        out_ref[samples, :] = grad.astype(bf16)


def mate_grads_body(inc_ref, dpooled_ref, out_ref):
    hot_half = out_ref.shape[0]
    out_ref[...] = jnp.dot(
        inc_ref[:, hot_half:2 * hot_half].T, dpooled_ref[...], preferred_element_type=f32
    ).astype(bf16)


def own_grads_body(inc_ref, dpooled_ref, hot_ref, cold_ref):
    hot_half = hot_ref.shape[0]
    dpooled = dpooled_ref[...]
    hot_ref[...] = jnp.dot(inc_ref[:, 0:hot_half].T, dpooled, preferred_element_type=f32)
    cold_ref[...] = jnp.dot(inc_ref[:, 2 * hot_half:].T, dpooled, preferred_element_type=f32).astype(bf16)


def pack_grads_body(hot_ref, got_ref, cold_ref, out_ref):
    owners, half, width = got_ref.shape
    hot = hot_ref[...] + got_ref[...].reshape(owners * half, width).astype(f32)
    slot_cap = out_ref.shape[1] - half
    for t in range(owners):
        out_ref[t, 0:half, :] = hot[t * half:(t + 1) * half].astype(bf16)
        out_ref[t, half:, :] = cold_ref[t * slot_cap:(t + 1) * slot_cap, :]


def collect_body(asked_ref, back_ref, out_ref):
    owners, slot_cap = asked_ref.shape
    half = back_ref.shape[1] - slot_cap
    out_ref[0:half, :] = jnp.sum(back_ref[:, 0:half, :].astype(f32), axis=0).astype(bf16)
    for t in range(owners):
        out_ref[half + t * slot_cap:half + (t + 1) * slot_cap, :] = back_ref[t, half:, :]
    asked = lanes([asked_ref[t:t + 1, :] for t in range(owners)])
    digit = lax.broadcasted_iota(i32, (TAIL, asked.shape[1]), 0)
    digits = jnp.where(digit == 0, asked >> 8, jnp.where(digit == 1, asked & 255, 0))
    out_ref[half + owners * slot_cap:, :] = digits.astype(f32).astype(bf16)


def hot_half(hot_ref, which):
    half = hot_ref.shape[1] // 2
    return jnp.where(which == 0, hot_ref[:, 0:half], hot_ref[:, half:])


def row_grads(which, hot_ref, part_refs, put, rows):
    half = hot_ref.shape[1] // 2
    hot_ids = hot_half(hot_ref, which)
    cold_ids = []
    for part_ref in part_refs:
        digits = part_ref[part_ref.shape[0] - TAIL:, :].astype(f32).astype(i32)
        cold_ids.append(digits[0:1, :] * 256 + digits[1:2, :])
    step = 128
    for start in range(0, rows, step):
        hot_pick = one_hot(hot_ids, (step, half), 0, start)
        grads = []
        for ids, part_ref in zip(cold_ids, part_refs):
            pick = one_hot(ids, (step, ids.shape[1]), 0, start)
            hot = jnp.dot(hot_pick, part_ref[0:half, :], preferred_element_type=f32)
            grads.append(hot + jnp.dot(pick, part_ref[half:part_ref.shape[0] - TAIL, :], preferred_element_type=f32))
        put(slice(start, start + step), grads)


def near_grads_body(hot_ref, *refs):
    near_refs, (far_ref, sum_ref, far_sum_ref) = refs[:-3], refs[-3:]

    def put_near(at, grads):
        sum_ref[at, :] = grads[0] + grads[1]

    def put_far(at, grads):
        far_sum_ref[at, :] = grads[0]

    row_grads(core(), hot_ref, near_refs, put_near, sum_ref.shape[0])
    row_grads(1 - core(), hot_ref, [far_ref], put_far, sum_ref.shape[0])


def update_body(hot_ref, sum_ref, table_ref, near_ref, far_ref, part_ref, *refs):
    new_table_ref, new_sum_ref, squares, grads, staged, sums, sems = refs
    rows, width = table_ref.shape
    step = 128

    def put(at, parts):
        grad = near_ref[at, :] + (far_ref[at, :] + parts[0])
        grads[at, :] = grad
        square = grad * grad
        square = sum(square[:, k:k + 128] for k in range(0, width, 128)).T
        squares[at.start // step:at.stop // step, :] = jnp.sum(square, axis=0, keepdims=True)

    row_grads(1 - core(), hot_ref, [part_ref], put, rows)
    new_sum = sum_ref[...] + squares[...] * (1.0 / width)
    sums[...] = new_sum
    scale = (learning_rate / jnp.sqrt(new_sum)).T
    for start in range(0, rows, step):
        at = slice(start, start + step)
        k = start // step
        staged[at, :] = table_ref[at, :] - grads[at, :] * scale[:, k:k + 1]
    copies = [
        pltpu.make_async_copy(staged, new_table_ref, sems.at[0]),
        pltpu.make_async_copy(sums, new_sum_ref, sems.at[1]),
    ]
    for copy in copies:
        copy.start()
    for copy in copies:
        copy.wait()


def dense_body(hot_ref, asked_ref, back_ref, out_ref):
    owners, slot_cap = asked_ref.shape
    half = back_ref.shape[1] - slot_cap
    rows = out_ref.shape[0]
    hot = jnp.sum(back_ref[:, 0:half, :].astype(f32), axis=0).astype(bf16)
    grad = jnp.dot(one_hot(hot_half(hot_ref, core()), (rows, half), 0), hot, preferred_element_type=f32)
    for t in range(owners):
        pick = one_hot(asked_ref[t:t + 1, :], (rows, slot_cap), 0)
        grad += jnp.dot(pick, back_ref[t, half:, :], preferred_element_type=f32)
    out_ref[...] = grad.astype(bf16)


def exchange(x):
    return lax.all_to_all(x, "table", split_axis=0, concat_axis=0, tiled=True)


def swap(x, bit):
    return lax.ppermute(x, "dp", [(g, g ^ bit) for g in range(lax.axis_size("dp"))])


def per_device(bag_slots, labels, cold_ids, cold_count, table, adagrad_sum, hot_ids, w_in, w_out):
    owners = lax.axis_size("table")
    groups = lax.axis_size("dp")
    hot_dev = hot_ids.shape[0]
    slot_cap = cold_ids.shape[2]
    batch = bag_slots.shape[0]
    rows, width = table.shape
    hidden_units = w_in.shape[1]
    half = hot_dev // 2
    vocab = owners * (hot_dev + slot_cap)
    shape = jax.ShapeDtypeStruct

    hot_row = hot_ids.reshape(1, hot_dev)
    asked = exchange(cold_ids[0])
    inc = call(
        functools.partial(incidence_body, hot_dev, slot_cap),
        shape((batch, vocab), bf16),
        (cold_count, bag_slots.T),
        [pltpu.VMEM((vocab, batch), bf16)],
        in_specs=[SMEM, VMEM],
    )
    hot, table_bf = call(
        pick_hot_body,
        (shape((hot_dev, width), bf16), shape((rows, width), bf16)),
        (hot_row, table),
        [pltpu.VMEM((1, hot_dev), i32), pltpu.VMEM((rows, width), f32), pltpu.SemaphoreType.DMA((2,))],
        in_specs=[HBM, HBM],
    )
    served = call(
        serve_body,
        shape((owners, half + slot_cap, width), bf16),
        (asked, hot, table_bf),
        [
            pltpu.VMEM((owners * slot_cap, rows), bf16),
            pltpu.VMEM((owners, half + slot_cap, width), bf16),
            pltpu.SemaphoreType.DMA,
        ],
        out_specs=HBM,
    )
    own_rows, inc = lax.optimization_barrier((exchange(served), inc))
    mate_rows = swap(call(first_rows_body, shape((owners, half, width), bf16), (own_rows,)), 1)
    dpooled = call(
        top_body,
        shape((batch, width), bf16),
        (labels.reshape(-1, 128), inc, own_rows, mate_rows, w_in, w_out.reshape(-1, 128)),
        [
            pltpu.VMEM((batch, hidden_units), bf16),
            pltpu.VMEM((vocab, width), bf16),
            pltpu.VMEM((batch, width), bf16),
            pltpu.VMEM((batch, 128), f32),
            pltpu.VMEM((batch, 128), f32),
        ],
    )
    hot_half = owners * half
    to_mate = call(mate_grads_body, shape((hot_half, width), bf16), (inc, dpooled))
    got = swap(to_mate.reshape(owners, half, width), 1)
    hot_grads, cold_grads = call(
        own_grads_body,
        (shape((hot_half, width), f32), shape((owners * slot_cap, width), bf16)),
        (inc, dpooled),
    )
    summed = call(pack_grads_body, shape((owners, half + slot_cap, width), bf16), (hot_grads, got, cold_grads))
    returned = exchange(summed)
    size = half + owners * slot_cap + TAIL
    if groups == 4 and 2 * size <= rows and owners * slot_cap == width:
        own = call(collect_body, shape((size, width), bf16), (asked, returned))
        beside = swap(own, 2)
        far_own, far_beside = swap(own, 1), swap(beside, 1)
        dense = shape((rows, width), f32)
        near, far = call(near_grads_body, (dense, dense), (hot_row, own, beside, far_own))
        new_table, new_sum = call(
            update_body,
            (dense, shape((rows // 128, 128), f32)),
            (hot_row, adagrad_sum.reshape(-1, 128), table, near, far, far_beside),
            [
                pltpu.VMEM((rows // 128, 128), f32),
                pltpu.VMEM((rows, width), f32),
                pltpu.VMEM((rows, width), f32),
                pltpu.VMEM((rows // 128, 128), f32),
                pltpu.SemaphoreType.DMA((2,)),
            ],
            out_specs=(HBM, HBM),
        )
        return new_table, new_sum.reshape(rows)
    grad = call(dense_body, shape((rows, width), bf16), (hot_row, asked, returned))
    grad = lax.psum(grad, "dp").astype(f32)
    new_sum = adagrad_sum + jnp.mean(grad * grad, axis=1)
    return table - learning_rate * grad / jnp.sqrt(new_sum)[:, None], new_sum


def solution(mesh):
    placed = (
        P(("dp", "table"), None),
        P(("dp", "table")),
        P(("dp", "table"), None, None),
        P(("dp", "table"), None),
        P("table", None),
        P("table"),
        P("table"),
        P(),
        P(),
    )
    return jax.shard_map(
        per_device,
        mesh=mesh,
        in_specs=placed,
        out_specs=(P("table", None), P("table")),
        check_vma=False,
    )
```

```python
import functools
import math

import jax
import jax.numpy as jnp
from jax import lax
from jax.experimental import pallas as pl
from jax.experimental.pallas import tpu as pltpu
from jax.sharding import PartitionSpec as P

learning_rate = 0.3
f32, bf16, i32 = jnp.float32, jnp.bfloat16, jnp.int32
VMEM = pl.BlockSpec(memory_space=pltpu.VMEM)
HBM = pl.BlockSpec(memory_space=pltpu.HBM)
FIELDS = 4
FIELD_BITS = 8
TAIL = 16
FIRST = 2


def call(body, outs, operands, scratch=(), in_specs=None, out_specs=None):
    held = jax.tree.leaves((outs, operands)) + [x for x in scratch if getattr(x, "memory_space", None) == pltpu.VMEM]
    limit = sum(math.prod(x.shape) * jnp.dtype(x.dtype).itemsize for x in held) + 4 * 1024 * 1024
    return pl.pallas_call(
        body,
        out_shape=outs,
        in_specs=in_specs or [VMEM] * len(operands),
        out_specs=out_specs or jax.tree.map(lambda _: VMEM, outs),
        scratch_shapes=list(scratch),
        compiler_params=pltpu.CompilerParams(vmem_limit_bytes=limit),
    )(*operands)


def lanes(pieces):
    return jnp.concatenate(pieces, axis=1)


def one_hot(ids, shape, axis, start=0):
    return (lax.broadcasted_iota(i32, shape, axis) + start == ids).astype(f32).astype(bf16)


def entries(hot_dev, counts, slots, field):
    owners = counts.shape[1]
    slot_cap = FIELDS * field // owners - hot_dev
    half = hot_dev // 2
    hot_cols = owners * hot_dev
    place = slots % hot_dev
    hot = jnp.where(place // half == core(), 0, owners * half) + (slots // hot_dev) * half + place % half
    column = jnp.where(slots < hot_cols, hot, slots)
    cold = slots - hot_cols
    live = slots >= 0
    for t in range(owners):
        at = cold - t * slot_cap
        live = live & ((at < counts[:, t:t + 1]) | (at >= slot_cap))
    key = jnp.where(live, column % field, -1)
    return key, jnp.left_shift(jnp.ones_like(slots), FIELD_BITS * (column // field))


def count(key, unit, field):
    row = lax.broadcasted_iota(i32, (field, key.shape[1]), 0)
    packed = jnp.zeros(row.shape, i32)
    for entry in range(key.shape[0]):
        packed += jnp.where(row == key[entry:entry + 1, :], unit[entry:entry + 1, :], 0)
    return packed


def prepare_body(count_ref, slots_ref, ids_ref, table_ref, packed_ref, key_ref, unit_ref, hot_ref, table_bf_ref, *scratch):
    counts, slots, ids, table, sems = scratch
    pairs = [(count_ref, counts), (slots_ref, slots), (ids_ref, ids), (table_ref, table)]
    copies = [pltpu.make_async_copy(src, dst, sems.at[k]) for k, (src, dst) in enumerate(pairs)]
    for copy in copies:
        copy.start()
    hot_dev = ids.shape[1]
    field, first = packed_ref.shape
    copies[0].wait()
    copies[1].wait()
    for start in range(0, slots.shape[1], 128):
        at = slice(start, start + 128)
        key, unit = entries(hot_dev, counts[...], slots[:, at], field)
        if start < first:
            packed_ref[:, at] = count(key, unit, field)
        else:
            rest = slice(start - first, start - first + 128)
            key_ref[:, rest], unit_ref[:, rest] = key, unit
    copies[2].wait()
    copies[3].wait()
    table_bf_ref[...] = table[...].astype(bf16)
    column = jnp.broadcast_to(ids[...], (8, hot_dev)).T[:, 0:1]
    pick = one_hot(column, (hot_dev, table.shape[0]), 1)
    hot_ref[...] = jnp.dot(pick, table_bf_ref[...], preferred_element_type=f32).astype(bf16)


def incidence_body(packed_ref, key_ref, unit_ref, out_ref, inc_t_ref):
    field, first = packed_ref.shape
    for start in range(0, out_ref.shape[0], 128):
        at = slice(start, start + 128)
        if start < first:
            packed = packed_ref[:, at]
        else:
            rest = slice(start - first, start - first + 128)
            packed = count(key_ref[:, rest], unit_ref[:, rest], field)
        for k in range(FIELDS):
            part = jnp.right_shift(packed, FIELD_BITS * k) & (2**FIELD_BITS - 1)
            inc_t_ref[k * field:(k + 1) * field, at] = part.astype(f32).astype(bf16)
    out_ref[...] = inc_t_ref[...].T


def core():
    return lax.rem(lax.axis_index("dp"), 2)


def serve_body(asked_ref, hot_ref, table_ref, out_ref, pick):
    owners, slot_cap = asked_ref.shape
    half = hot_ref.shape[0] // 2
    asked = asked_ref[...].T
    for t in range(owners):
        pick[t * slot_cap:(t + 1) * slot_cap, :] = one_hot(asked[:, t:t + 1], (slot_cap, table_ref.shape[0]), 1)
    picked = jnp.dot(pick[...], table_ref[...], preferred_element_type=f32).astype(bf16)
    hot = hot_ref[pl.ds(pl.multiple_of(core() * half, half), half), :]
    for t in range(owners):
        out_ref[t, 0:half, :] = hot
        out_ref[t, half:, :] = picked[t * slot_cap:(t + 1) * slot_cap]


def first_rows_body(rows_ref, out_ref):
    out_ref[...] = rows_ref[:, 0:out_ref.shape[1], :]


def top_body(labels_ref, inc_ref, own_ref, mate_ref, w_in_ref, w_out_ref, out_ref, hidden, rows, pooled, total, dlogit):
    batch = inc_ref.shape[0]
    hidden_units, width = w_in_ref.shape[1], w_in_ref.shape[0]
    owners, half, _ = mate_ref.shape
    hot_half = owners * half
    slot_cap = own_ref.shape[1] - half
    size, step, wide = batch // 2, 512, 1024
    blocks = [slice(at, at + size) for at in range(0, batch, size)]
    rows[hot_half:2 * hot_half, :] = mate_ref[...].reshape(hot_half, width)
    for t in range(owners):
        rows[t * half:(t + 1) * half, :] = own_ref[t, 0:half, :]
        rows[2 * hot_half + t * slot_cap:2 * hot_half + (t + 1) * slot_cap, :] = own_ref[t, half:, :]
    pooled[...] = jnp.dot(inc_ref[...], rows[...], preferred_element_type=f32).astype(bf16)
    w_out = w_out_ref[...].astype(f32)
    for samples in blocks:
        acc = jnp.zeros((size, 128), f32)
        for start in range(0, hidden_units, step):
            cols = slice(start, start + step)
            pre_act = jnp.dot(pooled[samples, :], w_in_ref[:, cols], preferred_element_type=f32)
            own = lanes([w_out[k:k + 1, :] for k in range(start // 128, (start + step) // 128)])
            act = jnp.maximum(pre_act.astype(bf16), jnp.zeros((), bf16))
            hidden[samples, cols] = act
            term = act.astype(f32) * own
            for k in range(0, step, 128):
                acc += term[:, k:k + 128]
        total[samples, :] = acc
    lines = [slice(at, at + 128) for at in range(0, batch, 128)]
    logit = lanes([jnp.sum(total[line, :], axis=1, keepdims=True) for line in lines])
    delta = jax.nn.sigmoid(logit) - labels_ref[...].T
    for k, line in enumerate(lines):
        dlogit[line, :] = jnp.broadcast_to(delta[:, k:k + 1], (128, 128))
    for samples in blocks:
        scale = dlogit[samples, :]
        grad = jnp.zeros((size, width), f32)
        for start in range(0, hidden_units, wide):
            dhidden = lanes([
                jnp.where(
                    hidden[samples, k:k + 128].astype(f32) > 0, scale * w_out[k // 128:k // 128 + 1, :], 0.0
                ).astype(bf16)
                for k in range(start, start + wide, 128)
            ])
            grad += lax.dot_general(
                dhidden, w_in_ref[:, start:start + wide], (((1,), (1,)), ((), ())), preferred_element_type=f32
            )
        out_ref[samples, :] = grad.astype(bf16)


def mate_grads_body(inc_ref, dpooled_ref, out_ref):
    hot_half = out_ref.shape[0]
    out_ref[...] = jnp.dot(
        inc_ref[:, hot_half:2 * hot_half].T, dpooled_ref[...], preferred_element_type=f32
    ).astype(bf16)


def own_grads_body(inc_ref, dpooled_ref, hot_ref, cold_ref):
    hot_half = hot_ref.shape[0]
    dpooled = dpooled_ref[...]
    hot_ref[...] = jnp.dot(inc_ref[:, 0:hot_half].T, dpooled, preferred_element_type=f32)
    cold_ref[...] = jnp.dot(inc_ref[:, 2 * hot_half:].T, dpooled, preferred_element_type=f32).astype(bf16)


def pack_grads_body(hot_ref, got_ref, cold_ref, out_ref):
    owners, half, width = got_ref.shape
    hot = hot_ref[...] + got_ref[...].reshape(owners * half, width).astype(f32)
    slot_cap = out_ref.shape[1] - half
    for t in range(owners):
        out_ref[t, 0:half, :] = hot[t * half:(t + 1) * half].astype(bf16)
        out_ref[t, half:, :] = cold_ref[t * slot_cap:(t + 1) * slot_cap, :]


def collect_body(asked_ref, back_ref, out_ref):
    owners, slot_cap = asked_ref.shape
    half = back_ref.shape[1] - slot_cap
    out_ref[0:half, :] = jnp.sum(back_ref[:, 0:half, :].astype(f32), axis=0).astype(bf16)
    for t in range(owners):
        out_ref[half + t * slot_cap:half + (t + 1) * slot_cap, :] = back_ref[t, half:, :]
    asked = lanes([asked_ref[t:t + 1, :] for t in range(owners)])
    digit = lax.broadcasted_iota(i32, (TAIL, asked.shape[1]), 0)
    digits = jnp.where(digit == 0, asked >> 8, jnp.where(digit == 1, asked & 255, 0))
    out_ref[half + owners * slot_cap:, :] = digits.astype(f32).astype(bf16)


def hot_half(hot_ref, which):
    half = hot_ref.shape[1] // 2
    return jnp.where(which == 0, hot_ref[:, 0:half], hot_ref[:, half:])


def row_grads(which, hot_ref, part_refs, put, rows):
    half = hot_ref.shape[1] // 2
    hot_ids = hot_half(hot_ref, which)
    cold_ids = []
    for part_ref in part_refs:
        digits = part_ref[part_ref.shape[0] - TAIL:, :].astype(f32).astype(i32)
        cold_ids.append(digits[0:1, :] * 256 + digits[1:2, :])
    step = 128
    for start in range(0, rows, step):
        hot_pick = one_hot(hot_ids, (step, half), 0, start)
        grads = []
        for ids, part_ref in zip(cold_ids, part_refs):
            pick = one_hot(ids, (step, ids.shape[1]), 0, start)
            hot = jnp.dot(hot_pick, part_ref[0:half, :], preferred_element_type=f32)
            grads.append(hot + jnp.dot(pick, part_ref[half:part_ref.shape[0] - TAIL, :], preferred_element_type=f32))
        put(slice(start, start + step), grads)


def near_grads_body(hot_ref, *refs):
    near_refs, (far_ref, sum_ref, far_sum_ref) = refs[:-3], refs[-3:]

    def put_near(at, grads):
        sum_ref[at, :] = grads[0] + grads[1]

    def put_far(at, grads):
        far_sum_ref[at, :] = grads[0]

    row_grads(core(), hot_ref, near_refs, put_near, sum_ref.shape[0])
    row_grads(1 - core(), hot_ref, [far_ref], put_far, sum_ref.shape[0])


def update_body(hot_ref, sum_ref, table_ref, near_ref, far_ref, part_ref, *refs):
    new_table_ref, new_sum_ref, squares, grads, staged, sums, sems = refs
    rows, width = table_ref.shape
    step = 128

    def put(at, parts):
        grad = near_ref[at, :] + (far_ref[at, :] + parts[0])
        grads[at, :] = grad
        square = grad * grad
        square = sum(square[:, k:k + 128] for k in range(0, width, 128)).T
        squares[at.start // step:at.stop // step, :] = jnp.sum(square, axis=0, keepdims=True)

    row_grads(1 - core(), hot_ref, [part_ref], put, rows)
    new_sum = sum_ref[...] + squares[...] * (1.0 / width)
    sums[...] = new_sum
    scale = (learning_rate / jnp.sqrt(new_sum)).T
    for start in range(0, rows, step):
        at = slice(start, start + step)
        k = start // step
        staged[at, :] = table_ref[at, :] - grads[at, :] * scale[:, k:k + 1]
    copies = [
        pltpu.make_async_copy(staged, new_table_ref, sems.at[0]),
        pltpu.make_async_copy(sums, new_sum_ref, sems.at[1]),
    ]
    for copy in copies:
        copy.start()
    for copy in copies:
        copy.wait()


def dense_body(hot_ref, asked_ref, back_ref, out_ref):
    owners, slot_cap = asked_ref.shape
    half = back_ref.shape[1] - slot_cap
    rows = out_ref.shape[0]
    hot = jnp.sum(back_ref[:, 0:half, :].astype(f32), axis=0).astype(bf16)
    grad = jnp.dot(one_hot(hot_half(hot_ref, core()), (rows, half), 0), hot, preferred_element_type=f32)
    for t in range(owners):
        pick = one_hot(asked_ref[t:t + 1, :], (rows, slot_cap), 0)
        grad += jnp.dot(pick, back_ref[t, half:, :], preferred_element_type=f32)
    out_ref[...] = grad.astype(bf16)


def exchange(x):
    return lax.all_to_all(x, "table", split_axis=0, concat_axis=0, tiled=True)


def swap(x, bit):
    return lax.ppermute(x, "dp", [(g, g ^ bit) for g in range(lax.axis_size("dp"))])


def per_device(bag_slots, labels, cold_ids, cold_count, table, adagrad_sum, hot_ids, w_in, w_out):
    owners = lax.axis_size("table")
    groups = lax.axis_size("dp")
    hot_dev = hot_ids.shape[0]
    slot_cap = cold_ids.shape[2]
    batch = bag_slots.shape[0]
    rows, width = table.shape
    hidden_units = w_in.shape[1]
    half = hot_dev // 2
    vocab = owners * (hot_dev + slot_cap)
    shape = jax.ShapeDtypeStruct

    hot_row = hot_ids.reshape(1, hot_dev)
    asked = exchange(cold_ids[0])
    slots = bag_slots.T
    first = FIRST * batch // 4
    rest = shape((slots.shape[0], batch - first), i32)
    packed, key, unit, hot, table_bf = call(
        prepare_body,
        (
            shape((vocab // FIELDS, first), i32),
            rest,
            rest,
            shape((hot_dev, width), bf16),
            shape((rows, width), bf16),
        ),
        tuple(pltpu.with_memory_space_constraint(x, pltpu.HBM) for x in (cold_count, slots, hot_row, table)),
        [
            pltpu.VMEM(cold_count.shape, i32),
            pltpu.VMEM(slots.shape, i32),
            pltpu.VMEM(hot_row.shape, i32),
            pltpu.VMEM(table.shape, f32),
            pltpu.SemaphoreType.DMA((4,)),
        ],
        in_specs=[HBM] * 4,
    )
    asked, packed = lax.optimization_barrier((asked, packed))
    served = call(
        serve_body,
        shape((owners, half + slot_cap, width), bf16),
        (asked, hot, table_bf),
        [pltpu.VMEM((owners * slot_cap, rows), bf16)],
    )
    own_rows = exchange(served)
    first_rows = call(first_rows_body, shape((owners, half, width), bf16), (own_rows,))
    first_rows, packed = lax.optimization_barrier((first_rows, packed))
    mate_rows = swap(first_rows, 1)
    inc = call(incidence_body, shape((batch, vocab), bf16), (packed, key, unit), [pltpu.VMEM((vocab, batch), bf16)])
    dpooled = call(
        top_body,
        shape((batch, width), bf16),
        (labels.reshape(-1, 128), inc, own_rows, mate_rows, w_in, w_out.reshape(-1, 128)),
        [
            pltpu.VMEM((batch, hidden_units), bf16),
            pltpu.VMEM((vocab, width), bf16),
            pltpu.VMEM((batch, width), bf16),
            pltpu.VMEM((batch, 128), f32),
            pltpu.VMEM((batch, 128), f32),
        ],
    )
    hot_half = owners * half
    to_mate = call(mate_grads_body, shape((hot_half, width), bf16), (inc, dpooled))
    got = swap(to_mate.reshape(owners, half, width), 1)
    hot_grads, cold_grads = call(
        own_grads_body,
        (shape((hot_half, width), f32), shape((owners * slot_cap, width), bf16)),
        (inc, dpooled),
    )
    summed = call(pack_grads_body, shape((owners, half + slot_cap, width), bf16), (hot_grads, got, cold_grads))
    returned = exchange(summed)
    size = half + owners * slot_cap + TAIL
    if groups == 4 and 2 * size <= rows and owners * slot_cap == width:
        own = call(collect_body, shape((size, width), bf16), (asked, returned))
        beside = swap(own, 2)
        far_own, far_beside = swap(own, 1), swap(beside, 1)
        dense = shape((rows, width), f32)
        near, far = call(near_grads_body, (dense, dense), (hot_row, own, beside, far_own))
        new_table, new_sum = call(
            update_body,
            (dense, shape((rows // 128, 128), f32)),
            (hot_row, adagrad_sum.reshape(-1, 128), table, near, far, far_beside),
            [
                pltpu.VMEM((rows // 128, 128), f32),
                pltpu.VMEM((rows, width), f32),
                pltpu.VMEM((rows, width), f32),
                pltpu.VMEM((rows // 128, 128), f32),
                pltpu.SemaphoreType.DMA((2,)),
            ],
            out_specs=(HBM, HBM),
        )
        return new_table, new_sum.reshape(rows)
    grad = call(dense_body, shape((rows, width), bf16), (hot_row, asked, returned))
    grad = lax.psum(grad, "dp").astype(f32)
    new_sum = adagrad_sum + jnp.mean(grad * grad, axis=1)
    return table - learning_rate * grad / jnp.sqrt(new_sum)[:, None], new_sum


def solution(mesh):
    placed = (
        P(("dp", "table"), None),
        P(("dp", "table")),
        P(("dp", "table"), None, None),
        P(("dp", "table"), None),
        P("table", None),
        P("table"),
        P("table"),
        P(),
        P(),
    )
    return jax.shard_map(
        per_device,
        mesh=mesh,
        in_specs=placed,
        out_specs=(P("table", None), P("table")),
        check_vma=False,
    )
```

```python
import functools
import math

import jax
import jax.numpy as jnp
from jax import lax
from jax.experimental import pallas as pl
from jax.experimental.pallas import tpu as pltpu
from jax.sharding import PartitionSpec as P

learning_rate = 0.3
f32, bf16, i32 = jnp.float32, jnp.bfloat16, jnp.int32
VMEM = pl.BlockSpec(memory_space=pltpu.VMEM)
HBM = pl.BlockSpec(memory_space=pltpu.HBM)
FIELDS = 4
FIELD_BITS = 8
TAIL = 16
FIRST = 2


def call(body, outs, operands, scratch=(), in_specs=None, out_specs=None):
    held = jax.tree.leaves((outs, operands)) + [x for x in scratch if getattr(x, "memory_space", None) == pltpu.VMEM]
    limit = sum(math.prod(x.shape) * jnp.dtype(x.dtype).itemsize for x in held) + 4 * 1024 * 1024
    return pl.pallas_call(
        body,
        out_shape=outs,
        in_specs=in_specs or [VMEM] * len(operands),
        out_specs=out_specs or jax.tree.map(lambda _: VMEM, outs),
        scratch_shapes=list(scratch),
        compiler_params=pltpu.CompilerParams(vmem_limit_bytes=limit),
    )(*operands)


def lanes(pieces):
    return jnp.concatenate(pieces, axis=1)


def one_hot(ids, shape, axis, start=0):
    return (lax.broadcasted_iota(i32, shape, axis) + start == ids).astype(f32).astype(bf16)


def entries(hot_dev, counts, slots, field):
    owners = counts.shape[1]
    slot_cap = FIELDS * field // owners - hot_dev
    half = hot_dev // 2
    hot_cols = owners * hot_dev
    place = slots % hot_dev
    hot = jnp.where(place // half == core(), 0, owners * half) + (slots // hot_dev) * half + place % half
    column = jnp.where(slots < hot_cols, hot, slots)
    cold = slots - hot_cols
    live = slots >= 0
    for t in range(owners):
        at = cold - t * slot_cap
        live = live & ((at < counts[:, t:t + 1]) | (at >= slot_cap))
    key = jnp.where(live, column % field, -1)
    return key, jnp.left_shift(jnp.ones_like(slots), FIELD_BITS * (column // field))


def count(key, unit, field):
    row = lax.broadcasted_iota(i32, (field, key.shape[1]), 0)
    packed = jnp.zeros(row.shape, i32)
    for entry in range(key.shape[0]):
        packed += jnp.where(row == key[entry:entry + 1, :], unit[entry:entry + 1, :], 0)
    return packed


def turn_body(ids_ref, out_ref, sems):
    half = ids_ref.shape[0] // 2
    copies = [
        pltpu.make_async_copy(ids_ref.at[k * half:(k + 1) * half], out_ref.at[(1 - k) * half:(2 - k) * half], sems.at[k])
        for k in range(2)
    ]
    for copy in copies:
        copy.start()
    for copy in copies:
        copy.wait()


def prepare_body(count_ref, slots_ref, ids_ref, table_ref, packed_ref, key_ref, unit_ref, hot_ref, table_bf_ref, *scratch):
    counts, slots, ids, table, sems = scratch
    pairs = [(count_ref, counts), (slots_ref, slots), (ids_ref, ids), (table_ref, table)]
    copies = [pltpu.make_async_copy(src, dst, sems.at[k]) for k, (src, dst) in enumerate(pairs)]
    for copy in copies:
        copy.start()
    hot_dev = ids.shape[1]
    field, first = packed_ref.shape
    copies[0].wait()
    copies[1].wait()
    for start in range(0, slots.shape[1], 128):
        at = slice(start, start + 128)
        key, unit = entries(hot_dev, counts[...], slots[:, at], field)
        if start < first:
            packed_ref[:, at] = count(key, unit, field)
        else:
            rest = slice(start - first, start - first + 128)
            key_ref[:, rest], unit_ref[:, rest] = key, unit
    copies[2].wait()
    copies[3].wait()
    table_bf_ref[...] = table[...].astype(bf16)
    column = jnp.broadcast_to(ids[...], (8, hot_dev)).T[:, 0:1]
    pick = one_hot(column, (hot_dev, table.shape[0]), 1)
    hot_ref[...] = jnp.dot(pick, table_bf_ref[...], preferred_element_type=f32).astype(bf16)


def incidence_body(packed_ref, key_ref, unit_ref, out_ref, inc_t_ref):
    field, first = packed_ref.shape
    for start in range(0, out_ref.shape[0], 128):
        at = slice(start, start + 128)
        if start < first:
            packed = packed_ref[:, at]
        else:
            rest = slice(start - first, start - first + 128)
            packed = count(key_ref[:, rest], unit_ref[:, rest], field)
        for k in range(FIELDS):
            part = jnp.right_shift(packed, FIELD_BITS * k) & (2**FIELD_BITS - 1)
            inc_t_ref[k * field:(k + 1) * field, at] = part.astype(f32).astype(bf16)
    out_ref[...] = inc_t_ref[...].T


def core():
    return lax.rem(lax.axis_index("dp"), 2)


def serve_body(order, asked_ref, hot_ref, table_ref, out_ref, pick):
    owners, slot_cap = asked_ref.shape
    half = hot_ref.shape[0] // 2
    asked = asked_ref[...].T
    for k, t in enumerate(order):
        pick[t * slot_cap:(t + 1) * slot_cap, :] = one_hot(asked[:, k:k + 1], (slot_cap, table_ref.shape[0]), 1)
    picked = jnp.dot(pick[...], table_ref[...], preferred_element_type=f32).astype(bf16)
    hot = hot_ref[pl.ds(pl.multiple_of(core() * half, half), half), :]
    for k, t in enumerate(order):
        out_ref[k, 0:half, :] = hot
        out_ref[k, half:, :] = picked[t * slot_cap:(t + 1) * slot_cap]


def first_rows_body(rows_ref, out_ref):
    out_ref[...] = rows_ref[:, 0:out_ref.shape[1], :]


def top_body(order, labels_ref, inc_ref, own_ref, mate_ref, w_in_ref, w_out_ref, out_ref, hidden, rows, pooled, total, dlogit):
    batch = inc_ref.shape[0]
    hidden_units, width = w_in_ref.shape[1], w_in_ref.shape[0]
    owners, half, _ = mate_ref.shape
    hot_half = owners * half
    slot_cap = own_ref.shape[1] - half
    size, step, wide = batch // 2, 512, 1024
    blocks = [slice(at, at + size) for at in range(0, batch, size)]
    for k, t in enumerate(order):
        rows[t * half:(t + 1) * half, :] = own_ref[k, 0:half, :]
        rows[hot_half + t * half:hot_half + (t + 1) * half, :] = mate_ref[k]
        rows[2 * hot_half + t * slot_cap:2 * hot_half + (t + 1) * slot_cap, :] = own_ref[k, half:, :]
    pooled[...] = jnp.dot(inc_ref[...], rows[...], preferred_element_type=f32).astype(bf16)
    w_out = w_out_ref[...].astype(f32)
    for samples in blocks:
        acc = jnp.zeros((size, 128), f32)
        for start in range(0, hidden_units, step):
            cols = slice(start, start + step)
            pre_act = jnp.dot(pooled[samples, :], w_in_ref[:, cols], preferred_element_type=f32)
            own = lanes([w_out[k:k + 1, :] for k in range(start // 128, (start + step) // 128)])
            act = jnp.maximum(pre_act.astype(bf16), jnp.zeros((), bf16))
            hidden[samples, cols] = act
            term = act.astype(f32) * own
            for k in range(0, step, 128):
                acc += term[:, k:k + 128]
        total[samples, :] = acc
    lines = [slice(at, at + 128) for at in range(0, batch, 128)]
    logit = lanes([jnp.sum(total[line, :], axis=1, keepdims=True) for line in lines])
    delta = jax.nn.sigmoid(logit) - labels_ref[...].T
    for k, line in enumerate(lines):
        dlogit[line, :] = jnp.broadcast_to(delta[:, k:k + 1], (128, 128))
    for samples in blocks:
        scale = dlogit[samples, :]
        grad = jnp.zeros((size, width), f32)
        for start in range(0, hidden_units, wide):
            dhidden = lanes([
                jnp.where(
                    hidden[samples, k:k + 128].astype(f32) > 0, scale * w_out[k // 128:k // 128 + 1, :], 0.0
                ).astype(bf16)
                for k in range(start, start + wide, 128)
            ])
            grad += lax.dot_general(
                dhidden, w_in_ref[:, start:start + wide], (((1,), (1,)), ((), ())), preferred_element_type=f32
            )
        out_ref[samples, :] = grad.astype(bf16)


def mate_grads_body(inc_ref, dpooled_ref, out_ref):
    hot_half = out_ref.shape[0]
    out_ref[...] = jnp.dot(
        inc_ref[:, hot_half:2 * hot_half].T, dpooled_ref[...], preferred_element_type=f32
    ).astype(bf16)


def own_grads_body(inc_ref, dpooled_ref, hot_ref, cold_ref):
    hot_half = hot_ref.shape[0]
    dpooled = dpooled_ref[...]
    hot_ref[...] = jnp.dot(inc_ref[:, 0:hot_half].T, dpooled, preferred_element_type=f32)
    cold_ref[...] = jnp.dot(inc_ref[:, 2 * hot_half:].T, dpooled, preferred_element_type=f32).astype(bf16)


def pack_grads_body(order, hot_ref, got_ref, cold_ref, out_ref):
    owners, half, width = got_ref.shape
    hot = hot_ref[...] + got_ref[...].reshape(owners * half, width).astype(f32)
    slot_cap = out_ref.shape[1] - half
    for k, t in enumerate(order):
        out_ref[k, 0:half, :] = hot[t * half:(t + 1) * half].astype(bf16)
        out_ref[k, half:, :] = cold_ref[t * slot_cap:(t + 1) * slot_cap, :]


def collect_body(order, asked_ref, back_ref, out_ref):
    owners, slot_cap = asked_ref.shape
    half = back_ref.shape[1] - slot_cap
    out_ref[0:half, :] = jnp.sum(back_ref[:, 0:half, :].astype(f32), axis=0).astype(bf16)
    for k, t in enumerate(order):
        out_ref[half + t * slot_cap:half + (t + 1) * slot_cap, :] = back_ref[k, half:, :]
    asked = lanes([asked_ref[order.index(t):order.index(t) + 1, :] for t in range(owners)])
    digit = lax.broadcasted_iota(i32, (TAIL, asked.shape[1]), 0)
    digits = jnp.where(digit == 0, asked >> 8, jnp.where(digit == 1, asked & 255, 0))
    out_ref[half + owners * slot_cap:, :] = digits.astype(f32).astype(bf16)


def hot_half(hot_ref, which):
    half = hot_ref.shape[1] // 2
    return jnp.where(which == 0, hot_ref[:, 0:half], hot_ref[:, half:])


def row_grads(which, hot_ref, part_refs, put, rows):
    half = hot_ref.shape[1] // 2
    hot_ids = hot_half(hot_ref, which)
    cold_ids = []
    for part_ref in part_refs:
        digits = part_ref[part_ref.shape[0] - TAIL:, :].astype(f32).astype(i32)
        cold_ids.append(digits[0:1, :] * 256 + digits[1:2, :])
    step = 128
    for start in range(0, rows, step):
        hot_pick = one_hot(hot_ids, (step, half), 0, start)
        grads = []
        for ids, part_ref in zip(cold_ids, part_refs):
            pick = one_hot(ids, (step, ids.shape[1]), 0, start)
            hot = jnp.dot(hot_pick, part_ref[0:half, :], preferred_element_type=f32)
            grads.append(hot + jnp.dot(pick, part_ref[half:part_ref.shape[0] - TAIL, :], preferred_element_type=f32))
        put(slice(start, start + step), grads)


def near_grads_body(hot_ref, *refs):
    near_refs, (far_ref, sum_ref, far_sum_ref) = refs[:-3], refs[-3:]

    def put_near(at, grads):
        sum_ref[at, :] = grads[0] + grads[1]

    def put_far(at, grads):
        far_sum_ref[at, :] = grads[0]

    row_grads(core(), hot_ref, near_refs, put_near, sum_ref.shape[0])
    row_grads(1 - core(), hot_ref, [far_ref], put_far, sum_ref.shape[0])


def update_body(hot_ref, sum_ref, table_ref, near_ref, far_ref, part_ref, *refs):
    new_table_ref, new_sum_ref, squares, grads, staged, sums, sems = refs
    rows, width = table_ref.shape
    step = 128

    def put(at, parts):
        grad = near_ref[at, :] + (far_ref[at, :] + parts[0])
        grads[at, :] = grad
        square = grad * grad
        square = sum(square[:, k:k + 128] for k in range(0, width, 128)).T
        squares[at.start // step:at.stop // step, :] = jnp.sum(square, axis=0, keepdims=True)

    row_grads(1 - core(), hot_ref, [part_ref], put, rows)
    new_sum = sum_ref[...] + squares[...] * (1.0 / width)
    sums[...] = new_sum
    scale = (learning_rate / jnp.sqrt(new_sum)).T
    for start in range(0, rows, step):
        at = slice(start, start + step)
        k = start // step
        staged[at, :] = table_ref[at, :] - grads[at, :] * scale[:, k:k + 1]
    copies = [
        pltpu.make_async_copy(staged, new_table_ref, sems.at[0]),
        pltpu.make_async_copy(sums, new_sum_ref, sems.at[1]),
    ]
    for copy in copies:
        copy.start()
    for copy in copies:
        copy.wait()


def dense_body(order, hot_ref, asked_ref, back_ref, out_ref):
    owners, slot_cap = asked_ref.shape
    half = back_ref.shape[1] - slot_cap
    rows = out_ref.shape[0]
    hot = jnp.sum(back_ref[:, 0:half, :].astype(f32), axis=0).astype(bf16)
    grad = jnp.dot(one_hot(hot_half(hot_ref, core()), (rows, half), 0), hot, preferred_element_type=f32)
    for k, t in enumerate(order):
        pick = one_hot(asked_ref[k:k + 1, :], (rows, slot_cap), 0)
        grad += jnp.dot(pick, back_ref[k, half:, :], preferred_element_type=f32)
    out_ref[...] = grad.astype(bf16)


def exchange(x, order):
    return lax.all_to_all(x, "table", split_axis=0, concat_axis=0, tiled=True, axis_index_groups=[list(order)])


def swap(x, bit):
    return lax.ppermute(x, "dp", [(g, g ^ bit) for g in range(lax.axis_size("dp"))])


def per_device(bag_slots, labels, cold_ids, cold_count, table, adagrad_sum, hot_ids, w_in, w_out):
    owners = lax.axis_size("table")
    groups = lax.axis_size("dp")
    hot_dev = hot_ids.shape[0]
    slot_cap = cold_ids.shape[2]
    batch = bag_slots.shape[0]
    rows, width = table.shape
    hidden_units = w_in.shape[1]
    half = hot_dev // 2
    vocab = owners * (hot_dev + slot_cap)
    shape = jax.ShapeDtypeStruct

    hot_row = hot_ids.reshape(1, hot_dev)
    straight = tuple(range(owners))
    requests = call(
        turn_body,
        shape((owners, slot_cap), i32),
        (pltpu.with_memory_space_constraint(cold_ids[0], pltpu.HBM),),
        [pltpu.SemaphoreType.DMA((2,))],
        in_specs=[HBM],
        out_specs=HBM,
    )
    order = straight[owners // 2:] + straight[:owners // 2]
    asked = exchange(requests, order)
    slots = bag_slots.T
    first = FIRST * batch // 4
    rest = shape((slots.shape[0], batch - first), i32)
    packed, key, unit, hot, table_bf = call(
        prepare_body,
        (
            shape((vocab // FIELDS, first), i32),
            rest,
            rest,
            shape((hot_dev, width), bf16),
            shape((rows, width), bf16),
        ),
        tuple(pltpu.with_memory_space_constraint(x, pltpu.HBM) for x in (cold_count, slots, hot_row, table)),
        [
            pltpu.VMEM(cold_count.shape, i32),
            pltpu.VMEM(slots.shape, i32),
            pltpu.VMEM(hot_row.shape, i32),
            pltpu.VMEM(table.shape, f32),
            pltpu.SemaphoreType.DMA((4,)),
        ],
        in_specs=[HBM] * 4,
    )
    asked, packed = lax.optimization_barrier((asked, packed))
    served = call(
        functools.partial(serve_body, order),
        shape((owners, half + slot_cap, width), bf16),
        (asked, hot, table_bf),
        [pltpu.VMEM((owners * slot_cap, rows), bf16)],
    )
    own_rows = exchange(served, order)
    first_rows = call(first_rows_body, shape((owners, half, width), bf16), (own_rows,))
    first_rows, packed = lax.optimization_barrier((first_rows, packed))
    mate_rows = swap(first_rows, 1)
    inc = call(incidence_body, shape((batch, vocab), bf16), (packed, key, unit), [pltpu.VMEM((vocab, batch), bf16)])
    dpooled = call(
        functools.partial(top_body, order),
        shape((batch, width), bf16),
        (labels.reshape(-1, 128), inc, own_rows, mate_rows, w_in, w_out.reshape(-1, 128)),
        [
            pltpu.VMEM((batch, hidden_units), bf16),
            pltpu.VMEM((vocab, width), bf16),
            pltpu.VMEM((batch, width), bf16),
            pltpu.VMEM((batch, 128), f32),
            pltpu.VMEM((batch, 128), f32),
        ],
    )
    hot_half = owners * half
    to_mate = call(mate_grads_body, shape((hot_half, width), bf16), (inc, dpooled))
    got = swap(to_mate.reshape(owners, half, width), 1)
    hot_grads, cold_grads = call(
        own_grads_body,
        (shape((hot_half, width), f32), shape((owners * slot_cap, width), bf16)),
        (inc, dpooled),
    )
    summed = call(
        functools.partial(pack_grads_body, order),
        shape((owners, half + slot_cap, width), bf16),
        (hot_grads, got, cold_grads),
    )
    returned = exchange(summed, order)
    size = half + owners * slot_cap + TAIL
    if groups == 4 and 2 * size <= rows and owners * slot_cap == width:
        own = call(functools.partial(collect_body, order), shape((size, width), bf16), (asked, returned))
        beside = swap(own, 2)
        far_own, far_beside = swap(own, 1), swap(beside, 1)
        dense = shape((rows, width), f32)
        near, far = call(near_grads_body, (dense, dense), (hot_row, own, beside, far_own))
        new_table, new_sum = call(
            update_body,
            (dense, shape((rows // 128, 128), f32)),
            (hot_row, adagrad_sum.reshape(-1, 128), table, near, far, far_beside),
            [
                pltpu.VMEM((rows // 128, 128), f32),
                pltpu.VMEM((rows, width), f32),
                pltpu.VMEM((rows, width), f32),
                pltpu.VMEM((rows // 128, 128), f32),
                pltpu.SemaphoreType.DMA((2,)),
            ],
            out_specs=(HBM, HBM),
        )
        return new_table, new_sum.reshape(rows)
    grad = call(functools.partial(dense_body, order), shape((rows, width), bf16), (hot_row, asked, returned))
    grad = lax.psum(grad, "dp").astype(f32)
    new_sum = adagrad_sum + jnp.mean(grad * grad, axis=1)
    return table - learning_rate * grad / jnp.sqrt(new_sum)[:, None], new_sum


def solution(mesh):
    placed = (
        P(("dp", "table"), None),
        P(("dp", "table")),
        P(("dp", "table"), None, None),
        P(("dp", "table"), None),
        P("table", None),
        P("table"),
        P("table"),
        P(),
        P(),
    )
    return jax.shard_map(
        per_device,
        mesh=mesh,
        in_specs=placed,
        out_specs=(P("table", None), P("table")),
        check_vma=False,
    )
```

```python
import functools
import math

import jax
import jax.numpy as jnp
from jax import lax
from jax.experimental import pallas as pl
from jax.experimental.pallas import tpu as pltpu
from jax.sharding import PartitionSpec as P

learning_rate = 0.3
f32, bf16, i32 = jnp.float32, jnp.bfloat16, jnp.int32
VMEM = pl.BlockSpec(memory_space=pltpu.VMEM)
HBM = pl.BlockSpec(memory_space=pltpu.HBM)
FIELDS = 4
FIELD_BITS = 8
TAIL = 16
FIRST = 2


def call(body, outs, operands, scratch=(), in_specs=None, out_specs=None):
    held = jax.tree.leaves((outs, operands)) + [x for x in scratch if getattr(x, "memory_space", None) == pltpu.VMEM]
    limit = sum(math.prod(x.shape) * jnp.dtype(x.dtype).itemsize for x in held) + 4 * 1024 * 1024
    return pl.pallas_call(
        body,
        out_shape=outs,
        in_specs=in_specs or [VMEM] * len(operands),
        out_specs=out_specs or jax.tree.map(lambda _: VMEM, outs),
        scratch_shapes=list(scratch),
        compiler_params=pltpu.CompilerParams(vmem_limit_bytes=limit),
    )(*operands)


def lanes(pieces):
    return jnp.concatenate(pieces, axis=1)


def one_hot(ids, shape, axis, start=0):
    return (lax.broadcasted_iota(i32, shape, axis) + start == ids).astype(f32).astype(bf16)


def entries(hot_dev, counts, slots, field):
    owners = counts.shape[1]
    slot_cap = FIELDS * field // owners - hot_dev
    half = hot_dev // 2
    hot_cols = owners * hot_dev
    place = slots % hot_dev
    hot = jnp.where(place // half == core(), 0, owners * half) + (slots // hot_dev) * half + place % half
    column = jnp.where(slots < hot_cols, hot, slots)
    cold = slots - hot_cols
    live = slots >= 0
    for t in range(owners):
        at = cold - t * slot_cap
        live = live & ((at < counts[:, t:t + 1]) | (at >= slot_cap))
    key = jnp.where(live, column % field, -1)
    return key, jnp.left_shift(jnp.ones_like(slots), FIELD_BITS * (column // field))


def count(key, unit, field):
    row = lax.broadcasted_iota(i32, (field, key.shape[1]), 0)
    packed = jnp.zeros(row.shape, i32)
    for entry in range(key.shape[0]):
        packed += jnp.where(row == key[entry:entry + 1, :], unit[entry:entry + 1, :], 0)
    return packed


def turn_body(ids_ref, out_ref, sems):
    half = ids_ref.shape[0] // 2
    copies = [
        pltpu.make_async_copy(ids_ref.at[k * half:(k + 1) * half], out_ref.at[(1 - k) * half:(2 - k) * half], sems.at[k])
        for k in range(2)
    ]
    for copy in copies:
        copy.start()
    for copy in copies:
        copy.wait()


def prepare_body(count_ref, slots_ref, ids_ref, table_ref, packed_ref, key_ref, unit_ref, hot_ref, table_bf_ref, *scratch):
    counts, slots, ids, table, sems = scratch
    pairs = [(count_ref, counts), (slots_ref, slots), (ids_ref, ids), (table_ref, table)]
    copies = [pltpu.make_async_copy(src, dst, sems.at[k]) for k, (src, dst) in enumerate(pairs)]
    for copy in copies:
        copy.start()
    hot_dev = ids.shape[1]
    field, first = packed_ref.shape
    copies[0].wait()
    copies[1].wait()
    for start in range(0, slots.shape[1], 128):
        at = slice(start, start + 128)
        key, unit = entries(hot_dev, counts[...], slots[:, at], field)
        if start < first:
            packed_ref[:, at] = count(key, unit, field)
        else:
            rest = slice(start - first, start - first + 128)
            key_ref[:, rest], unit_ref[:, rest] = key, unit
    copies[2].wait()
    copies[3].wait()
    table_bf_ref[...] = table[...].astype(bf16)
    column = jnp.broadcast_to(ids[...], (8, hot_dev)).T[:, 0:1]
    pick = one_hot(column, (hot_dev, table.shape[0]), 1)
    hot_ref[...] = jnp.dot(pick, table_bf_ref[...], preferred_element_type=f32).astype(bf16)


def incidence_body(packed_ref, key_ref, unit_ref, out_ref, inc_t_ref):
    field, first = packed_ref.shape
    for start in range(0, out_ref.shape[0], 128):
        at = slice(start, start + 128)
        if start < first:
            packed = packed_ref[:, at]
        else:
            rest = slice(start - first, start - first + 128)
            packed = count(key_ref[:, rest], unit_ref[:, rest], field)
        for k in range(FIELDS):
            part = jnp.right_shift(packed, FIELD_BITS * k) & (2**FIELD_BITS - 1)
            inc_t_ref[k * field:(k + 1) * field, at] = part.astype(f32).astype(bf16)
    out_ref[...] = inc_t_ref[...].T


def core():
    return lax.rem(lax.axis_index("dp"), 2)


def serve_body(order, asked_ref, hot_ref, table_ref, out_ref, pick):
    owners, slot_cap = asked_ref.shape
    half = hot_ref.shape[0] // 2
    asked = asked_ref[...].T
    for k, t in enumerate(order):
        pick[t * slot_cap:(t + 1) * slot_cap, :] = one_hot(asked[:, k:k + 1], (slot_cap, table_ref.shape[0]), 1)
    picked = jnp.dot(pick[...], table_ref[...], preferred_element_type=f32).astype(bf16)
    hot = hot_ref[pl.ds(pl.multiple_of(core() * half, half), half), :]
    for k, t in enumerate(order):
        out_ref[k, 0:half, :] = hot
        out_ref[k, half:, :] = picked[t * slot_cap:(t + 1) * slot_cap]


def first_rows_body(rows_ref, out_ref):
    out_ref[...] = rows_ref[:, 0:out_ref.shape[1], :]


def top_body(order, labels_ref, inc_ref, own_ref, mate_ref, w_in_ref, w_out_ref, out_ref, to_mate_ref, hidden, rows, pooled, total, dlogit):
    batch = inc_ref.shape[0]
    hidden_units, width = w_in_ref.shape[1], w_in_ref.shape[0]
    owners, half, _ = mate_ref.shape
    hot_half = owners * half
    slot_cap = own_ref.shape[1] - half
    size, step, wide = batch // 2, 512, 512
    blocks = [slice(at, at + size) for at in range(0, batch, size)]
    for k, t in enumerate(order):
        rows[t * half:(t + 1) * half, :] = own_ref[k, 0:half, :]
        rows[hot_half + t * half:hot_half + (t + 1) * half, :] = mate_ref[k]
        rows[2 * hot_half + t * slot_cap:2 * hot_half + (t + 1) * slot_cap, :] = own_ref[k, half:, :]
    pooled[...] = jnp.dot(inc_ref[...], rows[...], preferred_element_type=f32).astype(bf16)
    w_out = w_out_ref[...].astype(f32)
    labels = labels_ref[...].T
    for samples in blocks:
        acc = jnp.zeros((size, 128), f32)
        for start in range(0, hidden_units, step):
            cols = slice(start, start + step)
            pre_act = jnp.dot(pooled[samples, :], w_in_ref[:, cols], preferred_element_type=f32)
            own = lanes([w_out[k:k + 1, :] for k in range(start // 128, (start + step) // 128)])
            act = jnp.maximum(pre_act.astype(bf16), jnp.zeros((), bf16))
            hidden[samples, cols] = act
            term = act.astype(f32) * own
            for k in range(0, step, 128):
                acc += term[:, k:k + 128]
        total[samples, :] = acc
        for k in range(samples.start // 128, samples.stop // 128):
            line = slice(k * 128, (k + 1) * 128)
            logit = jnp.sum(total[line, :], axis=1, keepdims=True)
            dlogit[line, :] = jnp.broadcast_to(jax.nn.sigmoid(logit) - labels[:, k:k + 1], (128, 128))
    mate = jnp.zeros((hot_half, width), f32)
    for samples in blocks:
        scale = dlogit[samples, :]
        grad = jnp.zeros((size, width), f32)
        for start in range(0, hidden_units, wide):
            dhidden = lanes([
                jnp.where(
                    hidden[samples, k:k + 128].astype(f32) > 0, scale * w_out[k // 128:k // 128 + 1, :], 0.0
                ).astype(bf16)
                for k in range(start, start + wide, 128)
            ])
            grad += lax.dot_general(
                dhidden, w_in_ref[:, start:start + wide], (((1,), (1,)), ((), ())), preferred_element_type=f32
            )
        out_ref[samples, :] = grad.astype(bf16)
        mate += jnp.dot(
            inc_ref[samples, hot_half:2 * hot_half].T, out_ref[samples, :], preferred_element_type=f32
        )
    to_mate_ref[...] = mate.astype(bf16)


def own_grads_body(inc_ref, dpooled_ref, hot_ref, cold_ref):
    hot_half = hot_ref.shape[0]
    dpooled = dpooled_ref[...]
    hot_ref[...] = jnp.dot(inc_ref[:, 0:hot_half].T, dpooled, preferred_element_type=f32)
    cold_ref[...] = jnp.dot(inc_ref[:, 2 * hot_half:].T, dpooled, preferred_element_type=f32).astype(bf16)


def pack_grads_body(order, hot_ref, got_ref, cold_ref, out_ref):
    owners, half, width = got_ref.shape
    hot = hot_ref[...] + got_ref[...].reshape(owners * half, width).astype(f32)
    slot_cap = out_ref.shape[1] - half
    for k, t in enumerate(order):
        out_ref[k, 0:half, :] = hot[t * half:(t + 1) * half].astype(bf16)
        out_ref[k, half:, :] = cold_ref[t * slot_cap:(t + 1) * slot_cap, :]


def collect_body(order, asked_ref, back_ref, out_ref):
    owners, slot_cap = asked_ref.shape
    half = back_ref.shape[1] - slot_cap
    out_ref[0:half, :] = jnp.sum(back_ref[:, 0:half, :].astype(f32), axis=0).astype(bf16)
    for k, t in enumerate(order):
        out_ref[half + t * slot_cap:half + (t + 1) * slot_cap, :] = back_ref[k, half:, :]
    asked = lanes([asked_ref[order.index(t):order.index(t) + 1, :] for t in range(owners)])
    digit = lax.broadcasted_iota(i32, (TAIL, asked.shape[1]), 0)
    digits = jnp.where(digit == 0, asked >> 8, jnp.where(digit == 1, asked & 255, 0))
    out_ref[half + owners * slot_cap:, :] = digits.astype(f32).astype(bf16)


def hot_half(hot_ref, which):
    half = hot_ref.shape[1] // 2
    return jnp.where(which == 0, hot_ref[:, 0:half], hot_ref[:, half:])


def row_grads(which, hot_ref, part_refs, put, rows):
    half = hot_ref.shape[1] // 2
    hot_ids = hot_half(hot_ref, which)
    cold_ids = []
    for part_ref in part_refs:
        digits = part_ref[part_ref.shape[0] - TAIL:, :].astype(f32).astype(i32)
        cold_ids.append(digits[0:1, :] * 256 + digits[1:2, :])
    step = 128
    for start in range(0, rows, step):
        hot_pick = one_hot(hot_ids, (step, half), 0, start)
        grads = []
        for ids, part_ref in zip(cold_ids, part_refs):
            pick = one_hot(ids, (step, ids.shape[1]), 0, start)
            hot = jnp.dot(hot_pick, part_ref[0:half, :], preferred_element_type=f32)
            grads.append(hot + jnp.dot(pick, part_ref[half:part_ref.shape[0] - TAIL, :], preferred_element_type=f32))
        put(slice(start, start + step), grads)


def near_grads_body(hot_ref, *refs):
    near_refs, (far_ref, sum_ref, far_sum_ref) = refs[:-3], refs[-3:]

    def put_near(at, grads):
        sum_ref[at, :] = grads[0] + grads[1]

    def put_far(at, grads):
        far_sum_ref[at, :] = grads[0]

    row_grads(core(), hot_ref, near_refs, put_near, sum_ref.shape[0])
    row_grads(1 - core(), hot_ref, [far_ref], put_far, sum_ref.shape[0])


def update_body(hot_ref, sum_ref, table_ref, near_ref, far_ref, part_ref, *refs):
    new_table_ref, new_sum_ref, squares, grads, staged, sums, sems = refs
    rows, width = table_ref.shape
    step = 128

    def put(at, parts):
        grad = near_ref[at, :] + (far_ref[at, :] + parts[0])
        grads[at, :] = grad
        square = grad * grad
        square = sum(square[:, k:k + 128] for k in range(0, width, 128)).T
        squares[at.start // step:at.stop // step, :] = jnp.sum(square, axis=0, keepdims=True)

    row_grads(1 - core(), hot_ref, [part_ref], put, rows)
    new_sum = sum_ref[...] + squares[...] * (1.0 / width)
    sums[...] = new_sum
    scale = (learning_rate / jnp.sqrt(new_sum)).T
    for start in range(0, rows, step):
        at = slice(start, start + step)
        k = start // step
        staged[at, :] = table_ref[at, :] - grads[at, :] * scale[:, k:k + 1]
    copies = [
        pltpu.make_async_copy(staged, new_table_ref, sems.at[0]),
        pltpu.make_async_copy(sums, new_sum_ref, sems.at[1]),
    ]
    for copy in copies:
        copy.start()
    for copy in copies:
        copy.wait()


def dense_body(order, hot_ref, asked_ref, back_ref, out_ref):
    owners, slot_cap = asked_ref.shape
    half = back_ref.shape[1] - slot_cap
    rows = out_ref.shape[0]
    hot = jnp.sum(back_ref[:, 0:half, :].astype(f32), axis=0).astype(bf16)
    grad = jnp.dot(one_hot(hot_half(hot_ref, core()), (rows, half), 0), hot, preferred_element_type=f32)
    for k, t in enumerate(order):
        pick = one_hot(asked_ref[k:k + 1, :], (rows, slot_cap), 0)
        grad += jnp.dot(pick, back_ref[k, half:, :], preferred_element_type=f32)
    out_ref[...] = grad.astype(bf16)


def exchange(x, order):
    return lax.all_to_all(x, "table", split_axis=0, concat_axis=0, tiled=True, axis_index_groups=[list(order)])


def swap(x, bit):
    return lax.ppermute(x, "dp", [(g, g ^ bit) for g in range(lax.axis_size("dp"))])


def per_device(bag_slots, labels, cold_ids, cold_count, table, adagrad_sum, hot_ids, w_in, w_out):
    owners = lax.axis_size("table")
    groups = lax.axis_size("dp")
    hot_dev = hot_ids.shape[0]
    slot_cap = cold_ids.shape[2]
    batch = bag_slots.shape[0]
    rows, width = table.shape
    hidden_units = w_in.shape[1]
    half = hot_dev // 2
    vocab = owners * (hot_dev + slot_cap)
    shape = jax.ShapeDtypeStruct

    hot_row = hot_ids.reshape(1, hot_dev)
    straight = tuple(range(owners))
    requests = call(
        turn_body,
        shape((owners, slot_cap), i32),
        (pltpu.with_memory_space_constraint(cold_ids[0], pltpu.HBM),),
        [pltpu.SemaphoreType.DMA((2,))],
        in_specs=[HBM],
        out_specs=HBM,
    )
    order = straight[owners // 2:] + straight[:owners // 2]
    asked = exchange(requests, order)
    slots = bag_slots.T
    first = FIRST * batch // 4
    rest = shape((slots.shape[0], batch - first), i32)
    packed, key, unit, hot, table_bf = call(
        prepare_body,
        (
            shape((vocab // FIELDS, first), i32),
            rest,
            rest,
            shape((hot_dev, width), bf16),
            shape((rows, width), bf16),
        ),
        tuple(pltpu.with_memory_space_constraint(x, pltpu.HBM) for x in (cold_count, slots, hot_row, table)),
        [
            pltpu.VMEM(cold_count.shape, i32),
            pltpu.VMEM(slots.shape, i32),
            pltpu.VMEM(hot_row.shape, i32),
            pltpu.VMEM(table.shape, f32),
            pltpu.SemaphoreType.DMA((4,)),
        ],
        in_specs=[HBM] * 4,
    )
    asked, packed = lax.optimization_barrier((asked, packed))
    served = call(
        functools.partial(serve_body, order),
        shape((owners, half + slot_cap, width), bf16),
        (asked, hot, table_bf),
        [pltpu.VMEM((owners * slot_cap, rows), bf16)],
    )
    own_rows = exchange(served, order)
    first_rows = call(first_rows_body, shape((owners, half, width), bf16), (own_rows,))
    first_rows, packed = lax.optimization_barrier((first_rows, packed))
    mate_rows = swap(first_rows, 1)
    inc = call(incidence_body, shape((batch, vocab), bf16), (packed, key, unit), [pltpu.VMEM((vocab, batch), bf16)])
    hot_half = owners * half
    dpooled, to_mate = call(
        functools.partial(top_body, order),
        (shape((batch, width), bf16), shape((hot_half, width), bf16)),
        (labels.reshape(-1, 128), inc, own_rows, mate_rows, w_in, w_out.reshape(-1, 128)),
        [
            pltpu.VMEM((batch, hidden_units), bf16),
            pltpu.VMEM((vocab, width), bf16),
            pltpu.VMEM((batch, width), bf16),
            pltpu.VMEM((batch, 128), f32),
            pltpu.VMEM((batch, 128), f32),
        ],
    )
    got = swap(to_mate.reshape(owners, half, width), 1)
    hot_grads, cold_grads = call(
        own_grads_body,
        (shape((hot_half, width), f32), shape((owners * slot_cap, width), bf16)),
        (inc, dpooled),
    )
    summed = call(
        functools.partial(pack_grads_body, order),
        shape((owners, half + slot_cap, width), bf16),
        (hot_grads, got, cold_grads),
    )
    returned = exchange(summed, order)
    size = half + owners * slot_cap + TAIL
    if groups == 4 and 2 * size <= rows and owners * slot_cap == width:
        own = call(functools.partial(collect_body, order), shape((size, width), bf16), (asked, returned))
        beside = swap(own, 2)
        far_own, far_beside = swap(own, 1), swap(beside, 1)
        dense = shape((rows, width), f32)
        near, far = call(near_grads_body, (dense, dense), (hot_row, own, beside, far_own))
        new_table, new_sum = call(
            update_body,
            (dense, shape((rows // 128, 128), f32)),
            (hot_row, adagrad_sum.reshape(-1, 128), table, near, far, far_beside),
            [
                pltpu.VMEM((rows // 128, 128), f32),
                pltpu.VMEM((rows, width), f32),
                pltpu.VMEM((rows, width), f32),
                pltpu.VMEM((rows // 128, 128), f32),
                pltpu.SemaphoreType.DMA((2,)),
            ],
            out_specs=(HBM, HBM),
        )
        return new_table, new_sum.reshape(rows)
    grad = call(functools.partial(dense_body, order), shape((rows, width), bf16), (hot_row, asked, returned))
    grad = lax.psum(grad, "dp").astype(f32)
    new_sum = adagrad_sum + jnp.mean(grad * grad, axis=1)
    return table - learning_rate * grad / jnp.sqrt(new_sum)[:, None], new_sum


def solution(mesh):
    placed = (
        P(("dp", "table"), None),
        P(("dp", "table")),
        P(("dp", "table"), None, None),
        P(("dp", "table"), None),
        P("table", None),
        P("table"),
        P("table"),
        P(),
        P(),
    )
    return jax.shard_map(
        per_device,
        mesh=mesh,
        in_specs=placed,
        out_specs=(P("table", None), P("table")),
        check_vma=False,
    )
```

```python
import functools
import math

import jax
import jax.numpy as jnp
from jax import lax
from jax.experimental import pallas as pl
from jax.experimental.pallas import tpu as pltpu
from jax.sharding import PartitionSpec as P

learning_rate = 0.3
f32, bf16, i32 = jnp.float32, jnp.bfloat16, jnp.int32
VMEM = pl.BlockSpec(memory_space=pltpu.VMEM)
HBM = pl.BlockSpec(memory_space=pltpu.HBM)
FIELDS = 4
FIELD_BITS = 8
TAIL = 16
FIRST = 2


def call(body, outs, operands, scratch=(), in_specs=None, out_specs=None):
    held = jax.tree.leaves((outs, operands)) + [x for x in scratch if getattr(x, "memory_space", None) == pltpu.VMEM]
    limit = sum(math.prod(x.shape) * jnp.dtype(x.dtype).itemsize for x in held) + 4 * 1024 * 1024
    return pl.pallas_call(
        body,
        out_shape=outs,
        in_specs=in_specs or [VMEM] * len(operands),
        out_specs=out_specs or jax.tree.map(lambda _: VMEM, outs),
        scratch_shapes=list(scratch),
        compiler_params=pltpu.CompilerParams(vmem_limit_bytes=limit),
    )(*operands)


def lanes(pieces):
    return jnp.concatenate(pieces, axis=1)


def one_hot(ids, shape, axis, start=0):
    return (lax.broadcasted_iota(i32, shape, axis) + start == ids).astype(f32).astype(bf16)


def entries(hot_dev, counts, slots, field):
    owners = counts.shape[1]
    slot_cap = FIELDS * field // owners - hot_dev
    half = hot_dev // 2
    hot_cols = owners * hot_dev
    place = slots % hot_dev
    hot = jnp.where(place // half == core(), 0, owners * half) + (slots // hot_dev) * half + place % half
    column = jnp.where(slots < hot_cols, hot, slots)
    cold = slots - hot_cols
    live = slots >= 0
    for t in range(owners):
        at = cold - t * slot_cap
        live = live & ((at < counts[:, t:t + 1]) | (at >= slot_cap))
    key = jnp.where(live, column % field, -1)
    return key, jnp.left_shift(jnp.ones_like(slots), FIELD_BITS * (column // field))


def count(key, unit, field):
    row = lax.broadcasted_iota(i32, (field, key.shape[1]), 0)
    packed = jnp.zeros(row.shape, i32)
    for entry in range(key.shape[0]):
        packed += jnp.where(row == key[entry:entry + 1, :], unit[entry:entry + 1, :], 0)
    return packed


def turn_body(ids_ref, out_ref, sems):
    half = ids_ref.shape[0] // 2
    copies = [
        pltpu.make_async_copy(ids_ref.at[k * half:(k + 1) * half], out_ref.at[(1 - k) * half:(2 - k) * half], sems.at[k])
        for k in range(2)
    ]
    for copy in copies:
        copy.start()
    for copy in copies:
        copy.wait()


def prepare_body(count_ref, slots_ref, ids_ref, table_ref, packed_ref, key_ref, unit_ref, hot_ref, table_bf_ref, *scratch):
    counts, slots, ids, table, sems = scratch
    pairs = [(count_ref, counts), (slots_ref, slots), (ids_ref, ids), (table_ref, table)]
    copies = [pltpu.make_async_copy(src, dst, sems.at[k]) for k, (src, dst) in enumerate(pairs)]
    for copy in copies:
        copy.start()
    hot_dev = ids.shape[1]
    field, first = packed_ref.shape
    copies[0].wait()
    copies[1].wait()
    for start in range(0, slots.shape[1], 128):
        at = slice(start, start + 128)
        key, unit = entries(hot_dev, counts[...], slots[:, at], field)
        if start < first:
            packed_ref[:, at] = count(key, unit, field)
        else:
            rest = slice(start - first, start - first + 128)
            key_ref[:, rest], unit_ref[:, rest] = key, unit
    copies[2].wait()
    copies[3].wait()
    table_bf_ref[...] = table[...].astype(bf16)
    column = jnp.broadcast_to(ids[...], (8, hot_dev)).T[:, 0:1]
    pick = one_hot(column, (hot_dev, table.shape[0]), 1)
    hot_ref[...] = jnp.dot(pick, table_bf_ref[...], preferred_element_type=f32).astype(bf16)


def incidence_body(packed_ref, key_ref, unit_ref, out_ref, inc_t_ref):
    field, first = packed_ref.shape
    for start in range(0, out_ref.shape[0], 128):
        at = slice(start, start + 128)
        if start < first:
            packed = packed_ref[:, at]
        else:
            rest = slice(start - first, start - first + 128)
            packed = count(key_ref[:, rest], unit_ref[:, rest], field)
        for k in range(FIELDS):
            part = jnp.right_shift(packed, FIELD_BITS * k) & (2**FIELD_BITS - 1)
            inc_t_ref[k * field:(k + 1) * field, at] = part.astype(f32).astype(bf16)
    out_ref[...] = inc_t_ref[...].T


def core():
    return lax.rem(lax.axis_index("dp"), 2)


def serve_body(ask_order, order, asked_ref, hot_ref, table_ref, out_ref, pick):
    owners, slot_cap = asked_ref.shape
    half = hot_ref.shape[0] // 2
    asked = asked_ref[...].T
    for k, t in enumerate(ask_order):
        pick[t * slot_cap:(t + 1) * slot_cap, :] = one_hot(asked[:, k:k + 1], (slot_cap, table_ref.shape[0]), 1)
    picked = jnp.dot(pick[...], table_ref[...], preferred_element_type=f32).astype(bf16)
    hot = hot_ref[pl.ds(pl.multiple_of(core() * half, half), half), :]
    for k, t in enumerate(order):
        out_ref[k, 0:half, :] = hot
        out_ref[k, half:, :] = picked[t * slot_cap:(t + 1) * slot_cap]


def first_rows_body(rows_ref, out_ref):
    out_ref[...] = rows_ref[:, 0:out_ref.shape[1], :]


def top_body(order, labels_ref, inc_ref, own_ref, mate_ref, w_in_ref, w_out_ref, out_ref, to_mate_ref, hidden, rows, pooled, total, dlogit):
    batch = inc_ref.shape[0]
    hidden_units, width = w_in_ref.shape[1], w_in_ref.shape[0]
    owners, half, _ = mate_ref.shape
    hot_half = owners * half
    slot_cap = own_ref.shape[1] - half
    size, step, wide = batch // 2, 512, 512
    blocks = [slice(at, at + size) for at in range(0, batch, size)]
    for k, t in enumerate(order):
        rows[t * half:(t + 1) * half, :] = own_ref[k, 0:half, :]
        rows[hot_half + t * half:hot_half + (t + 1) * half, :] = mate_ref[k]
        rows[2 * hot_half + t * slot_cap:2 * hot_half + (t + 1) * slot_cap, :] = own_ref[k, half:, :]
    pooled[...] = jnp.dot(inc_ref[...], rows[...], preferred_element_type=f32).astype(bf16)
    w_out = w_out_ref[...].astype(f32)
    labels = labels_ref[...].T
    for samples in blocks:
        acc = jnp.zeros((size, 128), f32)
        for start in range(0, hidden_units, step):
            cols = slice(start, start + step)
            pre_act = jnp.dot(pooled[samples, :], w_in_ref[:, cols], preferred_element_type=f32)
            own = lanes([w_out[k:k + 1, :] for k in range(start // 128, (start + step) // 128)])
            act = jnp.maximum(pre_act.astype(bf16), jnp.zeros((), bf16))
            hidden[samples, cols] = act
            term = act.astype(f32) * own
            for k in range(0, step, 128):
                acc += term[:, k:k + 128]
        total[samples, :] = acc
        for k in range(samples.start // 128, samples.stop // 128):
            line = slice(k * 128, (k + 1) * 128)
            logit = jnp.sum(total[line, :], axis=1, keepdims=True)
            dlogit[line, :] = jnp.broadcast_to(jax.nn.sigmoid(logit) - labels[:, k:k + 1], (128, 128))
    mate = jnp.zeros((hot_half, width), f32)
    for samples in blocks:
        scale = dlogit[samples, :]
        grad = jnp.zeros((size, width), f32)
        for start in range(0, hidden_units, wide):
            dhidden = lanes([
                jnp.where(
                    hidden[samples, k:k + 128].astype(f32) > 0, scale * w_out[k // 128:k // 128 + 1, :], 0.0
                ).astype(bf16)
                for k in range(start, start + wide, 128)
            ])
            grad += lax.dot_general(
                dhidden, w_in_ref[:, start:start + wide], (((1,), (1,)), ((), ())), preferred_element_type=f32
            )
        out_ref[samples, :] = grad.astype(bf16)
        mate += jnp.dot(
            inc_ref[samples, hot_half:2 * hot_half].T, out_ref[samples, :], preferred_element_type=f32
        )
    to_mate_ref[...] = mate.astype(bf16)


def own_grads_body(inc_ref, dpooled_ref, hot_ref, cold_ref):
    hot_half = hot_ref.shape[0]
    dpooled = dpooled_ref[...]
    hot_ref[...] = jnp.dot(inc_ref[:, 0:hot_half].T, dpooled, preferred_element_type=f32)
    cold_ref[...] = jnp.dot(inc_ref[:, 2 * hot_half:].T, dpooled, preferred_element_type=f32).astype(bf16)


def pack_grads_body(order, hot_ref, got_ref, cold_ref, out_ref):
    owners, half, width = got_ref.shape
    hot = hot_ref[...] + got_ref[...].reshape(owners * half, width).astype(f32)
    slot_cap = out_ref.shape[1] - half
    for k, t in enumerate(order):
        out_ref[k, 0:half, :] = hot[t * half:(t + 1) * half].astype(bf16)
        out_ref[k, half:, :] = cold_ref[t * slot_cap:(t + 1) * slot_cap, :]


def collect_body(ask_order, order, asked_ref, back_ref, out_ref):
    owners, slot_cap = asked_ref.shape
    half = back_ref.shape[1] - slot_cap
    out_ref[0:half, :] = jnp.sum(back_ref[:, 0:half, :].astype(f32), axis=0).astype(bf16)
    for k, t in enumerate(order):
        out_ref[half + t * slot_cap:half + (t + 1) * slot_cap, :] = back_ref[k, half:, :]
    asked = lanes([asked_ref[ask_order.index(t):ask_order.index(t) + 1, :] for t in range(owners)])
    digit = lax.broadcasted_iota(i32, (TAIL, asked.shape[1]), 0)
    digits = jnp.where(digit == 0, asked >> 8, jnp.where(digit == 1, asked & 255, 0))
    out_ref[half + owners * slot_cap:, :] = digits.astype(f32).astype(bf16)


def hot_half(hot_ref, which):
    half = hot_ref.shape[1] // 2
    return jnp.where(which == 0, hot_ref[:, 0:half], hot_ref[:, half:])


def row_grads(which, hot_ref, part_refs, put, rows):
    half = hot_ref.shape[1] // 2
    hot_ids = hot_half(hot_ref, which)
    cold_ids = []
    for part_ref in part_refs:
        digits = part_ref[part_ref.shape[0] - TAIL:, :].astype(f32).astype(i32)
        cold_ids.append(digits[0:1, :] * 256 + digits[1:2, :])
    step = 128
    for start in range(0, rows, step):
        hot_pick = one_hot(hot_ids, (step, half), 0, start)
        grads = []
        for ids, part_ref in zip(cold_ids, part_refs):
            pick = one_hot(ids, (step, ids.shape[1]), 0, start)
            hot = jnp.dot(hot_pick, part_ref[0:half, :], preferred_element_type=f32)
            grads.append(hot + jnp.dot(pick, part_ref[half:part_ref.shape[0] - TAIL, :], preferred_element_type=f32))
        put(slice(start, start + step), grads)


def near_grads_body(hot_ref, *refs):
    near_refs, (far_ref, sum_ref, far_sum_ref) = refs[:-3], refs[-3:]

    def put_near(at, grads):
        sum_ref[at, :] = grads[0] + grads[1]

    def put_far(at, grads):
        far_sum_ref[at, :] = grads[0]

    row_grads(core(), hot_ref, near_refs, put_near, sum_ref.shape[0])
    row_grads(1 - core(), hot_ref, [far_ref], put_far, sum_ref.shape[0])


def update_body(hot_ref, sum_ref, table_ref, near_ref, far_ref, part_ref, *refs):
    new_table_ref, new_sum_ref, squares, grads, staged, sums, sems = refs
    rows, width = table_ref.shape
    step = 128

    def put(at, parts):
        grad = near_ref[at, :] + (far_ref[at, :] + parts[0])
        grads[at, :] = grad
        square = grad * grad
        square = sum(square[:, k:k + 128] for k in range(0, width, 128)).T
        squares[at.start // step:at.stop // step, :] = jnp.sum(square, axis=0, keepdims=True)

    row_grads(1 - core(), hot_ref, [part_ref], put, rows)
    new_sum = sum_ref[...] + squares[...] * (1.0 / width)
    sums[...] = new_sum
    scale = (learning_rate / jnp.sqrt(new_sum)).T
    for start in range(0, rows, step):
        at = slice(start, start + step)
        k = start // step
        staged[at, :] = table_ref[at, :] - grads[at, :] * scale[:, k:k + 1]
    copies = [
        pltpu.make_async_copy(staged, new_table_ref, sems.at[0]),
        pltpu.make_async_copy(sums, new_sum_ref, sems.at[1]),
    ]
    for copy in copies:
        copy.start()
    for copy in copies:
        copy.wait()


def dense_body(ask_order, order, hot_ref, asked_ref, back_ref, out_ref):
    owners, slot_cap = asked_ref.shape
    half = back_ref.shape[1] - slot_cap
    rows = out_ref.shape[0]
    hot = jnp.sum(back_ref[:, 0:half, :].astype(f32), axis=0).astype(bf16)
    grad = jnp.dot(one_hot(hot_half(hot_ref, core()), (rows, half), 0), hot, preferred_element_type=f32)
    for k, t in enumerate(order):
        at = ask_order.index(t)
        pick = one_hot(asked_ref[at:at + 1, :], (rows, slot_cap), 0)
        grad += jnp.dot(pick, back_ref[k, half:, :], preferred_element_type=f32)
    out_ref[...] = grad.astype(bf16)


def exchange(x, order):
    return lax.all_to_all(x, "table", split_axis=0, concat_axis=0, tiled=True, axis_index_groups=[list(order)])


def swap(x, bit):
    return lax.ppermute(x, "dp", [(g, g ^ bit) for g in range(lax.axis_size("dp"))])


def per_device(bag_slots, labels, cold_ids, cold_count, table, adagrad_sum, hot_ids, w_in, w_out):
    owners = lax.axis_size("table")
    groups = lax.axis_size("dp")
    hot_dev = hot_ids.shape[0]
    slot_cap = cold_ids.shape[2]
    batch = bag_slots.shape[0]
    rows, width = table.shape
    hidden_units = w_in.shape[1]
    half = hot_dev // 2
    vocab = owners * (hot_dev + slot_cap)
    shape = jax.ShapeDtypeStruct

    hot_row = hot_ids.reshape(1, hot_dev)
    requests = call(
        turn_body,
        shape((owners, slot_cap), i32),
        (pltpu.with_memory_space_constraint(cold_ids[0], pltpu.HBM),),
        [pltpu.SemaphoreType.DMA((2,))],
        in_specs=[HBM],
        out_specs=HBM,
    )
    ask_order = tuple((t + owners // 2) % owners for t in range(owners))
    order = tuple(t if t % 2 else ask_order[t] for t in range(owners))
    asked = exchange(requests, ask_order)
    slots = bag_slots.T
    first = FIRST * batch // 4
    rest = shape((slots.shape[0], batch - first), i32)
    packed, key, unit, hot, table_bf = call(
        prepare_body,
        (
            shape((vocab // FIELDS, first), i32),
            rest,
            rest,
            shape((hot_dev, width), bf16),
            shape((rows, width), bf16),
        ),
        tuple(pltpu.with_memory_space_constraint(x, pltpu.HBM) for x in (cold_count, slots, hot_row, table)),
        [
            pltpu.VMEM(cold_count.shape, i32),
            pltpu.VMEM(slots.shape, i32),
            pltpu.VMEM(hot_row.shape, i32),
            pltpu.VMEM(table.shape, f32),
            pltpu.SemaphoreType.DMA((4,)),
        ],
        in_specs=[HBM] * 4,
    )
    asked, packed = lax.optimization_barrier((asked, packed))
    served = call(
        functools.partial(serve_body, ask_order, order),
        shape((owners, half + slot_cap, width), bf16),
        (asked, hot, table_bf),
        [pltpu.VMEM((owners * slot_cap, rows), bf16)],
    )
    own_rows = exchange(served, order)
    first_rows = call(first_rows_body, shape((owners, half, width), bf16), (own_rows,))
    first_rows, packed = lax.optimization_barrier((first_rows, packed))
    mate_rows = swap(first_rows, 1)
    inc = call(incidence_body, shape((batch, vocab), bf16), (packed, key, unit), [pltpu.VMEM((vocab, batch), bf16)])
    hot_half = owners * half
    dpooled, to_mate = call(
        functools.partial(top_body, order),
        (shape((batch, width), bf16), shape((hot_half, width), bf16)),
        (labels.reshape(-1, 128), inc, own_rows, mate_rows, w_in, w_out.reshape(-1, 128)),
        [
            pltpu.VMEM((batch, hidden_units), bf16),
            pltpu.VMEM((vocab, width), bf16),
            pltpu.VMEM((batch, width), bf16),
            pltpu.VMEM((batch, 128), f32),
            pltpu.VMEM((batch, 128), f32),
        ],
    )
    got = swap(to_mate.reshape(owners, half, width), 1)
    hot_grads, cold_grads = call(
        own_grads_body,
        (shape((hot_half, width), f32), shape((owners * slot_cap, width), bf16)),
        (inc, dpooled),
    )
    summed = call(
        functools.partial(pack_grads_body, order),
        shape((owners, half + slot_cap, width), bf16),
        (hot_grads, got, cold_grads),
    )
    returned = exchange(summed, order)
    size = half + owners * slot_cap + TAIL
    if groups == 4 and 2 * size <= rows and owners * slot_cap == width:
        own = call(functools.partial(collect_body, ask_order, order), shape((size, width), bf16), (asked, returned))
        beside = swap(own, 2)
        far_own, far_beside = swap(own, 1), swap(beside, 1)
        dense = shape((rows, width), f32)
        near, far = call(near_grads_body, (dense, dense), (hot_row, own, beside, far_own))
        new_table, new_sum = call(
            update_body,
            (dense, shape((rows // 128, 128), f32)),
            (hot_row, adagrad_sum.reshape(-1, 128), table, near, far, far_beside),
            [
                pltpu.VMEM((rows // 128, 128), f32),
                pltpu.VMEM((rows, width), f32),
                pltpu.VMEM((rows, width), f32),
                pltpu.VMEM((rows // 128, 128), f32),
                pltpu.SemaphoreType.DMA((2,)),
            ],
            out_specs=(HBM, HBM),
        )
        return new_table, new_sum.reshape(rows)
    grad = call(functools.partial(dense_body, ask_order, order), shape((rows, width), bf16), (hot_row, asked, returned))
    grad = lax.psum(grad, "dp").astype(f32)
    new_sum = adagrad_sum + jnp.mean(grad * grad, axis=1)
    return table - learning_rate * grad / jnp.sqrt(new_sum)[:, None], new_sum


def solution(mesh):
    placed = (
        P(("dp", "table"), None),
        P(("dp", "table")),
        P(("dp", "table"), None, None),
        P(("dp", "table"), None),
        P("table", None),
        P("table"),
        P("table"),
        P(),
        P(),
    )
    return jax.shard_map(
        per_device,
        mesh=mesh,
        in_specs=placed,
        out_specs=(P("table", None), P("table")),
        check_vma=False,
    )
```

```python
import functools
import math

import jax
import jax.numpy as jnp
from jax import lax
from jax.experimental import pallas as pl
from jax.experimental.pallas import tpu as pltpu
from jax.sharding import PartitionSpec as P

learning_rate = 0.3
f32, bf16, i32 = jnp.float32, jnp.bfloat16, jnp.int32
VMEM = pl.BlockSpec(memory_space=pltpu.VMEM)
HBM = pl.BlockSpec(memory_space=pltpu.HBM)
FIELDS = 4
FIELD_BITS = 8
TAIL = 16
FIRST = 2


def call(body, outs, operands, scratch=(), in_specs=None, out_specs=None):
    held = jax.tree.leaves((outs, operands)) + [x for x in scratch if getattr(x, "memory_space", None) == pltpu.VMEM]
    limit = sum(math.prod(x.shape) * jnp.dtype(x.dtype).itemsize for x in held) + 4 * 1024 * 1024
    return pl.pallas_call(
        body,
        out_shape=outs,
        in_specs=in_specs or [VMEM] * len(operands),
        out_specs=out_specs or jax.tree.map(lambda _: VMEM, outs),
        scratch_shapes=list(scratch),
        compiler_params=pltpu.CompilerParams(vmem_limit_bytes=limit),
    )(*operands)


def lanes(pieces):
    return jnp.concatenate(pieces, axis=1)


def one_hot(ids, shape, axis, start=0):
    return (lax.broadcasted_iota(i32, shape, axis) + start == ids).astype(f32).astype(bf16)


def entries(hot_dev, counts, slots, field):
    owners = counts.shape[1]
    slot_cap = FIELDS * field // owners - hot_dev
    half = hot_dev // 2
    hot_cols = owners * hot_dev
    place = slots % hot_dev
    hot = jnp.where(place // half == core(), 0, owners * half) + (slots // hot_dev) * half + place % half
    column = jnp.where(slots < hot_cols, hot, slots)
    cold = slots - hot_cols
    live = slots >= 0
    for t in range(owners):
        at = cold - t * slot_cap
        live = live & ((at < counts[:, t:t + 1]) | (at >= slot_cap))
    key = jnp.where(live, column % field, -1)
    return key, jnp.left_shift(jnp.ones_like(slots), FIELD_BITS * (column // field))


def count(key, unit, field):
    row = lax.broadcasted_iota(i32, (field, key.shape[1]), 0)
    packed = jnp.zeros(row.shape, i32)
    for entry in range(key.shape[0]):
        packed += jnp.where(row == key[entry:entry + 1, :], unit[entry:entry + 1, :], 0)
    return packed


def turn_body(ids_ref, out_ref, sems):
    half = ids_ref.shape[0] // 2
    copies = [
        pltpu.make_async_copy(ids_ref.at[k * half:(k + 1) * half], out_ref.at[(1 - k) * half:(2 - k) * half], sems.at[k])
        for k in range(2)
    ]
    for copy in copies:
        copy.start()
    for copy in copies:
        copy.wait()


def prepare_body(count_ref, slots_ref, ids_ref, table_ref, packed_ref, key_ref, unit_ref, hot_ref, table_bf_ref, *scratch):
    counts, slots, ids, table, sems = scratch
    pairs = [(count_ref, counts), (slots_ref, slots), (ids_ref, ids), (table_ref, table)]
    copies = [pltpu.make_async_copy(src, dst, sems.at[k]) for k, (src, dst) in enumerate(pairs)]
    for copy in copies:
        copy.start()
    hot_dev = ids.shape[1]
    field, first = packed_ref.shape
    copies[0].wait()
    copies[1].wait()
    for start in range(0, slots.shape[1], 128):
        at = slice(start, start + 128)
        key, unit = entries(hot_dev, counts[...], slots[:, at], field)
        if start < first:
            packed_ref[:, at] = count(key, unit, field)
        else:
            rest = slice(start - first, start - first + 128)
            key_ref[:, rest], unit_ref[:, rest] = key, unit
    copies[2].wait()
    copies[3].wait()
    table_bf_ref[...] = table[...].astype(bf16)
    column = jnp.broadcast_to(ids[...], (8, hot_dev)).T[:, 0:1]
    pick = one_hot(column, (hot_dev, table.shape[0]), 1)
    hot_ref[...] = jnp.dot(pick, table_bf_ref[...], preferred_element_type=f32).astype(bf16)


def incidence_body(packed_ref, key_ref, unit_ref, out_ref, inc_t_ref):
    field, first = packed_ref.shape
    for start in range(0, out_ref.shape[0], 128):
        at = slice(start, start + 128)
        if start < first:
            packed = packed_ref[:, at]
        else:
            rest = slice(start - first, start - first + 128)
            packed = count(key_ref[:, rest], unit_ref[:, rest], field)
        for k in range(FIELDS):
            part = jnp.right_shift(packed, FIELD_BITS * k) & (2**FIELD_BITS - 1)
            inc_t_ref[k * field:(k + 1) * field, at] = part.astype(f32).astype(bf16)
    out_ref[...] = inc_t_ref[...].T


def core():
    return lax.rem(lax.axis_index("dp"), 2)


def serve_body(ask_order, order, asked_ref, hot_ref, table_ref, out_ref, pick):
    owners, slot_cap = asked_ref.shape
    half = hot_ref.shape[0] // 2
    asked = asked_ref[...].T
    for k, t in enumerate(ask_order):
        pick[t * slot_cap:(t + 1) * slot_cap, :] = one_hot(asked[:, k:k + 1], (slot_cap, table_ref.shape[0]), 1)
    picked = jnp.dot(pick[...], table_ref[...], preferred_element_type=f32).astype(bf16)
    hot = hot_ref[pl.ds(pl.multiple_of(core() * half, half), half), :]
    for k, t in enumerate(order):
        out_ref[k, 0:half, :] = hot
        out_ref[k, half:, :] = picked[t * slot_cap:(t + 1) * slot_cap]


def first_rows_body(rows_ref, out_ref):
    out_ref[...] = rows_ref[:, 0:out_ref.shape[1], :]


def top_body(order, labels_ref, inc_ref, own_ref, mate_ref, w_in_ref, w_out_ref, out_ref, to_mate_ref, hidden, rows, pooled, total, dlogit):
    batch = inc_ref.shape[0]
    hidden_units, width = w_in_ref.shape[1], w_in_ref.shape[0]
    owners, half, _ = mate_ref.shape
    hot_half = owners * half
    slot_cap = own_ref.shape[1] - half
    size, step, wide = batch // 2, 512, 512
    blocks = [slice(at, at + size) for at in range(0, batch, size)]
    for k, t in enumerate(order):
        rows[t * half:(t + 1) * half, :] = own_ref[k, 0:half, :]
        rows[hot_half + t * half:hot_half + (t + 1) * half, :] = mate_ref[k]
        rows[2 * hot_half + t * slot_cap:2 * hot_half + (t + 1) * slot_cap, :] = own_ref[k, half:, :]
    pooled[...] = jnp.dot(inc_ref[...], rows[...], preferred_element_type=f32).astype(bf16)
    w_out = w_out_ref[...].astype(f32)
    labels = labels_ref[...].T
    for samples in blocks:
        acc = jnp.zeros((size, 128), f32)
        for start in range(0, hidden_units, step):
            cols = slice(start, start + step)
            pre_act = jnp.dot(pooled[samples, :], w_in_ref[:, cols], preferred_element_type=f32)
            own = lanes([w_out[k:k + 1, :] for k in range(start // 128, (start + step) // 128)])
            act = jnp.maximum(pre_act.astype(bf16), jnp.zeros((), bf16))
            hidden[samples, cols] = act
            term = act.astype(f32) * own
            for k in range(0, step, 128):
                acc += term[:, k:k + 128]
        total[samples, :] = acc
        for k in range(samples.start // 128, samples.stop // 128):
            line = slice(k * 128, (k + 1) * 128)
            logit = jnp.sum(total[line, :], axis=1, keepdims=True)
            dlogit[line, :] = jnp.broadcast_to(jax.nn.sigmoid(logit) - labels[:, k:k + 1], (128, 128))
    mate = jnp.zeros((hot_half, width), f32)
    for samples in blocks:
        scale = dlogit[samples, :]
        grad = jnp.zeros((size, width), f32)
        for start in range(0, hidden_units, wide):
            dhidden = lanes([
                jnp.where(
                    hidden[samples, k:k + 128].astype(f32) > 0, scale * w_out[k // 128:k // 128 + 1, :], 0.0
                ).astype(bf16)
                for k in range(start, start + wide, 128)
            ])
            grad += lax.dot_general(
                dhidden, w_in_ref[:, start:start + wide], (((1,), (1,)), ((), ())), preferred_element_type=f32
            )
        out_ref[samples, :] = grad.astype(bf16)
        mate += jnp.dot(
            inc_ref[samples, hot_half:2 * hot_half].T, out_ref[samples, :], preferred_element_type=f32
        )
    to_mate_ref[...] = mate.astype(bf16)


def own_grads_body(inc_ref, dpooled_ref, hot_ref, cold_ref):
    hot_half = hot_ref.shape[0]
    dpooled = dpooled_ref[...]
    hot_ref[...] = jnp.dot(inc_ref[:, 0:hot_half].T, dpooled, preferred_element_type=f32)
    cold_ref[...] = jnp.dot(inc_ref[:, 2 * hot_half:].T, dpooled, preferred_element_type=f32).astype(bf16)


def pack_grads_body(order, hot_ref, got_ref, cold_ref, out_ref):
    owners, half, width = got_ref.shape
    hot = hot_ref[...] + got_ref[...].reshape(owners * half, width).astype(f32)
    slot_cap = out_ref.shape[1] - half
    for k, t in enumerate(order):
        out_ref[k, 0:half, :] = hot[t * half:(t + 1) * half].astype(bf16)
        out_ref[k, half:, :] = cold_ref[t * slot_cap:(t + 1) * slot_cap, :]


def collect_body(ask_order, order, asked_ref, back_ref, out_ref):
    owners, slot_cap = asked_ref.shape
    half = back_ref.shape[1] - slot_cap
    out_ref[0:half, :] = jnp.sum(back_ref[:, 0:half, :].astype(f32), axis=0).astype(bf16)
    for k, t in enumerate(order):
        out_ref[half + t * slot_cap:half + (t + 1) * slot_cap, :] = back_ref[k, half:, :]
    asked = lanes([asked_ref[ask_order.index(t):ask_order.index(t) + 1, :] for t in range(owners)])
    digit = lax.broadcasted_iota(i32, (TAIL, asked.shape[1]), 0)
    digits = jnp.where(digit == 0, asked >> 8, jnp.where(digit == 1, asked & 255, 0))
    out_ref[half + owners * slot_cap:, :] = digits.astype(f32).astype(bf16)


def hot_half(hot_ref, which):
    half = hot_ref.shape[1] // 2
    return jnp.where(which == 0, hot_ref[:, 0:half], hot_ref[:, half:])


def row_grads(which, hot_ref, part_refs, put, rows):
    half = hot_ref.shape[1] // 2
    hot_ids = hot_half(hot_ref, which)
    cold_ids = []
    for part_ref in part_refs:
        digits = part_ref[part_ref.shape[0] - TAIL:, :].astype(f32).astype(i32)
        cold_ids.append(digits[0:1, :] * 256 + digits[1:2, :])
    step = 128
    for start in range(0, rows, step):
        hot_pick = one_hot(hot_ids, (step, half), 0, start)
        grads = []
        for ids, part_ref in zip(cold_ids, part_refs):
            pick = one_hot(ids, (step, ids.shape[1]), 0, start)
            hot = jnp.dot(hot_pick, part_ref[0:half, :], preferred_element_type=f32)
            grads.append(hot + jnp.dot(pick, part_ref[half:part_ref.shape[0] - TAIL, :], preferred_element_type=f32))
        put(slice(start, start + step), grads)


def near_grads_body(hot_ref, *refs):
    near_refs, (far_ref, sum_ref, far_sum_ref) = refs[:-3], refs[-3:]

    def put_near(at, grads):
        sum_ref[at, :] = grads[0] + grads[1]

    def put_far(at, grads):
        far_sum_ref[at, :] = grads[0]

    row_grads(core(), hot_ref, near_refs, put_near, sum_ref.shape[0])
    row_grads(1 - core(), hot_ref, [far_ref], put_far, sum_ref.shape[0])


def update_body(hot_ref, sum_ref, table_ref, near_ref, far_ref, part_ref, *refs):
    new_table_ref, new_sum_ref, squares, grads, staged, sums, sems = refs
    rows, width = table_ref.shape
    step = 128

    def put(at, parts):
        grad = near_ref[at, :] + (far_ref[at, :] + parts[0])
        grads[at, :] = grad
        square = grad * grad
        square = sum(square[:, k:k + 128] for k in range(0, width, 128)).T
        squares[at.start // step:at.stop // step, :] = jnp.sum(square, axis=0, keepdims=True)

    row_grads(1 - core(), hot_ref, [part_ref], put, rows)
    lines = rows // 128 // 2
    copies = []
    for h in range(2):
        own = slice(h * lines, (h + 1) * lines)
        new_sum = sum_ref[own, :] + squares[own, :] * (1.0 / width)
        sums[own, :] = new_sum
        scale = (learning_rate / jnp.sqrt(new_sum)).T
        for k in range(lines):
            at = slice((h * lines + k) * step, (h * lines + k + 1) * step)
            staged[at, :] = table_ref[at, :] - grads[at, :] * scale[:, k:k + 1]
        done = slice(h * lines * step, (h + 1) * lines * step)
        copies.append(pltpu.make_async_copy(staged.at[done], new_table_ref.at[done], sems.at[h]))
        copies[-1].start()
    copies.append(pltpu.make_async_copy(sums, new_sum_ref, sems.at[2]))
    copies[-1].start()
    for copy in copies:
        copy.wait()


def dense_body(ask_order, order, hot_ref, asked_ref, back_ref, out_ref):
    owners, slot_cap = asked_ref.shape
    half = back_ref.shape[1] - slot_cap
    rows = out_ref.shape[0]
    hot = jnp.sum(back_ref[:, 0:half, :].astype(f32), axis=0).astype(bf16)
    grad = jnp.dot(one_hot(hot_half(hot_ref, core()), (rows, half), 0), hot, preferred_element_type=f32)
    for k, t in enumerate(order):
        at = ask_order.index(t)
        pick = one_hot(asked_ref[at:at + 1, :], (rows, slot_cap), 0)
        grad += jnp.dot(pick, back_ref[k, half:, :], preferred_element_type=f32)
    out_ref[...] = grad.astype(bf16)


def exchange(x, order):
    return lax.all_to_all(x, "table", split_axis=0, concat_axis=0, tiled=True, axis_index_groups=[list(order)])


def swap(x, bit):
    return lax.ppermute(x, "dp", [(g, g ^ bit) for g in range(lax.axis_size("dp"))])


def per_device(bag_slots, labels, cold_ids, cold_count, table, adagrad_sum, hot_ids, w_in, w_out):
    owners = lax.axis_size("table")
    groups = lax.axis_size("dp")
    hot_dev = hot_ids.shape[0]
    slot_cap = cold_ids.shape[2]
    batch = bag_slots.shape[0]
    rows, width = table.shape
    hidden_units = w_in.shape[1]
    half = hot_dev // 2
    vocab = owners * (hot_dev + slot_cap)
    shape = jax.ShapeDtypeStruct

    hot_row = hot_ids.reshape(1, hot_dev)
    requests = call(
        turn_body,
        shape((owners, slot_cap), i32),
        (pltpu.with_memory_space_constraint(cold_ids[0], pltpu.HBM),),
        [pltpu.SemaphoreType.DMA((2,))],
        in_specs=[HBM],
        out_specs=HBM,
    )
    ask_order = tuple((t + owners // 2) % owners for t in range(owners))
    order = tuple(t if t % 2 else ask_order[t] for t in range(owners))
    asked = exchange(requests, ask_order)
    slots = bag_slots.T
    first = FIRST * batch // 4
    rest = shape((slots.shape[0], batch - first), i32)
    packed, key, unit, hot, table_bf = call(
        prepare_body,
        (
            shape((vocab // FIELDS, first), i32),
            rest,
            rest,
            shape((hot_dev, width), bf16),
            shape((rows, width), bf16),
        ),
        tuple(pltpu.with_memory_space_constraint(x, pltpu.HBM) for x in (cold_count, slots, hot_row, table)),
        [
            pltpu.VMEM(cold_count.shape, i32),
            pltpu.VMEM(slots.shape, i32),
            pltpu.VMEM(hot_row.shape, i32),
            pltpu.VMEM(table.shape, f32),
            pltpu.SemaphoreType.DMA((4,)),
        ],
        in_specs=[HBM] * 4,
    )
    asked, packed = lax.optimization_barrier((asked, packed))
    served = call(
        functools.partial(serve_body, ask_order, order),
        shape((owners, half + slot_cap, width), bf16),
        (asked, hot, table_bf),
        [pltpu.VMEM((owners * slot_cap, rows), bf16)],
    )
    own_rows = exchange(served, order)
    first_rows = call(first_rows_body, shape((owners, half, width), bf16), (own_rows,))
    first_rows, packed = lax.optimization_barrier((first_rows, packed))
    mate_rows = swap(first_rows, 1)
    inc = call(incidence_body, shape((batch, vocab), bf16), (packed, key, unit), [pltpu.VMEM((vocab, batch), bf16)])
    hot_half = owners * half
    dpooled, to_mate = call(
        functools.partial(top_body, order),
        (shape((batch, width), bf16), shape((hot_half, width), bf16)),
        (labels.reshape(-1, 128), inc, own_rows, mate_rows, w_in, w_out.reshape(-1, 128)),
        [
            pltpu.VMEM((batch, hidden_units), bf16),
            pltpu.VMEM((vocab, width), bf16),
            pltpu.VMEM((batch, width), bf16),
            pltpu.VMEM((batch, 128), f32),
            pltpu.VMEM((batch, 128), f32),
        ],
    )
    got = swap(to_mate.reshape(owners, half, width), 1)
    hot_grads, cold_grads = call(
        own_grads_body,
        (shape((hot_half, width), f32), shape((owners * slot_cap, width), bf16)),
        (inc, dpooled),
    )
    summed = call(
        functools.partial(pack_grads_body, order),
        shape((owners, half + slot_cap, width), bf16),
        (hot_grads, got, cold_grads),
    )
    returned = exchange(summed, order)
    size = half + owners * slot_cap + TAIL
    if groups == 4 and 2 * size <= rows and owners * slot_cap == width:
        own = call(functools.partial(collect_body, ask_order, order), shape((size, width), bf16), (asked, returned))
        beside = swap(own, 2)
        far_own, far_beside = swap(own, 1), swap(beside, 1)
        dense = shape((rows, width), f32)
        near, far = call(near_grads_body, (dense, dense), (hot_row, own, beside, far_own))
        new_table, new_sum = call(
            update_body,
            (dense, shape((rows // 128, 128), f32)),
            (hot_row, adagrad_sum.reshape(-1, 128), table, near, far, far_beside),
            [
                pltpu.VMEM((rows // 128, 128), f32),
                pltpu.VMEM((rows, width), f32),
                pltpu.VMEM((rows, width), f32),
                pltpu.VMEM((rows // 128, 128), f32),
                pltpu.SemaphoreType.DMA((3,)),
            ],
            out_specs=(HBM, HBM),
        )
        return new_table, new_sum.reshape(rows)
    grad = call(functools.partial(dense_body, ask_order, order), shape((rows, width), bf16), (hot_row, asked, returned))
    grad = lax.psum(grad, "dp").astype(f32)
    new_sum = adagrad_sum + jnp.mean(grad * grad, axis=1)
    return table - learning_rate * grad / jnp.sqrt(new_sum)[:, None], new_sum


def solution(mesh):
    placed = (
        P(("dp", "table"), None),
        P(("dp", "table")),
        P(("dp", "table"), None, None),
        P(("dp", "table"), None),
        P("table", None),
        P("table"),
        P("table"),
        P(),
        P(),
    )
    return jax.shard_map(
        per_device,
        mesh=mesh,
        in_specs=placed,
        out_specs=(P("table", None), P("table")),
        check_vma=False,
    )
```

```python
import functools
import math

import jax
import jax.numpy as jnp
from jax import lax
from jax.experimental import pallas as pl
from jax.experimental.pallas import tpu as pltpu
from jax.sharding import PartitionSpec as P

learning_rate = 0.3
f32, bf16, i32 = jnp.float32, jnp.bfloat16, jnp.int32
VMEM = pl.BlockSpec(memory_space=pltpu.VMEM)
HBM = pl.BlockSpec(memory_space=pltpu.HBM)
FIELDS = 4
FIELD_BITS = 8
TAIL = 16
FIRST = 2


def call(body, outs, operands, scratch=(), in_specs=None, out_specs=None):
    held = jax.tree.leaves((outs, operands)) + [x for x in scratch if getattr(x, "memory_space", None) == pltpu.VMEM]
    limit = sum(math.prod(x.shape) * jnp.dtype(x.dtype).itemsize for x in held) + 4 * 1024 * 1024
    return pl.pallas_call(
        body,
        out_shape=outs,
        in_specs=in_specs or [VMEM] * len(operands),
        out_specs=out_specs or jax.tree.map(lambda _: VMEM, outs),
        scratch_shapes=list(scratch),
        compiler_params=pltpu.CompilerParams(vmem_limit_bytes=limit),
    )(*operands)


def lanes(pieces):
    return jnp.concatenate(pieces, axis=1)


def one_hot(ids, shape, axis, start=0):
    return (lax.broadcasted_iota(i32, shape, axis) + start == ids).astype(f32).astype(bf16)


def entries(hot_dev, counts, slots, field):
    owners = counts.shape[1]
    slot_cap = FIELDS * field // owners - hot_dev
    half = hot_dev // 2
    hot_cols = owners * hot_dev
    place = slots % hot_dev
    hot = jnp.where(place // half == core(), 0, owners * half) + (slots // hot_dev) * half + place % half
    column = jnp.where(slots < hot_cols, hot, slots)
    cold = slots - hot_cols
    live = slots >= 0
    for t in range(owners):
        at = cold - t * slot_cap
        live = live & ((at < counts[:, t:t + 1]) | (at >= slot_cap))
    key = jnp.where(live, column % field, -1)
    return key, jnp.left_shift(jnp.ones_like(slots), FIELD_BITS * (column // field))


def count(key, unit, field):
    row = lax.broadcasted_iota(i32, (field, key.shape[1]), 0)
    packed = jnp.zeros(row.shape, i32)
    for entry in range(key.shape[0]):
        packed += jnp.where(row == key[entry:entry + 1, :], unit[entry:entry + 1, :], 0)
    return packed


def turn_body(ids_ref, out_ref, sems):
    half = ids_ref.shape[0] // 2
    copies = [
        pltpu.make_async_copy(ids_ref.at[k * half:(k + 1) * half], out_ref.at[(1 - k) * half:(2 - k) * half], sems.at[k])
        for k in range(2)
    ]
    for copy in copies:
        copy.start()
    for copy in copies:
        copy.wait()


def prepare_body(count_ref, slots_ref, ids_ref, table_ref, packed_ref, key_ref, unit_ref, hot_ref, table_bf_ref, *scratch):
    counts, slots, ids, table, sems = scratch
    pairs = [(count_ref, counts), (slots_ref, slots), (ids_ref, ids), (table_ref, table)]
    copies = [pltpu.make_async_copy(src, dst, sems.at[k]) for k, (src, dst) in enumerate(pairs)]
    for copy in copies:
        copy.start()
    hot_dev = ids.shape[1]
    field, first = packed_ref.shape
    copies[0].wait()
    copies[1].wait()
    for start in range(0, slots.shape[1], 128):
        at = slice(start, start + 128)
        key, unit = entries(hot_dev, counts[...], slots[:, at], field)
        if start < first:
            packed_ref[:, at] = count(key, unit, field)
        else:
            rest = slice(start - first, start - first + 128)
            key_ref[:, rest], unit_ref[:, rest] = key, unit
    copies[2].wait()
    copies[3].wait()
    table_bf_ref[...] = table[...].astype(bf16)
    column = jnp.broadcast_to(ids[...], (8, hot_dev)).T[:, 0:1]
    pick = one_hot(column, (hot_dev, table.shape[0]), 1)
    hot_ref[...] = jnp.dot(pick, table_bf_ref[...], preferred_element_type=f32).astype(bf16)


def incidence_body(packed_ref, key_ref, unit_ref, out_ref, inc_t_ref):
    field, first = packed_ref.shape
    for start in range(0, out_ref.shape[0], 128):
        at = slice(start, start + 128)
        if start < first:
            packed = packed_ref[:, at]
        else:
            rest = slice(start - first, start - first + 128)
            packed = count(key_ref[:, rest], unit_ref[:, rest], field)
        for k in range(FIELDS):
            part = jnp.right_shift(packed, FIELD_BITS * k) & (2**FIELD_BITS - 1)
            inc_t_ref[k * field:(k + 1) * field, at] = part.astype(f32).astype(bf16)
    out_ref[...] = inc_t_ref[...].T


def core():
    return lax.rem(lax.axis_index("dp"), 2)


def serve_body(ask_order, order, asked_ref, hot_ref, table_ref, out_ref, pick):
    owners, slot_cap = asked_ref.shape
    half = hot_ref.shape[0] // 2
    asked = asked_ref[...].T
    for k, t in enumerate(ask_order):
        pick[t * slot_cap:(t + 1) * slot_cap, :] = one_hot(asked[:, k:k + 1], (slot_cap, table_ref.shape[0]), 1)
    picked = jnp.dot(pick[...], table_ref[...], preferred_element_type=f32).astype(bf16)
    hot = hot_ref[pl.ds(pl.multiple_of(core() * half, half), half), :]
    for k, t in enumerate(order):
        out_ref[k, 0:half, :] = hot
        out_ref[k, half:, :] = picked[t * slot_cap:(t + 1) * slot_cap]


def first_rows_body(rows_ref, out_ref):
    out_ref[...] = rows_ref[:, 0:out_ref.shape[1], :]


def top_body(order, labels_ref, inc_ref, own_ref, mate_ref, w_in_ref, w_out_ref, out_ref, to_mate_ref, hidden, rows, pooled, total, dlogit):
    batch = inc_ref.shape[0]
    hidden_units, width = w_in_ref.shape[1], w_in_ref.shape[0]
    owners, half, _ = mate_ref.shape
    hot_half = owners * half
    slot_cap = own_ref.shape[1] - half
    size, step, wide = batch // 2, 256, 256
    blocks = [slice(at, at + size) for at in range(0, batch, size)]
    for k, t in enumerate(order):
        rows[t * half:(t + 1) * half, :] = own_ref[k, 0:half, :]
        rows[hot_half + t * half:hot_half + (t + 1) * half, :] = mate_ref[k]
        rows[2 * hot_half + t * slot_cap:2 * hot_half + (t + 1) * slot_cap, :] = own_ref[k, half:, :]
    pooled[...] = jnp.dot(inc_ref[...], rows[...], preferred_element_type=f32).astype(bf16)
    w_out = w_out_ref[...].astype(f32)
    labels = labels_ref[...].T
    for samples in blocks:
        acc = jnp.zeros((size, 128), f32)
        for start in range(0, hidden_units, step):
            cols = slice(start, start + step)
            pre_act = jnp.dot(pooled[samples, :], w_in_ref[:, cols], preferred_element_type=f32)
            own = lanes([w_out[k:k + 1, :] for k in range(start // 128, (start + step) // 128)])
            act = jnp.maximum(pre_act.astype(bf16), jnp.zeros((), bf16))
            hidden[samples, cols] = act
            term = act.astype(f32) * own
            for k in range(0, step, 128):
                acc += term[:, k:k + 128]
        total[samples, :] = acc
        for k in range(samples.start // 128, samples.stop // 128):
            line = slice(k * 128, (k + 1) * 128)
            logit = jnp.sum(total[line, :], axis=1, keepdims=True)
            dlogit[line, :] = jnp.broadcast_to(jax.nn.sigmoid(logit) - labels[:, k:k + 1], (128, 128))
    mate = jnp.zeros((hot_half, width), f32)
    for samples in blocks:
        scale = dlogit[samples, :]
        grad = jnp.zeros((size, width), f32)
        for start in range(0, hidden_units, wide):
            dhidden = lanes([
                jnp.where(
                    hidden[samples, k:k + 128].astype(f32) > 0, scale * w_out[k // 128:k // 128 + 1, :], 0.0
                ).astype(bf16)
                for k in range(start, start + wide, 128)
            ])
            grad += lax.dot_general(
                dhidden, w_in_ref[:, start:start + wide], (((1,), (1,)), ((), ())), preferred_element_type=f32
            )
        out_ref[samples, :] = grad.astype(bf16)
        mate += jnp.dot(
            inc_ref[samples, hot_half:2 * hot_half].T, out_ref[samples, :], preferred_element_type=f32
        )
    to_mate_ref[...] = mate.astype(bf16)


def own_grads_body(inc_ref, dpooled_ref, hot_ref, cold_ref):
    hot_half = hot_ref.shape[0]
    dpooled = dpooled_ref[...]
    hot_ref[...] = jnp.dot(inc_ref[:, 0:hot_half].T, dpooled, preferred_element_type=f32)
    cold_ref[...] = jnp.dot(inc_ref[:, 2 * hot_half:].T, dpooled, preferred_element_type=f32).astype(bf16)


def pack_grads_body(order, hot_ref, got_ref, cold_ref, out_ref):
    owners, half, width = got_ref.shape
    hot = hot_ref[...] + got_ref[...].reshape(owners * half, width).astype(f32)
    slot_cap = out_ref.shape[1] - half
    for k, t in enumerate(order):
        out_ref[k, 0:half, :] = hot[t * half:(t + 1) * half].astype(bf16)
        out_ref[k, half:, :] = cold_ref[t * slot_cap:(t + 1) * slot_cap, :]


def collect_body(ask_order, order, asked_ref, back_ref, out_ref):
    owners, slot_cap = asked_ref.shape
    half = back_ref.shape[1] - slot_cap
    out_ref[0:half, :] = jnp.sum(back_ref[:, 0:half, :].astype(f32), axis=0).astype(bf16)
    for k, t in enumerate(order):
        out_ref[half + t * slot_cap:half + (t + 1) * slot_cap, :] = back_ref[k, half:, :]
    asked = lanes([asked_ref[ask_order.index(t):ask_order.index(t) + 1, :] for t in range(owners)])
    digit = lax.broadcasted_iota(i32, (TAIL, asked.shape[1]), 0)
    digits = jnp.where(digit == 0, asked >> 8, jnp.where(digit == 1, asked & 255, 0))
    out_ref[half + owners * slot_cap:, :] = digits.astype(f32).astype(bf16)


def hot_half(hot_ref, which):
    half = hot_ref.shape[1] // 2
    return jnp.where(which == 0, hot_ref[:, 0:half], hot_ref[:, half:])


def row_grads(which, hot_ref, part_refs, put, rows):
    half = hot_ref.shape[1] // 2
    hot_ids = hot_half(hot_ref, which)
    cold_ids = []
    for part_ref in part_refs:
        digits = part_ref[part_ref.shape[0] - TAIL:, :].astype(f32).astype(i32)
        cold_ids.append(digits[0:1, :] * 256 + digits[1:2, :])
    step = 128
    for start in range(0, rows, step):
        hot_pick = one_hot(hot_ids, (step, half), 0, start)
        grads = []
        for ids, part_ref in zip(cold_ids, part_refs):
            pick = one_hot(ids, (step, ids.shape[1]), 0, start)
            hot = jnp.dot(hot_pick, part_ref[0:half, :], preferred_element_type=f32)
            grads.append(hot + jnp.dot(pick, part_ref[half:part_ref.shape[0] - TAIL, :], preferred_element_type=f32))
        put(slice(start, start + step), grads)


def near_grads_body(hot_ref, *refs):
    near_refs, (far_ref, sum_ref, far_sum_ref) = refs[:-3], refs[-3:]

    def put_near(at, grads):
        sum_ref[at, :] = grads[0] + grads[1]

    def put_far(at, grads):
        far_sum_ref[at, :] = grads[0]

    row_grads(core(), hot_ref, near_refs, put_near, sum_ref.shape[0])
    row_grads(1 - core(), hot_ref, [far_ref], put_far, sum_ref.shape[0])


def update_body(hot_ref, sum_ref, table_ref, near_ref, far_ref, part_ref, *refs):
    new_table_ref, new_sum_ref, squares, grads, staged, sums, sems = refs
    rows, width = table_ref.shape
    step = 128

    def put(at, parts):
        grad = near_ref[at, :] + (far_ref[at, :] + parts[0])
        grads[at, :] = grad
        square = grad * grad
        square = sum(square[:, k:k + 128] for k in range(0, width, 128)).T
        squares[at.start // step:at.stop // step, :] = jnp.sum(square, axis=0, keepdims=True)

    row_grads(1 - core(), hot_ref, [part_ref], put, rows)
    lines = rows // 128 // 2
    copies = []
    for h in range(2):
        own = slice(h * lines, (h + 1) * lines)
        new_sum = sum_ref[own, :] + squares[own, :] * (1.0 / width)
        sums[own, :] = new_sum
        scale = (learning_rate / jnp.sqrt(new_sum)).T
        for k in range(lines):
            at = slice((h * lines + k) * step, (h * lines + k + 1) * step)
            staged[at, :] = table_ref[at, :] - grads[at, :] * scale[:, k:k + 1]
        done = slice(h * lines * step, (h + 1) * lines * step)
        copies.append(pltpu.make_async_copy(staged.at[done], new_table_ref.at[done], sems.at[h]))
        copies[-1].start()
    copies.append(pltpu.make_async_copy(sums, new_sum_ref, sems.at[2]))
    copies[-1].start()
    for copy in copies:
        copy.wait()


def dense_body(ask_order, order, hot_ref, asked_ref, back_ref, out_ref):
    owners, slot_cap = asked_ref.shape
    half = back_ref.shape[1] - slot_cap
    rows = out_ref.shape[0]
    hot = jnp.sum(back_ref[:, 0:half, :].astype(f32), axis=0).astype(bf16)
    grad = jnp.dot(one_hot(hot_half(hot_ref, core()), (rows, half), 0), hot, preferred_element_type=f32)
    for k, t in enumerate(order):
        at = ask_order.index(t)
        pick = one_hot(asked_ref[at:at + 1, :], (rows, slot_cap), 0)
        grad += jnp.dot(pick, back_ref[k, half:, :], preferred_element_type=f32)
    out_ref[...] = grad.astype(bf16)


def exchange(x, order):
    return lax.all_to_all(x, "table", split_axis=0, concat_axis=0, tiled=True, axis_index_groups=[list(order)])


def swap(x, bit):
    return lax.ppermute(x, "dp", [(g, g ^ bit) for g in range(lax.axis_size("dp"))])


def per_device(bag_slots, labels, cold_ids, cold_count, table, adagrad_sum, hot_ids, w_in, w_out):
    owners = lax.axis_size("table")
    groups = lax.axis_size("dp")
    hot_dev = hot_ids.shape[0]
    slot_cap = cold_ids.shape[2]
    batch = bag_slots.shape[0]
    rows, width = table.shape
    hidden_units = w_in.shape[1]
    half = hot_dev // 2
    vocab = owners * (hot_dev + slot_cap)
    shape = jax.ShapeDtypeStruct

    hot_row = hot_ids.reshape(1, hot_dev)
    requests = call(
        turn_body,
        shape((owners, slot_cap), i32),
        (pltpu.with_memory_space_constraint(cold_ids[0], pltpu.HBM),),
        [pltpu.SemaphoreType.DMA((2,))],
        in_specs=[HBM],
        out_specs=HBM,
    )
    ask_order = tuple((t + owners // 2) % owners for t in range(owners))
    order = tuple(t if t % 2 else ask_order[t] for t in range(owners))
    asked = exchange(requests, ask_order)
    slots = bag_slots.T
    first = FIRST * batch // 4
    rest = shape((slots.shape[0], batch - first), i32)
    packed, key, unit, hot, table_bf = call(
        prepare_body,
        (
            shape((vocab // FIELDS, first), i32),
            rest,
            rest,
            shape((hot_dev, width), bf16),
            shape((rows, width), bf16),
        ),
        tuple(pltpu.with_memory_space_constraint(x, pltpu.HBM) for x in (cold_count, slots, hot_row, table)),
        [
            pltpu.VMEM(cold_count.shape, i32),
            pltpu.VMEM(slots.shape, i32),
            pltpu.VMEM(hot_row.shape, i32),
            pltpu.VMEM(table.shape, f32),
            pltpu.SemaphoreType.DMA((4,)),
        ],
        in_specs=[HBM] * 4,
    )
    asked, packed = lax.optimization_barrier((asked, packed))
    served = call(
        functools.partial(serve_body, ask_order, order),
        shape((owners, half + slot_cap, width), bf16),
        (asked, hot, table_bf),
        [pltpu.VMEM((owners * slot_cap, rows), bf16)],
    )
    own_rows = exchange(served, order)
    first_rows = call(first_rows_body, shape((owners, half, width), bf16), (own_rows,))
    first_rows, packed = lax.optimization_barrier((first_rows, packed))
    mate_rows = swap(first_rows, 1)
    inc = call(incidence_body, shape((batch, vocab), bf16), (packed, key, unit), [pltpu.VMEM((vocab, batch), bf16)])
    hot_half = owners * half
    dpooled, to_mate = call(
        functools.partial(top_body, order),
        (shape((batch, width), bf16), shape((hot_half, width), bf16)),
        (labels.reshape(-1, 128), inc, own_rows, mate_rows, w_in, w_out.reshape(-1, 128)),
        [
            pltpu.VMEM((batch, hidden_units), bf16),
            pltpu.VMEM((vocab, width), bf16),
            pltpu.VMEM((batch, width), bf16),
            pltpu.VMEM((batch, 128), f32),
            pltpu.VMEM((batch, 128), f32),
        ],
    )
    got = swap(to_mate.reshape(owners, half, width), 1)
    hot_grads, cold_grads = call(
        own_grads_body,
        (shape((hot_half, width), f32), shape((owners * slot_cap, width), bf16)),
        (inc, dpooled),
    )
    summed = call(
        functools.partial(pack_grads_body, order),
        shape((owners, half + slot_cap, width), bf16),
        (hot_grads, got, cold_grads),
    )
    returned = exchange(summed, order)
    size = half + owners * slot_cap + TAIL
    if groups == 4 and 2 * size <= rows and owners * slot_cap == width:
        own = call(functools.partial(collect_body, ask_order, order), shape((size, width), bf16), (asked, returned))
        beside = swap(own, 2)
        far_own, far_beside = swap(own, 1), swap(beside, 1)
        dense = shape((rows, width), f32)
        near, far = call(near_grads_body, (dense, dense), (hot_row, own, beside, far_own))
        new_table, new_sum = call(
            update_body,
            (dense, shape((rows // 128, 128), f32)),
            (hot_row, adagrad_sum.reshape(-1, 128), table, near, far, far_beside),
            [
                pltpu.VMEM((rows // 128, 128), f32),
                pltpu.VMEM((rows, width), f32),
                pltpu.VMEM((rows, width), f32),
                pltpu.VMEM((rows // 128, 128), f32),
                pltpu.SemaphoreType.DMA((3,)),
            ],
            out_specs=(HBM, HBM),
        )
        return new_table, new_sum.reshape(rows)
    grad = call(functools.partial(dense_body, ask_order, order), shape((rows, width), bf16), (hot_row, asked, returned))
    grad = lax.psum(grad, "dp").astype(f32)
    new_sum = adagrad_sum + jnp.mean(grad * grad, axis=1)
    return table - learning_rate * grad / jnp.sqrt(new_sum)[:, None], new_sum


def solution(mesh):
    placed = (
        P(("dp", "table"), None),
        P(("dp", "table")),
        P(("dp", "table"), None, None),
        P(("dp", "table"), None),
        P("table", None),
        P("table"),
        P("table"),
        P(),
        P(),
    )
    return jax.shard_map(
        per_device,
        mesh=mesh,
        in_specs=placed,
        out_specs=(P("table", None), P("table")),
        check_vma=False,
    )
```
